32 devices in a mesh: section: 8 (over z, core), dp: 4 (over y, x).
Axes of the slice: x: 2, y: 2, z: 4, core: 2. Of those that a mesh axis runs over, the one named last changes fastest.
Arguments:
- section_inputs: bfloat16 [8, 512, 4096], P('section', 'dp'), may hold values from -6 to 6
- norm_gain: bfloat16 [8, 4096], P('section'), may hold values from 0.5 to 1.5
- down_proj: bfloat16 [8, 4096, 256], P('section', 'dp'), may hold values from -0.09375 to 0.09375
- up_proj: bfloat16 [8, 256, 4096], P('section', None, 'dp'), may hold values from -0.1875 to 0.1875
- readout_matrix: bfloat16 [4096, 128], P('dp'), may hold values from -0.09375 to 0.09375
- ground_truth_series: float32 [512, 128], P('dp'), may hold values from -6 to 6
- valid_len: int32 [32], P('dp'), may hold values from 1 to 16
Outputs:
- input_grads: bfloat16 [8, 512, 4096], P('section', 'dp')
- down_grads: bfloat16 [8, 4096, 256], P('section', 'dp')
- up_grads: bfloat16 [8, 256, 4096], P('section', None, 'dp')
The draws below stay inside these ranges and needn't reach their ends.
All inputs are finite; a program needn't handle non-finite values.
Results may differ from the reference program's by a relative error of at most 0.035.
Values may be sent and summed in bfloat16 or wider, within the bound.
No kernel may reach another device: no remote copies, remote signals or barrier semaphores. Data moves between devices by JAX's collectives and lax.ppermute only.
A program may use at most 64 MiB of HBM per device.

```python
import jax
import jax.numpy as jnp
from jax import lax

EMBED_WIDTH = 4096
LAT = 256
HORIZON_LENGTH = 128
ROWS = 16
SEQUENCE_TOTAL = 512
MICRO_ALL = 32
N_SECTION = 8


def place_ends(drawn, key, least, top_value):
    extent = drawn.shape
    place = [jax.random.randint(jax.random.fold_in(key, axis), (), 0, extent[axis]) for axis in range(len(extent))]
    drawn = drawn.at[tuple(place)].set(least)
    longest = extent.index(max(extent))
    place[longest] = (place[longest] + 1) % extent[longest]
    return drawn.at[tuple(place)].set(top_value)


def block_scale(stream_key, shape, pieces, low, largest):
    level = 1.0
    for dim, blocks in pieces:
        draws = jax.random.uniform(jax.random.fold_in(jax.random.fold_in(stream_key, 6), dim), (blocks,), jnp.float32, low / len(pieces), largest / len(pieces))
        level = level * jnp.repeat(jnp.exp(draws), shape[dim] // blocks).reshape((-1,) + (1,) * (len(shape) - 1 - dim))
    return level


def centred(own_key, dims, width, limit, cuts=(), held_as=jnp.bfloat16):
    array = width * jax.random.normal(own_key, dims, jnp.float32)
    if cuts:
        array = array * block_scale(own_key, dims, cuts, -0.22, 0.18)
    return jnp.clip(array, -limit, limit).astype(held_as)


def setup_inputs(seed: int = 0) -> dict:
    splits = jax.random.split(jax.random.key(seed), 8)
    section_inputs = centred(splits[0], (N_SECTION, SEQUENCE_TOTAL, EMBED_WIDTH), 1.0, 6.0, ((0, 8), (1, 4)))
    norm_gain = jnp.clip(1.0 + 0.1 * jax.random.normal(splits[1], (N_SECTION, EMBED_WIDTH), jnp.float32), 0.5, 1.5).astype(jnp.bfloat16)
    down_proj = centred(splits[2], (N_SECTION, EMBED_WIDTH, LAT), EMBED_WIDTH ** -0.5, 0.09375, ((0, 8), (1, 4)))
    up_proj = centred(splits[3], (N_SECTION, LAT, EMBED_WIDTH), (4 * LAT) ** -0.5, 0.1875, ((0, 8), (2, 4)))
    readout_matrix = centred(splits[4], (EMBED_WIDTH, HORIZON_LENGTH), EMBED_WIDTH ** -0.5, 0.09375, ((0, 4),))
    ground_truth_series = centred(splits[5], (SEQUENCE_TOTAL, HORIZON_LENGTH), 1.0, 6.0, ((0, 4),), jnp.float32)
    valid_len = place_ends(jax.random.randint(splits[6], (MICRO_ALL,), 1, ROWS + 1), jax.random.fold_in(splits[6], 1), 1, ROWS).astype(jnp.int32)
    return {"section_inputs": section_inputs, "norm_gain": norm_gain, "down_proj": down_proj, "up_proj": up_proj, "readout_matrix": readout_matrix, "ground_truth_series": ground_truth_series, "valid_len": valid_len}


EPSILON = 1e-05

def normalize(inputs, gain_row):
    values = inputs.astype(jnp.float32)
    inverse = lax.rsqrt(lax.optimization_barrier(jnp.mean(values * values, axis=-1, keepdims=True)) + EPSILON)
    unit = values * inverse
    normed = (unit * gain_row.astype(jnp.float32)).astype(jnp.bfloat16)
    return (inverse, unit, normed)

def multiply_trailing_factor(left, right):
    return lax.dot_general(left, right, (((1,), (1,)), ((), ())), preferred_element_type=jnp.float32)

def contract_rows(left, right):
    return lax.dot_general(left, right, (((0,), (0,)), ((), ())), preferred_element_type=jnp.float32)

def block_backward(inverse, unit, latent, gain_row, down_full, up_full, arriving_gradient):
    sigmoid = jax.nn.sigmoid(latent)
    hidden_grad = multiply_trailing_factor(arriving_gradient, up_full)
    latent_grad = (hidden_grad * sigmoid * (1.0 + latent * (1.0 - sigmoid))).astype(jnp.bfloat16)
    scaled = multiply_trailing_factor(latent_grad, down_full) * gain_row.astype(jnp.float32)
    inputs_grad = arriving_gradient.astype(jnp.float32) + inverse * (scaled - unit * lax.optimization_barrier(jnp.mean(scaled * unit, axis=-1, keepdims=True)))
    return (inputs_grad.astype(jnp.bfloat16), latent_grad)

def reference(section_inputs, norm_gain, down_proj, up_proj, readout_matrix, ground_truth_series, valid_len):
    positions = jnp.arange(SEQUENCE_TOTAL)
    micro_ids = positions // ROWS
    offsets = positions % ROWS
    observed_entry_indicator = (offsets < valid_len[micro_ids]).astype(jnp.float32)
    last = N_SECTION - 1
    inverse, unit, normed = normalize(section_inputs[last], norm_gain[last])
    latent = jnp.dot(normed, down_proj[last], preferred_element_type=jnp.float32)
    activated = jax.nn.silu(latent).astype(jnp.bfloat16)
    adapter_output = (section_inputs[last].astype(jnp.float32) + jnp.dot(activated, up_proj[last], preferred_element_type=jnp.float32)).astype(jnp.bfloat16)
    estimated_horizon = jnp.dot(adapter_output, readout_matrix, preferred_element_type=jnp.float32)
    prediction_discrepancy = (observed_entry_indicator[:, None] * (estimated_horizon - ground_truth_series)).astype(jnp.bfloat16)
    arriving_gradient = multiply_trailing_factor(prediction_discrepancy, readout_matrix).astype(jnp.bfloat16)
    input_list = []
    down_list = []
    up_list = []
    for index in range(N_SECTION - 1, -1, -1):
        inverse, unit, normed = normalize(section_inputs[index], norm_gain[index])
        latent = jnp.dot(normed, down_proj[index], preferred_element_type=jnp.float32)
        activated = jax.nn.silu(latent).astype(jnp.bfloat16)
        inputs_grad, latent_grad = block_backward(inverse, unit, latent, norm_gain[index], down_proj[index], up_proj[index], arriving_gradient)
        down_list.append(contract_rows(normed, latent_grad).astype(jnp.bfloat16))
        up_list.append(contract_rows(activated, arriving_gradient).astype(jnp.bfloat16))
        input_list.append(inputs_grad)
        arriving_gradient = inputs_grad
    return (jnp.stack(input_list[::-1]), jnp.stack(down_list[::-1]), jnp.stack(up_list[::-1]))
```

```python
import functools

import jax
import jax.numpy as jnp
from jax import lax
from jax.experimental import pallas as pl
from jax.experimental.pallas import tpu as pltpu
from jax.sharding import PartitionSpec as P

EPSILON = 1e-05
CHUNKS = 2
ANY = pl.BlockSpec(memory_space=pl.ANY)
VMEM = pl.BlockSpec(memory_space=pltpu.VMEM)
SMEM = pl.BlockSpec(memory_space=pltpu.SMEM)
PARAMS = pltpu.CompilerParams(vmem_limit_bytes=40 * 1024 * 1024)


def dot_nn(left, right):
    return lax.dot_general(
        left, right, (((1,), (0,)), ((), ())), preferred_element_type=jnp.float32
    )


def dot_nt(left, right):
    return lax.dot_general(
        left, right, (((1,), (1,)), ((), ())), preferred_element_type=jnp.float32
    )


def dot_tn(left, right):
    return lax.dot_general(
        left, right, (((0,), (0,)), ((), ())), preferred_element_type=jnp.float32
    )


def silu_slope(latent):
    sigmoid = jax.nn.sigmoid(latent)
    return sigmoid * (1.0 + latent * (1.0 - sigmoid))


def move(block, pairs):
    return lax.ppermute(block, ("section", "dp"), pairs)


def peers(sections, size, k):
    return [(s * size + i, s * size + (i ^ k)) for s in sections for i in range(size)]


def gather_pieces(block, sections, size):
    rows = block.shape[0]
    if size == 4:
        half = rows // 2
        from_x = move(block, peers(sections, size, 1))
        from_y = move(block, peers(sections, size, 2))
        low = move(from_y[:half], peers(sections, size, 1))
        high = move(from_x[half:], peers(sections, size, 2))
        return [[(0, rows, from_x)], [(0, rows, from_y)], [(0, half, low), (half, half, high)]]
    return [[(0, rows, move(block, peers(sections, size, k)))] for k in range(1, size)]


def flatten(pieces):
    return [part[2] for piece in pieces for part in piece]


def shapes_of(pieces):
    return [[(row, count) for row, count, _ in piece] for piece in pieces]


def copies(refs, layout, held, sems, base):
    out, at = [], 0
    for slot, parts in enumerate(layout, 1):
        group = []
        for row, count in parts:
            group.append(
                pltpu.make_async_copy(
                    refs[at], held.at[slot, pl.ds(row, count)], sems.at[base + at]
                )
            )
            at += 1
        out.append(group)
    return out


def start_all(groups):
    for group in groups:
        for copy in group:
            copy.start()


def wait_all(group):
    for copy in group:
        copy.wait()


def columns(flag, k, width):
    return pl.ds(pl.multiple_of((flag ^ k) * width, width), width)


def latent_of(normed_ref, held, dp_index, size, wait):
    total = None
    for k in range(size):
        wait(k)
        part = dot_nn(normed_ref[:, columns(dp_index, k, held.shape[1])], held[k])
        total = part if total is None else total + part
    return total


def latent_kernel(size, layout, want, *refs):
    flags, normed, own = refs[:3]
    count = sum(len(parts) for parts in layout)
    pieces = refs[3 : 3 + count]
    latent, held, sems = refs[3 + count :]

    @pl.when(flags[1] == want)
    def _():
        mine = pltpu.make_async_copy(own, held.at[0], sems.at[0])
        mine.start()
        groups = [[mine]] + copies(pieces, layout, held, sems, 1)
        start_all(groups[1:])
        latent[...] = latent_of(normed, held, flags[0], size, lambda k: wait_all(groups[k]))


def top_kernel(size, layout, head_layout, *refs):
    flags, x, normed, gain, inverse, truth, mask, own, own_head = refs[:9]
    count = sum(len(parts) for parts in layout)
    head_count = sum(len(parts) for parts in head_layout)
    pieces = refs[9 : 9 + count]
    head_pieces = refs[9 + count : 9 + count + head_count]
    latent_out, latent_grad_out, arriving_out, grads_out, held, head, sems = refs[
        9 + count + head_count :
    ]
    dp_index = flags[0]
    is_top = flags[2] == 1
    width = held.shape[1]

    @pl.when(flags[1] == 1)
    def _():
        mine = pltpu.make_async_copy(own, held.at[0], sems.at[0])
        mine.start()
        groups = [[mine]] + copies(pieces, layout, held, sems, 1)
        start_all(groups[1:])
        latent_out[...] = latent_of(normed, held, dp_index, size, lambda k: wait_all(groups[k]))

    @pl.when(is_top)
    def _():
        mine = pltpu.make_async_copy(own_head, head.at[0], sems.at[1 + count])
        mine.start()
        groups = [[mine]] + copies(head_pieces, head_layout, head, sems, 2 + count)
        start_all(groups[1:])
        latent = latent_out[...]
        activated = jax.nn.silu(latent).astype(jnp.bfloat16)
        estimate = None
        product = None
        for k in range(size):
            wait_all(groups[k])
            part = dot_nn(x[:, columns(dp_index, k, width)], head[k, :width])
            extra = head[k, width:].astype(jnp.float32)
            estimate = part if estimate is None else estimate + part
            product = extra if product is None else product + extra
        product = product.astype(jnp.bfloat16)
        estimate = estimate + dot_nn(activated, product)
        error = (mask[:, :1] * (estimate - truth[...])).astype(jnp.bfloat16)
        hidden_grad = dot_nt(error, product)
        latent_grad = (hidden_grad * silu_slope(latent)).astype(jnp.bfloat16)
        latent_grad_out[...] = latent_grad
        scale = inverse[:, :1]
        mean = jnp.sum(latent_grad.astype(jnp.float32) * latent, axis=-1, keepdims=True) / (
            width * size
        )
        slope = scale * scale * mean
        for k in range(size):
            at = columns(dp_index, k, width)
            arriving = dot_nt(error, head[k, :width]).astype(jnp.bfloat16)
            arriving_out[:, at] = arriving
            scaled = dot_nt(latent_grad, held[k]) * gain[:, at].astype(jnp.float32)
            grads = (
                arriving.astype(jnp.float32)
                + scale * scaled
                - x[:, at].astype(jnp.float32) * slope
            )
            grads_out[:, at] = grads.astype(jnp.bfloat16)


def tick_kernel(size, down_layout, even_layout, up_layout, *refs):
    flags, received, gain, x_all, inverse_all, latent_odd, latent_even, down_own, up_own = refs[:9]
    at = 9
    groups_of_refs = []
    for layout in (down_layout, even_layout, up_layout):
        count = sum(len(parts) for parts in layout)
        groups_of_refs.append(refs[at : at + count])
        at += count
    odd_refs, even_refs, up_refs = groups_of_refs
    at += 3
    send, latent_grads, arrivals, grads = refs[at : at + 4]
    down, up, arriving, x, inverse, latent, latent_grad, result, sems, up_sems, io_sems = refs[
        at + 4 :
    ]
    dp_index, odd, active, row = flags[0], flags[1], flags[3], flags[4]
    rows = arriving.shape[0]
    width = down.shape[1]
    row = pl.multiple_of(row, rows)

    @pl.when(active == 1)
    def _():
        fetch = pltpu.make_async_copy(received, arriving, io_sems.at[0])
        fetch.start()
        up_mine = pltpu.make_async_copy(up_own, up.at[0], up_sems.at[0])
        up_mine.start()
        up_groups = [[up_mine]] + copies(up_refs, up_layout, up, up_sems, 1)
        start_all(up_groups[1:])
        fetch_inverse = pltpu.make_async_copy(
            inverse_all.at[pl.ds(row, rows)], inverse, io_sems.at[1]
        )
        fetch_inverse.start()
        latent_from_odd = pltpu.make_async_copy(
            latent_odd.at[pl.ds(row, rows)], latent, io_sems.at[2]
        )
        latent_from_even = pltpu.make_async_copy(
            latent_even.at[pl.ds(row, rows)], latent, io_sems.at[2]
        )
        mine = pltpu.make_async_copy(down_own, down.at[0], sems.at[0])
        mine.start()
        odd_groups = [[mine]] + copies(odd_refs, down_layout, down, sems, 1)
        even_groups = [[mine]] + copies(even_refs, even_layout, down, sems, 1)

        @pl.when(odd == 1)
        def _():
            latent_from_odd.start()
            start_all(odd_groups[1:])

        @pl.when(odd == 0)
        def _():
            latent_from_even.start()
            start_all(even_groups[1:])

        fetch_x = pltpu.make_async_copy(x_all.at[pl.ds(row, rows)], x, io_sems.at[3])
        fetch_x.start()
        fetch.wait()
        keep = pltpu.make_async_copy(arriving, arrivals.at[pl.ds(row, rows)], io_sems.at[0])
        keep.start()
        hidden_grad = None
        for k in range(size):
            wait_all(up_groups[k])
            part = dot_nt(arriving[:, columns(dp_index, k, width)], up[k])
            hidden_grad = part if hidden_grad is None else hidden_grad + part
        fetch_inverse.wait()
        latent_from_odd.wait()
        lat = latent[...]
        lat_grad = (hidden_grad * silu_slope(lat)).astype(jnp.bfloat16)
        latent_grad[...] = lat_grad
        keep_grad = pltpu.make_async_copy(
            latent_grad, latent_grads.at[pl.ds(row, rows)], io_sems.at[4]
        )
        keep_grad.start()
        scale = inverse[:, :1]
        mean = jnp.sum(lat_grad.astype(jnp.float32) * lat, axis=-1, keepdims=True) / (width * size)
        slope = scale * scale * mean
        fetch_x.wait()
        for k in range(size):
            wait_all(odd_groups[k])
            at_k = columns(dp_index, k, width)
            scaled = dot_nt(lat_grad, down[k]) * gain[:, at_k].astype(jnp.float32)
            value = (
                arriving[:, at_k].astype(jnp.float32)
                + scale * scaled
                - x[:, at_k].astype(jnp.float32) * slope
            )
            result[:, at_k] = value.astype(jnp.bfloat16)
        put = pltpu.make_async_copy(result, send, io_sems.at[5])
        put.start()
        keep_result = pltpu.make_async_copy(result, grads.at[pl.ds(row, rows)], io_sems.at[6])
        keep_result.start()
        keep.wait()
        keep_grad.wait()
        put.wait()
        keep_result.wait()


def per_device(
    section_inputs, norm_gain, down_proj, up_proj, readout_matrix, ground_truth_series, valid_len
):
    size = lax.axis_size("dp")
    sections = lax.axis_size("section")
    top = sections - 1
    dp_index = lax.axis_index("dp")
    section = lax.axis_index("section")
    odds = [s for s in range(sections) if s % 2 == 1]
    evens = [s for s in range(sections) if s % 2 == 0]

    x = section_inputs[0]
    down_own, up_own = down_proj[0], up_proj[0]
    tokens, width = x.shape
    shard, latent_width = down_own.shape
    horizon = readout_matrix.shape[1]
    rows = tokens // CHUNKS

    values = x.astype(jnp.float32)
    inverse = lax.rsqrt(jnp.mean(values * values, axis=-1, keepdims=True) + EPSILON)
    normed = (values * inverse * norm_gain.astype(jnp.float32)).astype(jnp.bfloat16)
    inverse = jnp.broadcast_to(inverse, (tokens, 128))
    per_micro = tokens // valid_len.shape[0]
    mask = (
        (jnp.arange(per_micro)[None, :] < valid_len[:, None]).astype(jnp.float32).reshape(tokens, 1)
    )
    mask = jnp.broadcast_to(mask, (tokens, 128))

    head_own = jnp.concatenate(
        [readout_matrix, dot_nn(up_own, readout_matrix).astype(jnp.bfloat16)], axis=0
    )
    odd_pieces = gather_pieces(down_own, odds, size)
    head_pieces = gather_pieces(head_own, [top], size)
    up_pieces = gather_pieces(up_own, [s for s in range(sections) if s != top], size)
    even_pieces = gather_pieces(down_own, evens, size)

    odd = (section % 2).astype(jnp.int32)
    is_top = (section == top).astype(jnp.int32)
    zero = jnp.int32(0)

    def flags_at(active, row):
        return jnp.stack([dp_index.astype(jnp.int32), odd, is_top, active, row])

    still = flags_at(zero, zero)
    f32, bf16 = jnp.float32, jnp.bfloat16
    odd_refs, head_refs = flatten(odd_pieces), flatten(head_pieces)
    latent_odd, latent_grads, arrivals, grads = pl.pallas_call(
        functools.partial(top_kernel, size, shapes_of(odd_pieces), shapes_of(head_pieces)),
        out_shape=(
            jax.ShapeDtypeStruct((tokens, latent_width), f32),
            jax.ShapeDtypeStruct((tokens, latent_width), bf16),
            jax.ShapeDtypeStruct((tokens, width), bf16),
            jax.ShapeDtypeStruct((tokens, width), bf16),
        ),
        in_specs=[SMEM] + [VMEM] * 6 + [ANY] * (2 + len(odd_refs) + len(head_refs)),
        out_specs=(VMEM,) * 4,
        scratch_shapes=[
            pltpu.VMEM((size, shard, latent_width), bf16),
            pltpu.VMEM((size, shard + latent_width, horizon), bf16),
            pltpu.SemaphoreType.DMA((2 + len(odd_refs) + len(head_refs),)),
        ],
        compiler_params=PARAMS,
    )(
        still, x, normed, norm_gain, inverse, ground_truth_series, mask, down_own, head_own,
        *odd_refs, *head_refs,
    )

    even_refs = flatten(even_pieces)
    latent_even = pl.pallas_call(
        functools.partial(latent_kernel, size, shapes_of(even_pieces), 0),
        out_shape=jax.ShapeDtypeStruct((tokens, latent_width), f32),
        in_specs=[SMEM, VMEM] + [ANY] * (1 + len(even_refs)),
        out_specs=VMEM,
        scratch_shapes=[
            pltpu.VMEM((size, shard, latent_width), bf16),
            pltpu.SemaphoreType.DMA((1 + len(even_refs),)),
        ],
        compiler_params=PARAMS,
    )(still, normed, down_own, *even_refs)

    up_refs = flatten(up_pieces)
    fixed = 9 + len(odd_refs) + len(even_refs) + len(up_refs)
    tick = pl.pallas_call(
        functools.partial(
            tick_kernel, size, shapes_of(odd_pieces), shapes_of(even_pieces), shapes_of(up_pieces)
        ),
        out_shape=(
            jax.ShapeDtypeStruct((rows, width), bf16),
            jax.ShapeDtypeStruct((tokens, latent_width), bf16),
            jax.ShapeDtypeStruct((tokens, width), bf16),
            jax.ShapeDtypeStruct((tokens, width), bf16),
        ),
        in_specs=[SMEM, ANY, VMEM] + [ANY] * (fixed - 3 + 3),
        out_specs=(ANY,) * 4,
        input_output_aliases={fixed: 1, fixed + 1: 2, fixed + 2: 3},
        scratch_shapes=[
            pltpu.VMEM((size, shard, latent_width), bf16),
            pltpu.VMEM((size, latent_width, shard), bf16),
            pltpu.VMEM((rows, width), bf16),
            pltpu.VMEM((rows, width), bf16),
            pltpu.VMEM((rows, 128), f32),
            pltpu.VMEM((rows, latent_width), f32),
            pltpu.VMEM((rows, latent_width), bf16),
            pltpu.VMEM((rows, width), bf16),
            pltpu.SemaphoreType.DMA((1 + len(odd_refs),)),
            pltpu.SemaphoreType.DMA((1 + len(up_refs),)),
            pltpu.SemaphoreType.DMA((7,)),
        ],
        compiler_params=PARAMS,
    )

    def hop(block, senders):
        return move(
            block, [(s * size + i, (s - 1) * size + i) for s in senders for i in range(size)]
        )

    first = [hop(grads[c * rows : (c + 1) * rows], [top]) for c in range(CHUNKS)]
    send = None
    for step in range(1, top + CHUNKS):
        piece = step - (top - section)
        active = ((piece >= 0) & (piece < CHUNKS) & (section < top)).astype(jnp.int32)
        row = jnp.clip(piece, 0, CHUNKS - 1).astype(jnp.int32) * rows
        if send is None:
            received = first[0]
        else:
            senders = [
                s
                for s in range(1, top)
                if 0 <= step - 1 - (top - s) < CHUNKS
            ]
            received = hop(send, senders)
            if step - 1 < CHUNKS:
                received = jnp.where(section == top - 1, first[step - 1], received)
        send, latent_grads, arrivals, grads = tick(
            flags_at(active, row), received, norm_gain, x, inverse, latent_odd, latent_even,
            down_own, up_own, *odd_refs, *even_refs, *up_refs, latent_grads, arrivals, grads,
        )

    def exchange(block):
        out = [lax.dynamic_slice_in_dim(block, dp_index * shard, shard, 1)]
        for k in range(1, size):
            part = lax.dynamic_slice_in_dim(block, (dp_index ^ k) * shard, shard, 1)
            out.append(move(part, peers(range(sections), size, k)))
        return jnp.concatenate(out, axis=0)

    def spread(block):
        return jnp.concatenate(
            [block]
            + [move(block, peers(range(sections), size, k)) for k in range(1, size)],
            axis=0,
        )

    latent = jnp.where(odd == 1, latent_odd, latent_even)
    activated = jax.nn.silu(latent).astype(bf16)
    normed_columns = exchange(normed)
    activated_all = spread(activated)
    arriving_columns = exchange(arrivals)
    latent_grads_all = spread(latent_grads)
    down_grads = dot_tn(normed_columns, latent_grads_all).astype(bf16)
    up_grads = dot_tn(activated_all, arriving_columns).astype(bf16)
    return (grads[None], down_grads[None], up_grads[None])


def solution(mesh):
    placed = (
        P("section", "dp", None),
        P("section", None),
        P("section", "dp", None),
        P("section", None, "dp"),
        P("dp", None),
        P("dp", None),
        P("dp"),
    )
    return jax.shard_map(
        per_device,
        mesh=mesh,
        in_specs=placed,
        out_specs=(P("section", "dp", None), P("section", "dp", None), P("section", None, "dp")),
        check_vma=False,
    )
```

```python
import functools

import jax
import jax.numpy as jnp
from jax import lax
from jax.experimental import pallas as pl
from jax.experimental.pallas import tpu as pltpu
from jax.sharding import PartitionSpec as P

EPSILON = 1e-05
CHUNKS = 2
ANY = pl.BlockSpec(memory_space=pl.ANY)
VMEM = pl.BlockSpec(memory_space=pltpu.VMEM)
SMEM = pl.BlockSpec(memory_space=pltpu.SMEM)
PARAMS = pltpu.CompilerParams(vmem_limit_bytes=20 * 1024 * 1024)


def dot_nn(left, right):
    return lax.dot_general(
        left, right, (((1,), (0,)), ((), ())), preferred_element_type=jnp.float32
    )


def dot_nt(left, right):
    return lax.dot_general(
        left, right, (((1,), (1,)), ((), ())), preferred_element_type=jnp.float32
    )


def dot_tn(left, right):
    return lax.dot_general(
        left, right, (((0,), (0,)), ((), ())), preferred_element_type=jnp.float32
    )


def silu_slope(latent):
    sigmoid = jax.nn.sigmoid(latent)
    return sigmoid * (1.0 + latent * (1.0 - sigmoid))


def move(block, pairs):
    return lax.ppermute(block, ("section", "dp"), pairs)


def peers(sections, size, k):
    return [(s * size + i, s * size + (i ^ k)) for s in sections for i in range(size)]


def gather_pieces(block, sections, size, relay):
    rows = block.shape[0]
    if relay and size == 4:
        half = rows // 2
        from_x = move(block, peers(sections, size, 1))
        from_y = move(block, peers(sections, size, 2))
        low = move(from_y[:half], peers(sections, size, 1))
        high = move(from_x[half:], peers(sections, size, 2))
        return [[(0, rows, from_x)], [(0, rows, from_y)], [(0, half, low), (half, half, high)]]
    return [[(0, rows, move(block, peers(sections, size, k)))] for k in range(1, size)]


def flatten(pieces):
    return [part[2] for piece in pieces for part in piece]


def shapes_of(pieces):
    return [[(row, count) for row, count, _ in piece] for piece in pieces]


def pin(block):
    return pltpu.with_memory_space_constraint(block, pltpu.VMEM)


def columns(dp_index, k, width):
    return pl.ds(pl.multiple_of((dp_index ^ k) * width, width), width)


def top_kernel(size, layout, head_layout, *refs):
    flags, x, normed, gain, inverse, truth, mask = refs[:7]
    count = 1 + sum(len(parts) for parts in layout)
    head_count = 1 + sum(len(parts) for parts in head_layout)
    pieces = refs[7 : 7 + count]
    head_pieces = refs[7 + count : 7 + count + head_count]
    latent_out, latent_grad_out, arriving_out, grads_out, held, head, sems = refs[
        7 + count + head_count :
    ]
    dp_index = flags[0]
    width = held.shape[1]

    @pl.when(flags[2] == 1)
    def _():
        groups, at = [], 0
        for refs_of, layout_of, place in ((pieces, layout, held), (head_pieces, head_layout, head)):
            rows = place.shape[1]
            ref_at = 0
            for slot, parts in enumerate([[(0, rows)]] + layout_of):
                group = []
                for row, part_rows in parts:
                    copy = pltpu.make_async_copy(
                        refs_of[ref_at], place.at[slot, pl.ds(row, part_rows)], sems.at[at]
                    )
                    copy.start()
                    group.append(copy)
                    ref_at += 1
                    at += 1
                groups.append(group)
        latent = None
        for k in range(size):
            for copy in groups[k]:
                copy.wait()
            part = dot_nn(normed[:, columns(dp_index, k, width)], held[k])
            latent = part if latent is None else latent + part
        latent_out[...] = latent
        activated = jax.nn.silu(latent).astype(jnp.bfloat16)
        estimate = None
        product = None
        for k in range(size):
            for copy in groups[size + k]:
                copy.wait()
            part = dot_nn(x[:, columns(dp_index, k, width)], head[k, :width])
            extra = head[k, width:].astype(jnp.float32)
            estimate = part if estimate is None else estimate + part
            product = extra if product is None else product + extra
        product = product.astype(jnp.bfloat16)
        estimate = estimate + dot_nn(activated, product)
        error = (mask[:, :1] * (estimate - truth[...])).astype(jnp.bfloat16)
        hidden_grad = dot_nt(error, product)
        latent_grad = (hidden_grad * silu_slope(latent)).astype(jnp.bfloat16)
        latent_grad_out[...] = latent_grad
        scale = inverse[:, :1]
        mean = jnp.sum(latent_grad.astype(jnp.float32) * latent, axis=-1, keepdims=True) / (
            width * size
        )
        slope = scale * scale * mean
        for k in range(size):
            at_k = columns(dp_index, k, width)
            arriving = dot_nt(error, head[k, :width]).astype(jnp.bfloat16)
            arriving_out[:, at_k] = arriving
            scaled = dot_nt(latent_grad, held[k]) * gain[:, at_k].astype(jnp.float32)
            grads = (
                arriving.astype(jnp.float32)
                + scale * scaled
                - x[:, at_k].astype(jnp.float32) * slope
            )
            grads_out[:, at_k] = grads.astype(jnp.bfloat16)


def assemble_kernel(size, down_layout, up_layout, *refs):
    flags, normed, latent_in = refs[:3]
    down_count = 1 + sum(len(parts) for parts in down_layout)
    up_count = 1 + sum(len(parts) for parts in up_layout)
    down_refs = refs[3 : 3 + down_count]
    up_refs = refs[3 + down_count : 3 + down_count + up_count]
    latent, down, up, sems = refs[3 + down_count + up_count :]
    dp_index = flags[0]
    width = down.shape[0] // size
    latent_rows = up.shape[0] // size

    @pl.when(flags[2] == 0)
    def _():
        at = 0
        groups = []
        for refs_of, layout_of, place, rows in (
            (down_refs, down_layout, down, width),
            (up_refs, up_layout, up, latent_rows),
        ):
            ref_at = 0
            for slot, parts in enumerate([[(0, rows)]] + layout_of):
                group = []
                for row, part_rows in parts:
                    start = pl.multiple_of((dp_index ^ slot) * rows + row, 128)
                    copy = pltpu.make_async_copy(
                        refs_of[ref_at], place.at[pl.ds(start, part_rows)], sems.at[at]
                    )
                    copy.start()
                    group.append(copy)
                    ref_at += 1
                    at += 1
                groups.append(group)
        total = None
        for k in range(size):
            for copy in groups[k]:
                copy.wait()
            at_k = columns(dp_index, k, width)
            part = dot_nn(normed[:, at_k], down[at_k, :])
            total = part if total is None else total + part
        latent[...] = total
        for k in range(size):
            for copy in groups[size + k]:
                copy.wait()


def tick_kernel(step, size, sections, *refs):
    flags, received, gain, inverse = refs[:4]
    send, latent, down, up, x, latent_grads, arrivals, grads = refs[11:]
    rows, width = received.shape
    shard = width // size
    top = sections - 1
    section = flags[1]
    piece = step - (top - section)

    if step < CHUNKS:

        @pl.when(section == top)
        def _():
            send[...] = grads[step * rows : (step + 1) * rows]

    @pl.when((section < top) & (piece >= 0) & (piece < CHUNKS))
    def _():
        at_rows = pl.ds(pl.multiple_of(piece * rows, rows), rows)
        hidden_grad = None
        for k in range(size):
            at_k = slice(k * shard, (k + 1) * shard)
            part = dot_nt(received[:, at_k], up[k * up.shape[0] // size : (k + 1) * up.shape[0] // size])
            hidden_grad = part if hidden_grad is None else hidden_grad + part
        lat = latent[at_rows]
        latent_grad = (hidden_grad * silu_slope(lat)).astype(jnp.bfloat16)
        latent_grads[at_rows] = latent_grad
        scale = inverse[at_rows][:, :1]
        mean = jnp.sum(latent_grad.astype(jnp.float32) * lat, axis=-1, keepdims=True) / width
        slope = scale * scale * mean
        for k in range(size):
            at_k = slice(k * shard, (k + 1) * shard)
            arriving = received[:, at_k]
            arrivals[at_rows, at_k] = arriving
            scaled = dot_nt(latent_grad, down[at_k]) * gain[:, at_k].astype(jnp.float32)
            value = (
                arriving.astype(jnp.float32)
                + scale * scaled
                - x[at_rows, at_k].astype(jnp.float32) * slope
            ).astype(jnp.bfloat16)
            send[:, at_k] = value
            grads[at_rows, at_k] = value


def per_device(
    section_inputs, norm_gain, down_proj, up_proj, readout_matrix, ground_truth_series, valid_len
):
    size = lax.axis_size("dp")
    sections = lax.axis_size("section")
    top = sections - 1
    dp_index = lax.axis_index("dp")
    section = lax.axis_index("section")
    f32, bf16 = jnp.float32, jnp.bfloat16

    x = section_inputs[0]
    down_own, up_own = down_proj[0], up_proj[0]
    tokens, width = x.shape
    shard, latent_width = down_own.shape
    horizon = readout_matrix.shape[1]
    rows = tokens // CHUNKS

    down_top = gather_pieces(down_own, [top], size, False)
    head_own = jnp.concatenate(
        [readout_matrix, dot_nn(up_own, readout_matrix).astype(bf16)], axis=0
    )
    head_pieces = gather_pieces(head_own, [top], size, False)

    values = x.astype(f32)
    inverse = lax.rsqrt(jnp.mean(values * values, axis=-1, keepdims=True) + EPSILON)
    normed = (values * inverse * norm_gain.astype(f32)).astype(bf16)
    inverse = jnp.broadcast_to(inverse, (tokens, 128))
    per_micro = tokens // valid_len.shape[0]
    mask = (
        (jnp.arange(per_micro)[None, :] < valid_len[:, None]).astype(f32).reshape(tokens, 1)
    )
    mask = jnp.broadcast_to(mask, (tokens, 128))

    rest = list(range(top))
    up_rest, down_rest, _ = lax.optimization_barrier((up_own, down_own, down_top[0][0][2]))
    up_pieces = gather_pieces(up_rest, rest, size, True)
    down_pieces = gather_pieces(down_rest, rest, size, True)

    flags = jnp.stack(
        [dp_index.astype(jnp.int32), section.astype(jnp.int32), (section == top).astype(jnp.int32)]
    )

    down_refs = [down_own] + flatten(down_top)
    head_refs = [head_own] + flatten(head_pieces)
    latent, latent_grads, arrivals, grads = pl.pallas_call(
        functools.partial(top_kernel, size, shapes_of(down_top), shapes_of(head_pieces)),
        out_shape=(
            pltpu.VMEM((tokens, latent_width), f32),
            pltpu.VMEM((tokens, latent_width), bf16),
            pltpu.VMEM((tokens, width), bf16),
            pltpu.VMEM((tokens, width), bf16),
        ),
        in_specs=[SMEM] + [VMEM] * 6 + [ANY] * (len(down_refs) + len(head_refs)),
        out_specs=(VMEM,) * 4,
        scratch_shapes=[
            pltpu.VMEM((size, shard, latent_width), bf16),
            pltpu.VMEM((size, shard + latent_width, horizon), bf16),
            pltpu.SemaphoreType.DMA((len(down_refs) + len(head_refs),)),
        ],
        compiler_params=PARAMS,
    )(flags, x, normed, norm_gain, inverse, ground_truth_series, mask, *down_refs, *head_refs)

    def hop(block, senders):
        return move(
            block, [(s * size + i, (s - 1) * size + i) for s in senders for i in range(size)]
        )

    received = hop(grads[:rows], [top])

    down_refs = [down_own] + flatten(down_pieces)
    up_refs = [up_own] + flatten(up_pieces)
    latent, down, up = pl.pallas_call(
        functools.partial(assemble_kernel, size, shapes_of(down_pieces), shapes_of(up_pieces)),
        out_shape=(
            pltpu.VMEM((tokens, latent_width), f32),
            pltpu.VMEM((width, latent_width), bf16),
            pltpu.VMEM((size * latent_width, shard), bf16),
        ),
        in_specs=[SMEM, VMEM, VMEM] + [ANY] * (len(down_refs) + len(up_refs)),
        out_specs=(VMEM,) * 3,
        input_output_aliases={2: 0},
        scratch_shapes=[pltpu.SemaphoreType.DMA((len(down_refs) + len(up_refs),))],
        compiler_params=PARAMS,
    )(flags, normed, pin(latent), *down_refs, *up_refs)

    state = (latent, down, up, x, latent_grads, arrivals, grads)

    def tick(step, received, state):
        out = pl.pallas_call(
            functools.partial(tick_kernel, step, size, sections),
            out_shape=(jax.ShapeDtypeStruct((rows, width), bf16),)
            + tuple(pltpu.VMEM(part.shape, part.dtype) for part in state),
            in_specs=[SMEM, VMEM, VMEM, VMEM] + [VMEM] * len(state),
            out_specs=(VMEM,) * (1 + len(state)),
            input_output_aliases={4 + i: 1 + i for i in range(len(state))},
            compiler_params=PARAMS,
        )(flags, received, norm_gain, inverse, *[pin(part) for part in state])
        return out[0], tuple(out[1:])

    def exchange(block):
        out = [lax.dynamic_slice_in_dim(block, dp_index * shard, shard, 1)]
        for k in range(1, size):
            part = lax.dynamic_slice_in_dim(block, (dp_index ^ k) * shard, shard, 1)
            out.append(move(part, peers(range(sections), size, k)))
        return out

    def spread(block):
        return jnp.concatenate(
            [block]
            + [move(block, peers(range(sections), size, k)) for k in range(1, size)],
            axis=0,
        )

    exchanged = []
    for step in range(1, top + CHUNKS):
        if step >= top:
            piece = step - top
            block = state[5][piece * rows : (piece + 1) * rows]
            exchanged.append(exchange(jnp.where(section == 0, received, block)))
        send, state = tick(step, received, state)
        senders = [s for s in range(1, sections) if 0 <= step - (top - s) < CHUNKS]
        if senders:
            received = hop(send, senders)
    latent, _, _, _, latent_grads, arrivals, grads = state

    activated = jax.nn.silu(latent).astype(bf16)
    normed_columns = jnp.concatenate(exchange(normed), axis=0)
    activated_all = spread(activated)
    arriving_columns = jnp.concatenate(
        [exchanged[piece][k] for k in range(size) for piece in range(CHUNKS)], axis=0
    )
    latent_grads_all = spread(latent_grads)
    down_grads = dot_tn(normed_columns, latent_grads_all).astype(bf16)
    up_grads = dot_tn(activated_all, arriving_columns).astype(bf16)
    return (grads[None], down_grads[None], up_grads[None])


def solution(mesh):
    placed = (
        P("section", "dp", None),
        P("section", None),
        P("section", "dp", None),
        P("section", None, "dp"),
        P("dp", None),
        P("dp", None),
        P("dp"),
    )
    return jax.shard_map(
        per_device,
        mesh=mesh,
        in_specs=placed,
        out_specs=(P("section", "dp", None), P("section", "dp", None), P("section", None, "dp")),
        check_vma=False,
    )
```

```python
import functools

import jax
import jax.numpy as jnp
from jax import lax
from jax.experimental import pallas as pl
from jax.experimental.pallas import tpu as pltpu
from jax.sharding import PartitionSpec as P

EPSILON = 1e-05
CHUNKS = 2
VMEM = pl.BlockSpec(memory_space=pltpu.VMEM)
SMEM = pl.BlockSpec(memory_space=pltpu.SMEM)
PARAMS = pltpu.CompilerParams(vmem_limit_bytes=20 * 1024 * 1024)


def dot_nn(left, right):
    return lax.dot_general(
        left, right, (((1,), (0,)), ((), ())), preferred_element_type=jnp.float32
    )


def dot_nt(left, right):
    return lax.dot_general(
        left, right, (((1,), (1,)), ((), ())), preferred_element_type=jnp.float32
    )


def dot_tn(left, right):
    return lax.dot_general(
        left, right, (((0,), (0,)), ((), ())), preferred_element_type=jnp.float32
    )


def silu_slope(latent):
    sigmoid = jax.nn.sigmoid(latent)
    return sigmoid * (1.0 + latent * (1.0 - sigmoid))


def move(block, pairs):
    return lax.ppermute(block, ("section", "dp"), pairs)


def peers(sections, size, k):
    return [(s * size + i, s * size + (i ^ k)) for s in sections for i in range(size)]


def gather_pieces(block, sections, size, relay):
    rows = block.shape[0]
    if relay and size == 4:
        half = rows // 2
        from_x = move(block, peers(sections, size, 1))
        from_y = move(block, peers(sections, size, 2))
        low = move(from_y[:half], peers(sections, size, 1))
        high = move(from_x[half:], peers(sections, size, 2))
        return [[(0, rows, from_x)], [(0, rows, from_y)], [(0, half, low), (half, half, high)]]
    return [[(0, rows, move(block, peers(sections, size, k)))] for k in range(1, size)]


def flatten(pieces):
    return [part[2] for piece in pieces for part in piece]


def shapes_of(pieces):
    return [[(row, count) for row, count, _ in piece] for piece in pieces]


def pin(block):
    return pltpu.with_memory_space_constraint(block, pltpu.VMEM)


def held_like(block):
    return pltpu.VMEM(block.shape, block.dtype)


def columns(dp_index, k, width):
    return pl.ds(pl.multiple_of((dp_index ^ k) * width, width), width)


def by_slot(refs, layout):
    out, at = [], 0
    for parts in layout:
        out.append([(row, rows, refs[at + i]) for i, (row, rows) in enumerate(parts)])
        at += len(parts)
    return out


def shift(dp_index, k, width, row, rows):
    return pl.ds(pl.multiple_of((dp_index ^ k) * width + row, 128), rows)


def head_kernel(readout, up, out):
    shard = readout.shape[0]
    out[:shard] = readout[...]
    out[shard:] = dot_nn(up[...], readout[...]).astype(jnp.bfloat16)


def norm_kernel(x, gain, x_out, normed_out, inverse_out):
    values = x[...].astype(jnp.float32)
    inverse = lax.rsqrt(jnp.mean(values * values, axis=-1, keepdims=True) + EPSILON)
    x_out[...] = x[...]
    normed_out[...] = (values * inverse * gain[...].astype(jnp.float32)).astype(jnp.bfloat16)
    inverse_out[...] = jnp.broadcast_to(inverse, inverse_out.shape)


def top_kernel(size, layout, head_layout, *refs):
    flags, gain, truth, mask = refs[:4]
    count = sum(len(parts) for parts in layout)
    head_count = sum(len(parts) for parts in head_layout)
    pieces = by_slot(refs[7 : 7 + count], layout)
    head = by_slot(refs[7 + count : 7 + count + head_count], head_layout)
    x, normed, inverse, latent_out, latent_grad_out, arriving_out, grads_out = refs[
        7 + count + head_count : 14 + count + head_count
    ]
    sends = refs[14 + count + head_count :]
    dp_index = flags[0]
    width = x.shape[1] // size
    rows = sends[0].shape[0]

    @pl.when(flags[2] == 1)
    def _():
        latent = None
        for k in range(size):
            for row, count, ref in pieces[k]:
                part = dot_nn(normed[:, shift(dp_index, k, width, row, count)], ref[...])
                latent = part if latent is None else latent + part
        latent_out[...] = latent
        activated = jax.nn.silu(latent).astype(jnp.bfloat16)
        estimate = None
        product = None
        for k in range(size):
            ref = head[k][0][2]
            part = dot_nn(x[:, columns(dp_index, k, width)], ref[:width])
            extra = ref[width:].astype(jnp.float32)
            estimate = part if estimate is None else estimate + part
            product = extra if product is None else product + extra
        product = product.astype(jnp.bfloat16)
        estimate = estimate + dot_nn(activated, product)
        error = (mask[:, :1] * (estimate - truth[...])).astype(jnp.bfloat16)
        hidden_grad = dot_nt(error, product)
        latent_grad = (hidden_grad * silu_slope(latent)).astype(jnp.bfloat16)
        latent_grad_out[...] = latent_grad
        scale = inverse[:, :1]
        mean = jnp.sum(latent_grad.astype(jnp.float32) * latent, axis=-1, keepdims=True) / (
            width * size
        )
        slope = scale * scale * mean
        for k in range(size):
            for row, count, ref in pieces[k]:
                at_k = shift(dp_index, k, width, row, count)
                arriving = dot_nt(error, head[k][0][2][row : row + count]).astype(jnp.bfloat16)
                arriving_out[:, at_k] = arriving
                scaled = dot_nt(latent_grad, ref[...]) * gain[:, at_k].astype(jnp.float32)
                grads = (
                    arriving.astype(jnp.float32)
                    + scale * scaled
                    - x[:, at_k].astype(jnp.float32) * slope
                ).astype(jnp.bfloat16)
                grads_out[:, at_k] = grads
                for i, send in enumerate(sends):
                    send[:, at_k] = grads[i * rows : (i + 1) * rows]


def latent_kernel(size, layout, *refs):
    flags = refs[0]
    count = sum(len(parts) for parts in layout)
    normed, latent = refs[3 + count : 5 + count]
    down = by_slot(refs[5 + count :], layout)
    width = normed.shape[1] // size

    @pl.when(flags[2] == 0)
    def _():
        total = None
        for k in range(size):
            for row, rows, ref in down[k]:
                part = dot_nn(normed[:, shift(flags[0], k, width, row, rows)], ref[...])
                total = part if total is None else total + part
        latent[...] = total


def message_kernel(size, *refs):
    flags = refs[0]
    normed, latent = refs[3:5]
    messages = refs[5:]
    shard = normed.shape[1] // size
    activated = jax.nn.silu(latent[...]).astype(jnp.bfloat16)
    for k in range(size):
        messages[k][:, :shard] = normed[:, columns(flags[0], k, shard)]
        messages[k][:, shard:] = activated


def stage_kernel(stage, piece, size, down_layout, up_layout, *refs):
    flags, received = refs[:2]
    down_count = sum(len(parts) for parts in down_layout)
    held = 7 + down_count + sum(len(parts) for parts in up_layout)
    state = refs[2 + held : 2 + 2 * held]
    gain, inverse, latent, x, latent_grads, arrivals, grads = state[:7]
    down = by_slot(state[7 : 7 + down_count], down_layout)
    up = by_slot(state[7 + down_count :], up_layout)
    outs = refs[2 + 2 * held :]
    rows, width = received.shape
    shard = width // size
    at_rows = slice(piece * rows, (piece + 1) * rows)

    @pl.when(flags[1] == stage)
    def _():
        hidden_grad = None
        for k in range(size):
            block = received[:, columns(flags[0], k, shard)]
            parts = [dot_nt(block, ref[...]) for _, _, ref in up[k]]
            part = parts[0] if len(parts) == 1 else jnp.concatenate(parts, axis=1)
            hidden_grad = part if hidden_grad is None else hidden_grad + part
        lat = latent[at_rows]
        latent_grad = (hidden_grad * silu_slope(lat)).astype(jnp.bfloat16)
        latent_grads[at_rows] = latent_grad
        scale = inverse[at_rows][:, :1]
        mean = jnp.sum(latent_grad.astype(jnp.float32) * lat, axis=-1, keepdims=True) / width
        slope = scale * scale * mean
        for k in range(size):
            for row, count, ref in down[k]:
                at_k = shift(flags[0], k, shard, row, count)
                arriving = received[:, at_k]
                arrivals[at_rows, at_k] = arriving
                scaled = dot_nt(latent_grad, ref[...]) * gain[:, at_k].astype(jnp.float32)
                value = (
                    arriving.astype(jnp.float32)
                    + scale * scaled
                    - x[at_rows, at_k].astype(jnp.float32) * slope
                ).astype(jnp.bfloat16)
                grads[at_rows, at_k] = value
                if stage:
                    outs[0][:, at_k] = value

    if stage == 0:
        for k in range(size):
            outs[k][:, :shard] = arrivals[at_rows, columns(flags[0], k, shard)]
            outs[k][:, shard:] = latent_grads[at_rows]


def weight_kernel(size, *refs):
    early = refs[:size]
    late = refs[size : size + size * CHUNKS]
    down_grads, up_grads, left, right = refs[size + size * CHUNKS :]
    tokens = early[0].shape[0]
    rows = tokens // CHUNKS
    shard = down_grads.shape[0]
    for k in range(size):
        left[k * tokens : (k + 1) * tokens] = early[k][...]
        for i in range(CHUNKS):
            at = k * tokens + i * rows
            right[at : at + rows] = late[i * size + k][...]
    down_grads[...] = dot_tn(left[:, :shard], right[:, shard:]).astype(jnp.bfloat16)
    up_grads[...] = dot_tn(left[:, shard:], right[:, :shard]).astype(jnp.bfloat16)


def per_device(
    section_inputs, norm_gain, down_proj, up_proj, readout_matrix, ground_truth_series, valid_len
):
    size = lax.axis_size("dp")
    sections = lax.axis_size("section")
    top = sections - 1
    dp_index = lax.axis_index("dp")
    section = lax.axis_index("section")
    f32, bf16 = jnp.float32, jnp.bfloat16

    x = section_inputs[0]
    down_own, up_own = down_proj[0], up_proj[0]
    tokens, width = x.shape
    shard, latent_width = down_own.shape
    horizon = readout_matrix.shape[1]
    rows = tokens // CHUNKS

    flags = jnp.stack(
        [dp_index.astype(jnp.int32), section.astype(jnp.int32), (section == top).astype(jnp.int32)]
    )
    down_top = gather_pieces(down_own, [top], size, False)
    head_own = pl.pallas_call(
        head_kernel,
        out_shape=jax.ShapeDtypeStruct((shard + latent_width, horizon), bf16),
        in_specs=[VMEM] * 2,
        out_specs=VMEM,
        compiler_params=PARAMS,
    )(readout_matrix, up_own)
    head_pieces = gather_pieces(head_own, [top], size, False)

    x, normed, inverse = pl.pallas_call(
        norm_kernel,
        out_shape=(
            pltpu.VMEM((tokens, width), bf16),
            pltpu.VMEM((tokens, width), bf16),
            pltpu.VMEM((tokens, 128), f32),
        ),
        in_specs=[VMEM] * 2,
        out_specs=(VMEM,) * 3,
        compiler_params=PARAMS,
    )(x, norm_gain)
    per_micro = tokens // valid_len.shape[0]
    mask = (
        (jnp.arange(per_micro)[None, :] < valid_len[:, None]).astype(f32).reshape(tokens, 1)
    )
    mask = jnp.broadcast_to(mask, (tokens, 128))

    rest = list(range(top))
    token = move(
        down_top[0][0][2][:16, :128], [(top * size + i, (top - 1) * size + i) for i in range(size)]
    )
    up_rest, down_rest, _ = lax.optimization_barrier((up_own, down_own, token))
    up_pieces = gather_pieces(up_rest, rest, size, False)
    down_pieces = gather_pieces(down_rest, rest, size, False)

    down_refs = [pin(part) for part in [down_own] + flatten(down_top)]
    head_refs = [pin(part) for part in [head_own] + flatten(head_pieces)]
    down_layout = [[(0, shard)]] + shapes_of(down_top)
    head_layout = [[(0, shard + latent_width)]] + shapes_of(head_pieces)
    x, normed, inverse, latent, latent_grads, arrivals, grads, *sends = pl.pallas_call(
        functools.partial(top_kernel, size, down_layout, head_layout),
        out_shape=(
            held_like(x),
            held_like(normed),
            held_like(inverse),
            pltpu.VMEM((tokens, latent_width), f32),
            pltpu.VMEM((tokens, latent_width), bf16),
            pltpu.VMEM((tokens, width), bf16),
            pltpu.VMEM((tokens, width), bf16),
        )
        + (jax.ShapeDtypeStruct((rows, width), bf16),) * CHUNKS,
        in_specs=[SMEM] + [VMEM] * (6 + len(down_refs) + len(head_refs)),
        out_specs=(VMEM,) * (7 + CHUNKS),
        input_output_aliases={4: 0, 5: 1, 6: 2},
        compiler_params=PARAMS,
    )(
        flags, norm_gain, ground_truth_series, mask, pin(x), pin(normed), pin(inverse),
        *down_refs, *head_refs,
    )

    def hop(block, sender):
        return move(block, [(sender * size + i, (sender - 1) * size + i) for i in range(size)])

    received = [hop(send, top) for send in sends]

    down_refs = [down_own] + flatten(down_pieces)
    up_refs = [up_own] + flatten(up_pieces)
    down_layout = [[(0, shard)]] + shapes_of(down_pieces)
    up_layout = [[(0, latent_width)]] + shapes_of(up_pieces)
    normed, latent, *down_refs = pl.pallas_call(
        functools.partial(latent_kernel, size, down_layout),
        out_shape=tuple(held_like(part) for part in (normed, latent, *down_refs)),
        in_specs=[SMEM] + [VMEM] * (2 + len(down_refs)),
        out_specs=(VMEM,) * (2 + len(down_refs)),
        input_output_aliases={1 + i: i for i in range(2 + len(down_refs))},
        compiler_params=PARAMS,
    )(flags, pin(normed), pin(latent), *[pin(part) for part in down_refs])

    message = jax.ShapeDtypeStruct((tokens, shard + latent_width), bf16)
    late_message = jax.ShapeDtypeStruct((rows, shard + latent_width), bf16)
    state = (norm_gain, inverse, latent, x, latent_grads, arrivals, grads, *down_refs, *up_refs)

    def run_stage(stage, piece, received, state):
        outs = (late_message,) * size if stage == 0 else (jax.ShapeDtypeStruct((rows, width), bf16),)
        results = pl.pallas_call(
            functools.partial(stage_kernel, stage, piece, size, down_layout, up_layout),
            out_shape=tuple(held_like(part) for part in state) + outs,
            in_specs=[SMEM] + [VMEM] * (1 + len(state)),
            out_specs=(VMEM,) * (len(state) + len(outs)),
            input_output_aliases={2 + i: i for i in range(len(state))},
            compiler_params=PARAMS,
        )(flags, received, *[pin(part) for part in state])
        return tuple(results[: len(state)]), results[len(state) :]

    def send_messages(messages):
        return [messages[0]] + [
            move(messages[k], peers(range(sections), size, k)) for k in range(1, size)
        ]

    late = []
    for stage in range(top - 1, -1, -1):
        sent = []
        for piece in range(CHUNKS):
            state, outs = run_stage(stage, piece, received[piece], state)
            if stage:
                sent.append(hop(outs[0], stage))
            else:
                late += send_messages(outs)
        received = sent
        if stage == top - 1:
            _, latent, *messages = pl.pallas_call(
                functools.partial(message_kernel, size),
                out_shape=(held_like(normed), held_like(latent)) + (message,) * size,
                in_specs=[SMEM, VMEM, VMEM],
                out_specs=(VMEM,) * (2 + size),
                input_output_aliases={1: 0, 2: 1},
                compiler_params=PARAMS,
            )(flags, pin(normed), pin(state[2]))
            state = state[:2] + (latent,) + state[3:]
            early = send_messages(messages)

    down_grads, up_grads = pl.pallas_call(
        functools.partial(weight_kernel, size),
        out_shape=(
            jax.ShapeDtypeStruct((shard, latent_width), bf16),
            jax.ShapeDtypeStruct((latent_width, shard), bf16),
        ),
        in_specs=[VMEM] * (size * (1 + CHUNKS)),
        out_specs=(VMEM,) * 2,
        scratch_shapes=[pltpu.VMEM((size * tokens, shard + latent_width), bf16)] * 2,
        compiler_params=PARAMS,
    )(*early, *late)
    return (state[6][None], down_grads[None], up_grads[None])


def solution(mesh):
    placed = (
        P("section", "dp", None),
        P("section", None),
        P("section", "dp", None),
        P("section", None, "dp"),
        P("dp", None),
        P("dp", None),
        P("dp"),
    )
    return jax.shard_map(
        per_device,
        mesh=mesh,
        in_specs=placed,
        out_specs=(P("section", "dp", None), P("section", "dp", None), P("section", None, "dp")),
        check_vma=False,
    )
```

```python
import functools

import jax
import jax.numpy as jnp
from jax import lax
from jax.experimental import pallas as pl
from jax.experimental.pallas import tpu as pltpu
from jax.sharding import PartitionSpec as P

EPSILON = 1e-05
CHUNK_SHARES = (4, 4)
ANY = pl.BlockSpec(memory_space=pl.ANY)
VMEM = pl.BlockSpec(memory_space=pltpu.VMEM)
SMEM = pl.BlockSpec(memory_space=pltpu.SMEM)
PARAMS = pltpu.CompilerParams(vmem_limit_bytes=20 * 1024 * 1024)


def dot_nn(left, right):
    return lax.dot_general(
        left, right, (((1,), (0,)), ((), ())), preferred_element_type=jnp.float32
    )


def dot_nt(left, right):
    return lax.dot_general(
        left, right, (((1,), (1,)), ((), ())), preferred_element_type=jnp.float32
    )


def dot_tn(left, right):
    return lax.dot_general(
        left, right, (((0,), (0,)), ((), ())), preferred_element_type=jnp.float32
    )


def silu_slope(latent):
    sigmoid = jax.nn.sigmoid(latent)
    return sigmoid * (1.0 + latent * (1.0 - sigmoid))


def move(block, pairs):
    return lax.ppermute(block, ("section", "dp"), pairs)


def peers(sections, size, k):
    return [(s * size + i, s * size + (i ^ k)) for s in sections for i in range(size)]


def gather(block, sections, size):
    return [block] + [move(block, peers(sections, size, k)) for k in range(1, size)]


def gather_halves(low, high, sections, size):
    if size != 4:
        return list(zip(gather(low, sections, size), gather(high, sections, size)))
    across, along = peers(sections, size, 1), peers(sections, size, 2)
    low_along = move(low, along)
    high_across = move(high, across)
    high_along = move(high, along)
    low_across = move(low, across)
    low_far = move(low_along, across)
    high_far = move(high_across, along)
    return [(low, high), (low_across, high_across), (low_along, high_along), (low_far, high_far)]


def pin(block):
    return pltpu.with_memory_space_constraint(block, pltpu.VMEM)


def stay(block):
    return pltpu.with_memory_space_constraint(block, pltpu.HBM)


def held_like(block):
    return pltpu.VMEM(block.shape, block.dtype)


def columns(dp_index, k, width):
    return pl.ds(pl.multiple_of((dp_index ^ k) * width, width), width)


def half_columns(dp_index, k, half, width):
    start = (dp_index ^ k) * width + half * (width // 2)
    return pl.ds(pl.multiple_of(start, width // 2), width // 2)


def down_kernel(down, low, high, held, sem):
    copy = pltpu.make_async_copy(down, held, sem)
    copy.start()
    copy.wait()
    turned = held[0].T
    half = turned.shape[1] // 2
    low[...] = turned[:, :half]
    high[...] = turned[:, half:]


def up_kernel(up, readout, up_out, head, up_held, readout_held, sems):
    copies = [
        pltpu.make_async_copy(up, up_held, sems.at[0]),
        pltpu.make_async_copy(readout, readout_held, sems.at[1]),
    ]
    for copy in copies:
        copy.start()
    for copy in copies:
        copy.wait()
    latent_width, shard = up_held.shape[1:]
    horizon = readout_held.shape[1]
    values = up_held[0]
    product = dot_nn(values, readout_held[...]).astype(jnp.bfloat16)
    head[:horizon] = readout_held[...].T
    rows = latent_width * horizon // shard
    for at in range(0, shard, horizon):
        row = at // horizon * rows
        head[horizon:, at : at + horizon] = product[row : row + rows]
    block = min(latent_width, shard)
    for at in range(0, shard, block):
        up_out[:, at // block * latent_width : (at // block + 1) * latent_width] = values[
            :, at : at + block
        ].T


def norm_kernel(x, gain, x_out, normed_out, inverse_out, gain_out):
    values = x[...].astype(jnp.float32)
    inverse = lax.rsqrt(jnp.mean(values * values, axis=-1, keepdims=True) + EPSILON)
    x_out[...] = x[...]
    normed_out[...] = (values * inverse * gain[...].astype(jnp.float32)).astype(jnp.bfloat16)
    inverse_out[...] = jnp.broadcast_to(inverse, inverse_out.shape)
    gain_out[...] = gain[...]


def top_kernel(size, bounds, *refs):
    flags, truth, mask = refs[:3]
    down = refs[7 : 7 + 2 * size]
    head = refs[7 + 2 * size : 7 + 3 * size]
    gain, x, inverse, latent_ref, latent_grad_out, arriving_out, grads_out = refs[
        7 + 3 * size : 14 + 3 * size
    ]
    sends = refs[14 + 3 * size :]
    dp_index = flags[0]
    width = x.shape[1] // size
    horizon = truth.shape[1]

    @pl.when(flags[2] == 1)
    def _():
        latent = latent_ref[...]
        activated = jax.nn.silu(latent).astype(jnp.bfloat16)
        estimate = None
        product = None
        for k in range(size):
            part = dot_nt(x[:, columns(dp_index, k, width)], head[k][:horizon])
            extra = jnp.concatenate(
                [head[k][horizon:, at : at + horizon] for at in range(0, width, horizon)], axis=0
            ).astype(jnp.float32)
            estimate = part if estimate is None else estimate + part
            product = extra if product is None else product + extra
        product = product.astype(jnp.bfloat16)
        estimate = estimate + dot_nn(activated, product)
        error = (mask[:, :1] * (estimate - truth[...])).astype(jnp.bfloat16)
        hidden_grad = dot_nt(error, product)
        latent_grad = (hidden_grad * silu_slope(latent)).astype(jnp.bfloat16)
        latent_grad_out[...] = latent_grad
        scale = inverse[:, :1]
        mean = jnp.sum(latent_grad.astype(jnp.float32) * latent, axis=-1, keepdims=True) / (
            width * size
        )
        slope = scale * scale * mean
        for k in range(size):
            for half in range(2):
                at_k = half_columns(dp_index, k, half, width)
                here = slice(half * (width // 2), (half + 1) * (width // 2))
                arriving = dot_nn(error, head[k][:horizon, here]).astype(jnp.bfloat16)
                arriving_out[:, at_k] = arriving
                scaled = dot_nn(latent_grad, down[2 * k + half][...])
                grads = (
                    arriving.astype(jnp.float32)
                    + scale * (scaled * gain[:, at_k].astype(jnp.float32))
                    - x[:, at_k].astype(jnp.float32) * slope
                ).astype(jnp.bfloat16)
                grads_out[:, at_k] = grads
                for (row, end), send in zip(bounds, sends):
                    send[:, at_k] = grads[row:end]


def latent_kernel(size, *refs):
    flags, normed = refs[:2]
    down = refs[2 : 2 + 2 * size]
    latent = refs[3 + 2 * size]
    width = normed.shape[1] // size
    total = None
    for k in range(size):
        for half in range(2):
            block = normed[:, half_columns(flags[0], k, half, width)]
            part = dot_nt(block, down[2 * k + half][...])
            total = part if total is None else total + part
    latent[...] = total


def message_kernel(size, *refs):
    flags, normed = refs[:2]
    latent = refs[3 + 3 * size]
    shards = refs[3 : 3 + 3 * size]
    kept = refs[4 + 3 * size : 4 + 6 * size]
    messages = refs[4 + 6 * size :]
    shard = normed.shape[1] // size
    activated = jax.nn.silu(latent[...]).astype(jnp.bfloat16)
    for k in range(size):
        messages[k][:, :shard] = normed[:, columns(flags[0], k, shard)]
        messages[k][:, shard:] = activated
    for source, place in zip(shards, kept):
        place[...] = source[...]


def stage_kernel(stage, bounds, size, held, *refs):
    flags = refs[0]
    pieces = refs[1 : 1 + len(bounds)]
    at = 1 + len(bounds)
    if held == 7:
        shards = refs[at + 7 : at + 7 + 3 * size]
        state = refs[at + 7 + 3 * size : at + 14 + 3 * size]
        outs = refs[at + 14 + 3 * size :]
    else:
        state = refs[at + held : at + held + 7]
        shards = refs[at + held + 7 : at + 2 * held]
        outs = refs[at + 2 * held :]
    gain, inverse, latent, x, latent_grads, arrivals, grads = state
    down, up = shards[: 2 * size], shards[2 * size :]
    width = x.shape[1]
    shard = width // size
    latent_width = latent.shape[1]
    block = min(latent_width, shard)
    at_rows = slice(bounds[0][0], bounds[-1][1])

    def take(place):
        parts = [piece[:, place] for piece in pieces]
        return parts[0] if len(parts) == 1 else jnp.concatenate(parts, axis=0)

    @pl.when(flags[1] == stage)
    def _():
        hidden_grad = None
        for k in range(size):
            arriving = take(columns(flags[0], k, shard))
            for at in range(0, shard, block):
                lanes = at // block * latent_width
                part = dot_nn(arriving[:, at : at + block], up[k][:, lanes : lanes + latent_width])
                hidden_grad = part if hidden_grad is None else hidden_grad + part
        lat = latent[at_rows]
        latent_grad = (hidden_grad * silu_slope(lat)).astype(jnp.bfloat16)
        latent_grads[at_rows] = latent_grad
        scale = inverse[at_rows][:, :1]
        mean = jnp.sum(latent_grad.astype(jnp.float32) * lat, axis=-1, keepdims=True) / width
        slope = scale * scale * mean
        for k in range(size):
            for half in range(2):
                at_k = half_columns(flags[0], k, half, shard)
                arriving = take(at_k)
                arrivals[at_rows, at_k] = arriving
                scaled = dot_nn(latent_grad, down[2 * k + half][...])
                value = (
                    arriving.astype(jnp.float32)
                    + scale * (scaled * gain[:, at_k].astype(jnp.float32))
                    - x[at_rows, at_k].astype(jnp.float32) * slope
                ).astype(jnp.bfloat16)
                grads[at_rows, at_k] = value
                if stage:
                    outs[0][:, at_k] = value

    if stage == 0:
        for k in range(size):
            outs[k][:, :shard] = arrivals[:, columns(flags[0], k, shard)]
            outs[k][:, shard:] = latent_grads[...]


def touch_kernel(*refs):
    pass


def weight_kernel(size, *refs):
    early, late = refs[:size], refs[size : 2 * size]
    down_grads, up_grads, left, right = refs[2 * size :]
    tokens = early[0].shape[0]
    shard = down_grads.shape[0]
    for k in range(size):
        left[k * tokens : (k + 1) * tokens] = early[k][...]
        right[k * tokens : (k + 1) * tokens] = late[k][...]
    down_grads[...] = dot_tn(left[:, :shard], right[:, shard:]).astype(jnp.bfloat16)
    up_grads[...] = dot_tn(left[:, shard:], right[:, :shard]).astype(jnp.bfloat16)


def per_device(
    section_inputs, norm_gain, down_proj, up_proj, readout_matrix, ground_truth_series, valid_len
):
    size = lax.axis_size("dp")
    sections = lax.axis_size("section")
    top = sections - 1
    dp_index = lax.axis_index("dp")
    section = lax.axis_index("section")
    f32, bf16 = jnp.float32, jnp.bfloat16

    x = section_inputs[0]
    tokens, width = x.shape
    shard, latent_width = down_proj.shape[1:]
    horizon = readout_matrix.shape[1]
    share = tokens // sum(CHUNK_SHARES)
    ends = [share * sum(CHUNK_SHARES[: i + 1]) for i in range(len(CHUNK_SHARES))]
    bounds = list(zip([0] + ends, ends))

    flags = jnp.stack(
        [dp_index.astype(jnp.int32), section.astype(jnp.int32), (section == top).astype(jnp.int32)]
    )
    everyone, rest = list(range(sections)), list(range(top))
    low, high = pl.pallas_call(
        down_kernel,
        out_shape=(jax.ShapeDtypeStruct((latent_width, shard // 2), bf16),) * 2,
        in_specs=[ANY],
        out_specs=(VMEM,) * 2,
        scratch_shapes=[
            pltpu.VMEM((1, shard, latent_width), bf16),
            pltpu.SemaphoreType.DMA(()),
        ],
        compiler_params=PARAMS,
    )(stay(down_proj))
    down = gather_halves(low, high, everyone, size)
    up_block = min(latent_width, shard)
    up_own, head_own = pl.pallas_call(
        up_kernel,
        out_shape=(
            jax.ShapeDtypeStruct((up_block, latent_width * shard // up_block), bf16),
            jax.ShapeDtypeStruct((horizon + latent_width * horizon // shard, shard), bf16),
        ),
        in_specs=[ANY] * 2,
        out_specs=(VMEM,) * 2,
        scratch_shapes=[
            pltpu.VMEM((1, latent_width, shard), bf16),
            pltpu.VMEM((shard, horizon), bf16),
            pltpu.SemaphoreType.DMA((2,)),
        ],
        compiler_params=PARAMS,
    )(stay(up_proj), stay(readout_matrix))
    head = gather(head_own, [top], size)
    up_held, down_first = lax.optimization_barrier((up_own, down[2 % size][0]))
    down[2 % size] = (down_first, down[2 % size][1])
    up = gather(up_held, rest, size)
    down = [half for pair in down for half in pair]

    x, normed, inverse, gain = pl.pallas_call(
        norm_kernel,
        out_shape=(
            pltpu.VMEM((tokens, width), bf16),
            pltpu.VMEM((tokens, width), bf16),
            pltpu.VMEM((tokens, 128), f32),
            pltpu.VMEM((1, width), bf16),
        ),
        in_specs=[VMEM] * 2,
        out_specs=(VMEM,) * 4,
        compiler_params=PARAMS,
    )(x, norm_gain)
    per_micro = tokens // valid_len.shape[0]
    mask = (
        (jnp.arange(per_micro)[None, :] < valid_len[:, None]).astype(f32).reshape(tokens, 1)
    )
    mask = jnp.broadcast_to(mask, (tokens, 128))

    normed, latent = pl.pallas_call(
        functools.partial(latent_kernel, size),
        out_shape=(held_like(normed), pltpu.VMEM((tokens, latent_width), f32)),
        in_specs=[SMEM] + [VMEM] * (1 + 2 * size),
        out_specs=(VMEM,) * 2,
        input_output_aliases={1: 0},
        compiler_params=PARAMS,
    )(flags, pin(normed), *[pin(half) for half in down])

    gain, x, inverse, latent, latent_grads, arrivals, grads, *sends = pl.pallas_call(
        functools.partial(top_kernel, size, bounds),
        out_shape=(
            held_like(gain),
            held_like(x),
            held_like(inverse),
            held_like(latent),
            pltpu.VMEM((tokens, latent_width), bf16),
            pltpu.VMEM((tokens, width), bf16),
            pltpu.VMEM((tokens, width), bf16),
        )
        + tuple(jax.ShapeDtypeStruct((end - row, width), bf16) for row, end in bounds),
        in_specs=[SMEM] + [VMEM] * (6 + 3 * size),
        out_specs=(VMEM,) * (7 + len(bounds)),
        input_output_aliases={3: 0, 4: 1, 5: 2, 6: 3},
        compiler_params=PARAMS,
    )(
        flags, ground_truth_series, mask, pin(gain), pin(x), pin(inverse), pin(latent),
        *[pin(part) for part in down + head],
    )

    def hop(block, sender):
        return move(block, [(sender * size + i, (sender - 1) * size + i) for i in range(size)])

    received = [hop(send, top) for send in sends]

    message = jax.ShapeDtypeStruct((tokens, shard + latent_width), bf16)
    shards = (*down, *up)
    state = (gain, inverse, latent, x, latent_grads, arrivals, grads)

    def run_stage(stage, bounds, received, state, shards):
        rows = bounds[-1][1] - bounds[0][0]
        if stage:
            outs = (jax.ShapeDtypeStruct((rows, width), bf16),)
        else:
            outs = (message,) * size
        first = 1 + len(received)
        results = pl.pallas_call(
            functools.partial(stage_kernel, stage, bounds, size, len(state)),
            out_shape=tuple(held_like(part) for part in state) + outs,
            in_specs=[SMEM] + [VMEM] * (len(received) + len(state) + len(shards)),
            out_specs=(VMEM,) * (len(state) + len(outs)),
            input_output_aliases={first + i: i for i in range(len(state))},
            cost_estimate=pl.CostEstimate(
                flops=4 * rows * width * latent_width,
                bytes_accessed=8 * width * latent_width,
                transcendentals=rows * latent_width,
            ),
            compiler_params=PARAMS,
        )(flags, *received, *[pin(part) for part in state + shards])
        return tuple(results[: len(state)]), results[len(state) :]

    def send_messages(messages):
        return [messages[0]] + [
            move(messages[k], peers(range(sections), size, k)) for k in range(1, size)
        ]

    for stage in range(top - 1, 0, -1):
        sent = []
        for bound, block in zip(bounds, received):
            state, outs = run_stage(stage, [bound], [block], state, shards)
            sent.append(hop(outs[0], stage))
        received = sent
        if stage == top - 1:
            results = pl.pallas_call(
                functools.partial(message_kernel, size),
                out_shape=(held_like(state[2]),)
                + tuple(held_like(part) for part in shards)
                + (message,) * size,
                in_specs=[SMEM] + [VMEM] * (2 + len(shards)),
                out_specs=(VMEM,) * (1 + len(shards) + size),
                input_output_aliases={2: 0},
                compiler_params=PARAMS,
            )(flags, pin(normed), pin(state[2]), *[pin(part) for part in shards])
            state = state[:2] + (results[0],) + state[3:] + tuple(results[1 : 1 + len(shards)])
            shards = ()
            early = send_messages(results[-size:])
        if stage == max(top - 3, 1):
            latent, *early = pl.pallas_call(
                touch_kernel,
                out_shape=(held_like(state[2]),) + tuple(held_like(part) for part in early),
                in_specs=[VMEM] * (1 + size),
                out_specs=(VMEM,) * (1 + size),
                input_output_aliases={i: i for i in range(1 + size)},
                compiler_params=PARAMS,
            )(pin(state[2]), *[pin(part) for part in early])
            state = state[:2] + (latent,) + state[3:]

    state, outs = run_stage(0, bounds, received, state, shards)
    late = send_messages(outs)
    down_grads, up_grads = pl.pallas_call(
        functools.partial(weight_kernel, size),
        out_shape=(
            jax.ShapeDtypeStruct((shard, latent_width), bf16),
            jax.ShapeDtypeStruct((latent_width, shard), bf16),
        ),
        in_specs=[VMEM] * (2 * size),
        out_specs=(VMEM,) * 2,
        scratch_shapes=[pltpu.VMEM((size * tokens, shard + latent_width), bf16)] * 2,
        compiler_params=PARAMS,
    )(*early, *late)
    return (state[6][None], down_grads[None], up_grads[None])


def solution(mesh):
    placed = (
        P("section", "dp", None),
        P("section", None),
        P("section", "dp", None),
        P("section", None, "dp"),
        P("dp", None),
        P("dp", None),
        P("dp"),
    )
    return jax.shard_map(
        per_device,
        mesh=mesh,
        in_specs=placed,
        out_specs=(P("section", "dp", None), P("section", "dp", None), P("section", None, "dp")),
        check_vma=False,
    )
```

```python
import functools

import jax
import jax.numpy as jnp
from jax import lax
from jax.experimental import pallas as pl
from jax.experimental.pallas import tpu as pltpu
from jax.sharding import PartitionSpec as P

EPSILON = 1e-05
CHUNK_SHARES = (4, 4)
GAIN_ROWS = 16
ANY = pl.BlockSpec(memory_space=pl.ANY)
VMEM = pl.BlockSpec(memory_space=pltpu.VMEM)
SMEM = pl.BlockSpec(memory_space=pltpu.SMEM)
NOTHING = pl.CostEstimate(flops=0, bytes_accessed=0, transcendentals=0)
PARAMS = pltpu.CompilerParams(vmem_limit_bytes=20 * 1024 * 1024)


def dot_nn(left, right):
    return lax.dot_general(
        left, right, (((1,), (0,)), ((), ())), preferred_element_type=jnp.float32
    )


def dot_nt(left, right):
    return lax.dot_general(
        left, right, (((1,), (1,)), ((), ())), preferred_element_type=jnp.float32
    )


def dot_tn(left, right):
    return lax.dot_general(
        left, right, (((0,), (0,)), ((), ())), preferred_element_type=jnp.float32
    )


def silu_slope(latent):
    sigmoid = jax.nn.sigmoid(latent)
    return sigmoid * (1.0 + latent * (1.0 - sigmoid))


def move(block, pairs):
    return lax.ppermute(block, ("section", "dp"), pairs)


def peers(sections, size, k):
    return [(s * size + i, s * size + (i ^ k)) for s in sections for i in range(size)]


def gather(block, sections, size):
    return [block] + [move(block, peers(sections, size, k)) for k in range(1, size)]


def gather_halves(low, high, sections, size):
    if size != 4:
        return list(zip(gather(low, sections, size), gather(high, sections, size)))
    across, along = peers(sections, size, 1), peers(sections, size, 2)
    low_along = move(low, along)
    high_across = move(high, across)
    high_along = move(high, along)
    low_across = move(low, across)
    low_far = move(low_along, across)
    high_far = move(high_across, along)
    return [(low, high), (low_across, high_across), (low_along, high_along), (low_far, high_far)]


def pin(block):
    return pltpu.with_memory_space_constraint(block, pltpu.VMEM)


def stay(block):
    return pltpu.with_memory_space_constraint(block, pltpu.HBM)


def held_like(block):
    return pltpu.VMEM(block.shape, block.dtype)


def columns(dp_index, k, width):
    return pl.ds(pl.multiple_of((dp_index ^ k) * width, width), width)


def half_columns(dp_index, k, half, width):
    start = (dp_index ^ k) * width + half * (width // 2)
    return pl.ds(pl.multiple_of(start, width // 2), width // 2)


def prepare_kernel(flags, down, up, readout, *refs):
    low, high, *rest, down_held, up_held, readout_held, sems = refs
    copies = [
        pltpu.make_async_copy(down, down_held, sems.at[0]),
        pltpu.make_async_copy(up, up_held, sems.at[1]),
        pltpu.make_async_copy(readout, readout_held, sems.at[2]),
    ]
    for copy in copies:
        copy.start()
    latent_width, shard = up_held.shape[1:]
    horizon = readout_held.shape[1]
    half = shard // 2
    head_rows = low.shape[0] - latent_width
    copies[0].wait()
    turned = down_held[0].T
    low[:latent_width] = turned[:, :half]
    high[:latent_width] = turned[:, half:]
    copies[1].wait()
    copies[2].wait()
    values = up_held[0]

    @pl.when(flags[2] == 1)
    def _():
        product = dot_nn(values, readout_held[...]).astype(jnp.bfloat16)
        turned_readout = readout_held[...].T
        rows = latent_width * horizon // shard
        for out, start in ((low, 0), (high, half)):
            out[latent_width : latent_width + horizon] = turned_readout[:, start : start + half]
            for at in range(0, half, horizon):
                row = (start + at) // horizon * rows
                out[latent_width + horizon :, at : at + horizon] = product[row : row + rows]

    @pl.when(flags[2] == 0)
    def _():
        block = min(latent_width, shard)
        blocks = [values[:, at : at + block].T for at in range(0, shard, block)]
        whole = blocks[0] if len(blocks) == 1 else jnp.concatenate(blocks, axis=1)
        low[latent_width:] = whole[:head_rows, :half]
        high[latent_width:] = whole[:head_rows, half:]
        if rest:
            rest[0][...] = whole[head_rows:]


def norm_kernel(x, gain, x_out, normed_out, inverse_out, gain_out):
    values = x[...].astype(jnp.float32)
    inverse = lax.rsqrt(jnp.mean(values * values, axis=-1, keepdims=True) + EPSILON)
    x_out[...] = x[...]
    normed_out[...] = (values * inverse * gain[...].astype(jnp.float32)).astype(jnp.bfloat16)
    inverse_out[...] = jnp.broadcast_to(inverse, inverse_out.shape)
    gain_out[...] = gain[...]


def top_kernel(size, bounds, *refs):
    flags, truth, mask = refs[:3]
    halves = refs[7 : 7 + 2 * size]
    gain, x, inverse, latent_ref, latent_grad_out, arriving_out, grads_out = refs[
        7 + 2 * size : 14 + 2 * size
    ]
    sends = refs[14 + 2 * size :]
    dp_index = flags[0]
    width = x.shape[1] // size
    latent_width = latent_ref.shape[1]
    horizon = truth.shape[1]
    head = slice(latent_width, latent_width + horizon)

    @pl.when(flags[2] == 1)
    def _():
        latent = latent_ref[...]
        activated = jax.nn.silu(latent).astype(jnp.bfloat16)
        estimate = None
        product = None
        for k in range(size):
            extra = []
            for half in range(2):
                ref = halves[2 * k + half]
                part = dot_nt(x[:, half_columns(dp_index, k, half, width)], ref[head])
                estimate = part if estimate is None else estimate + part
                extra += [
                    ref[latent_width + horizon :, at : at + horizon]
                    for at in range(0, width // 2, horizon)
                ]
            extra = jnp.concatenate(extra, axis=0).astype(jnp.float32)
            product = extra if product is None else product + extra
        product = product.astype(jnp.bfloat16)
        estimate = estimate + dot_nn(activated, product)
        error = (mask[:, :1] * (estimate - truth[...])).astype(jnp.bfloat16)
        hidden_grad = dot_nt(error, product)
        latent_grad = (hidden_grad * silu_slope(latent)).astype(jnp.bfloat16)
        latent_grad_out[...] = latent_grad
        scale = inverse[:, :1]
        mean = jnp.sum(latent_grad.astype(jnp.float32) * latent, axis=-1, keepdims=True) / (
            width * size
        )
        slope = scale * scale * mean
        for k in range(size):
            for half in range(2):
                at_k = half_columns(dp_index, k, half, width)
                ref = halves[2 * k + half]
                arriving = dot_nn(error, ref[head]).astype(jnp.bfloat16)
                arriving_out[:, at_k] = arriving
                scaled = dot_nn(latent_grad, ref[:latent_width])
                grads = (
                    arriving.astype(jnp.float32)
                    + scale * (scaled * gain[:, at_k].astype(jnp.float32))
                    - x[:, at_k].astype(jnp.float32) * slope
                ).astype(jnp.bfloat16)
                grads_out[:, at_k] = grads
                for (row, end), send in zip(bounds, sends):
                    send[:, at_k] = grads[row:end]


def latent_kernel(size, *refs):
    flags, normed = refs[:2]
    down = refs[2 : 2 + 2 * size]
    latent = refs[3 + 2 * size]
    width = normed.shape[1] // size
    total = None
    for k in range(size):
        for half in range(2):
            block = normed[:, half_columns(flags[0], k, half, width)]
            part = dot_nt(block, down[2 * k + half][: latent.shape[1]])
            total = part if total is None else total + part
    latent[...] = total


def shard_of(raw, size, latent_width, rows):
    def down(k, half):
        return raw[2 * k + half][:latent_width]

    def up(k, lanes):
        half = raw[0].shape[1]
        parts = []
        for which in range(2):
            start, end = max(lanes.start - which * half, 0), min(lanes.stop - which * half, half)
            if start < end:
                parts.append(raw[2 * k + which][latent_width:, start:end])
        first = parts[0] if len(parts) == 1 else jnp.concatenate(parts, axis=1)
        if len(raw) == 2 * size:
            return first
        return jnp.concatenate([first, raw[2 * size + k][:, lanes]], axis=0)

    return down, up


def keep_kernel(size, count, *refs):
    flags = refs[0]
    gain, inverse, latent, x = refs[1:5]
    raw = refs[8 : 8 + count]
    kept = refs[15 + count : 15 + count + 2 * size]
    (bundle,) = refs[15 + count + 2 * size :]
    tokens, width = x.shape
    latent_width = latent.shape[1]
    shard = width // size
    block, lanes = kept[-1].shape
    down, up = shard_of(raw, size, latent_width, block)

    @pl.when(flags[3] == 1)
    def _():
        for k in range(size):
            for half in range(2):
                here = slice(half * (shard // 2), (half + 1) * (shard // 2))
                kept[k][:, here] = down(k, half)
            step = lanes // 2
            for at in range(0, lanes, step):
                kept[size + k][:, at : at + step] = up(k, slice(at, at + step))

    @pl.when((flags[1] % 2 == 0) & (flags[3] == 1))
    def _():
        for k in range(size):
            bundle[k * latent_width : (k + 1) * latent_width] = kept[k][...]
            row = size * latent_width + k * block
            bundle[row : row + block] = kept[size + k][...]
        at = size * (latent_width + block)
        for k in range(size):
            here = slice(k * shard, (k + 1) * shard)
            bundle[at + k * tokens : at + (k + 1) * tokens] = x[:, here]
            row = at + size * tokens + k * GAIN_ROWS
            bundle[row : row + GAIN_ROWS] = jnp.broadcast_to(gain[:, here], (GAIN_ROWS, shard))
        at += size * (tokens + GAIN_ROWS)
        for values in (latent[...], inverse[...]):
            high = values.astype(jnp.bfloat16)
            low = (values - high.astype(jnp.float32)).astype(jnp.bfloat16)
            for part in (high, low):
                bundle[at : at + tokens, : part.shape[1]] = part
                at += tokens


def message_kernel(size, *refs):
    flags, normed = refs[:2]
    latent = refs[3]
    messages = refs[4:]
    shard = normed.shape[1] // size
    activated = jax.nn.silu(latent[...]).astype(jnp.bfloat16)
    for k in range(size):
        messages[k][:, :shard] = normed[:, columns(flags[0], k, shard)]
        messages[k][:, shard:] = activated


def step_back(dp_index, size, width, take, down, up, lat, scale, gain, x, write):
    latent_width = lat.shape[1]
    shard = width // size
    block = min(latent_width, shard)
    hidden_grad = None
    for k in range(size):
        arriving = take(columns(dp_index, k, shard))
        for at in range(0, shard, block):
            lanes = at // block * latent_width
            part = dot_nn(arriving[:, at : at + block], up(k, slice(lanes, lanes + latent_width)))
            hidden_grad = part if hidden_grad is None else hidden_grad + part
    latent_grad = (hidden_grad * silu_slope(lat)).astype(jnp.bfloat16)
    mean = jnp.sum(latent_grad.astype(jnp.float32) * lat, axis=-1, keepdims=True) / width
    slope = scale * scale * mean
    for k in range(size):
        for half in range(2):
            place = half_columns(dp_index, k, half, shard)
            arriving = take(place)
            scaled = dot_nn(latent_grad, down(k, half))
            value = (
                arriving.astype(jnp.float32)
                + scale * (scaled * gain(k, half).astype(jnp.float32))
                - x(k, half).astype(jnp.float32) * slope
            ).astype(jnp.bfloat16)
            write(place, arriving, value)
    return latent_grad


def kept_of(kept, size, shard):
    def down(k, half):
        return kept[k][:, half * (shard // 2) : (half + 1) * (shard // 2)]

    return down, lambda k, lanes: kept[size + k][:, lanes]


def stage_kernel(stage, bounds, size, held, count, *refs):
    flags = refs[0]
    pieces = refs[1 : 1 + len(bounds)]
    at = 1 + len(bounds)
    raw = refs[at + held : at + held + count]
    state = refs[at + held + count : at + 2 * held + count]
    outs = refs[at + 2 * held + count :]
    shard = state[3].shape[1] // size
    if raw:
        down, up = shard_of(raw, size, state[2].shape[1], None)
    else:
        down, up = kept_of(state[7:], size, shard)
    state = state[:7]
    gain, inverse, latent, x, latent_grads, arrivals, grads = state
    at_rows = slice(bounds[0][0], bounds[-1][1])

    def take(place):
        parts = [piece[:, place] for piece in pieces]
        return parts[0] if len(parts) == 1 else jnp.concatenate(parts, axis=0)

    def write(place, arriving, value):
        arrivals[at_rows, place] = arriving
        grads[at_rows, place] = value
        if stage and outs:
            outs[0][:, place] = value

    @pl.when(flags[1] == stage)
    def _():
        latent_grads[at_rows] = step_back(
            flags[0],
            size,
            x.shape[1],
            take,
            down,
            up,
            latent[at_rows],
            inverse[at_rows][:, :1],
            lambda k, half: gain[:, half_columns(flags[0], k, half, shard)],
            lambda k, half: x[at_rows, half_columns(flags[0], k, half, shard)],
            write,
        )

    if stage == 0:
        for k in range(size):
            outs[k][:, :shard] = arrivals[:, columns(flags[0], k, shard)]
            outs[k][:, shard:] = latent_grads[...]


def pair_kernel(stage, bound, size, held, *refs):
    flags, received = refs[:2]
    state = refs[2 + held : 9 + held]
    kept = refs[9 + held : 9 + held + 2 * size]
    bundle = refs[1 + 2 * held]
    middle, last = refs[2 + 2 * held :]
    gain, inverse, latent, x, latent_grads, arrivals, grads = state
    tokens = x.shape[0]
    latent_width = latent.shape[1]
    shard = x.shape[1] // size
    down, up = kept_of(kept, size, shard)
    block = kept[-1].shape[0]
    at_rows = slice(*bound)

    def write(place, arriving, value):
        arrivals[at_rows, place] = arriving
        grads[at_rows, place] = value
        middle[:, place] = value

    def write_last(place, arriving, value):
        last[:, place] = value

    def next_down(k, half):
        here = slice(half * (shard // 2), (half + 1) * (shard // 2))
        return bundle[k * latent_width : (k + 1) * latent_width, here]

    def both(index, lanes):
        row = size * (latent_width + block + tokens + GAIN_ROWS) + index * tokens + bound[0]
        end = row + bound[1] - bound[0]
        high = bundle[row:end, :lanes].astype(jnp.float32)
        return high + bundle[row + tokens : end + tokens, :lanes].astype(jnp.float32)

    def next_x(k, half):
        here = slice(half * (shard // 2), (half + 1) * (shard // 2))
        start = size * (latent_width + block) + (flags[0] ^ k) * tokens + bound[0]
        return bundle[pl.ds(pl.multiple_of(start, 16), bound[1] - bound[0]), here]

    def next_gain(k, half):
        here = slice(half * (shard // 2), (half + 1) * (shard // 2))
        start = size * (latent_width + block + tokens) + (flags[0] ^ k) * GAIN_ROWS
        return bundle[pl.ds(pl.multiple_of(start, 16), GAIN_ROWS), here][:1]

    def next_up(k, lanes):
        row = size * latent_width + k * block
        return bundle[row : row + block, lanes]

    @pl.when(flags[1] == stage)
    def _():
        latent_grads[at_rows] = step_back(
            flags[0],
            size,
            x.shape[1],
            lambda place: received[:, place],
            down,
            up,
            latent[at_rows],
            inverse[at_rows][:, :1],
            lambda k, half: gain[:, half_columns(flags[0], k, half, shard)],
            lambda k, half: x[at_rows, half_columns(flags[0], k, half, shard)],
            write,
        )
        step_back(
            flags[0],
            size,
            x.shape[1],
            lambda place: middle[:, place],
            next_down,
            next_up,
            both(0, latent_width),
            both(2, 128)[:, :1],
            next_gain,
            next_x,
            write_last,
        )


def touch_kernel(*refs):
    pass


def weight_kernel(size, *refs):
    early, late = refs[:size], refs[size : 2 * size]
    down_grads, up_grads, left, right = refs[2 * size :]
    tokens = early[0].shape[0]
    shard = down_grads.shape[0]
    for k in range(size):
        left[k * tokens : (k + 1) * tokens] = early[k][...]
        right[k * tokens : (k + 1) * tokens] = late[k][...]
    down_grads[...] = dot_tn(left[:, :shard], right[:, shard:]).astype(jnp.bfloat16)
    up_grads[...] = dot_tn(left[:, shard:], right[:, :shard]).astype(jnp.bfloat16)


def per_device(
    section_inputs, norm_gain, down_proj, up_proj, readout_matrix, ground_truth_series, valid_len
):
    size = lax.axis_size("dp")
    sections = lax.axis_size("section")
    top = sections - 1
    dp_index = lax.axis_index("dp")
    section = lax.axis_index("section")
    f32, bf16 = jnp.float32, jnp.bfloat16

    x = section_inputs[0]
    tokens, width = x.shape
    shard, latent_width = down_proj.shape[1:]
    horizon = readout_matrix.shape[1]
    share = tokens // sum(CHUNK_SHARES)
    ends = [share * sum(CHUNK_SHARES[: i + 1]) for i in range(len(CHUNK_SHARES))]
    bounds = list(zip([0] + ends, ends))

    flags = jnp.stack(
        [
            dp_index.astype(jnp.int32),
            section.astype(jnp.int32),
            (section == top).astype(jnp.int32),
            (section < top - 1).astype(jnp.int32),
        ]
    )
    everyone, rest = list(range(sections)), list(range(top))
    up_block = min(latent_width, shard)
    up_lanes = latent_width * shard // up_block
    head_rows = horizon + latent_width * horizon // shard
    more = max(up_block - head_rows, 0)
    low, high, *up_rest = pl.pallas_call(
        prepare_kernel,
        out_shape=(jax.ShapeDtypeStruct((latent_width + head_rows, shard // 2), bf16),) * 2
        + (jax.ShapeDtypeStruct((more, up_lanes), bf16),) * (more > 0),
        in_specs=[SMEM] + [ANY] * 3,
        out_specs=(VMEM,) * (2 + (more > 0)),
        scratch_shapes=[
            pltpu.VMEM((1, shard, latent_width), bf16),
            pltpu.VMEM((1, latent_width, shard), bf16),
            pltpu.VMEM((shard, horizon), bf16),
            pltpu.SemaphoreType.DMA((3,)),
        ],
        cost_estimate=NOTHING,
        compiler_params=PARAMS,
    )(flags, stay(down_proj), stay(up_proj), stay(readout_matrix))
    halves = gather_halves(low, high, everyone, size)
    if more:
        up_rest, first = lax.optimization_barrier((up_rest[0], halves[2 % size][0]))
        halves[2 % size] = (first, halves[2 % size][1])
        up_rest = gather(up_rest, rest, size)
    halves = [half for pair in halves for half in pair]

    x, normed, inverse, gain = pl.pallas_call(
        norm_kernel,
        out_shape=(
            pltpu.VMEM((tokens, width), bf16),
            pltpu.VMEM((tokens, width), bf16),
            pltpu.VMEM((tokens, 128), f32),
            pltpu.VMEM((1, width), bf16),
        ),
        in_specs=[VMEM] * 2,
        out_specs=(VMEM,) * 4,
        cost_estimate=NOTHING,
        compiler_params=PARAMS,
    )(x, norm_gain)
    per_micro = tokens // valid_len.shape[0]
    mask = (
        (jnp.arange(per_micro)[None, :] < valid_len[:, None]).astype(f32).reshape(tokens, 1)
    )
    mask = jnp.broadcast_to(mask, (tokens, 128))

    normed, latent = pl.pallas_call(
        functools.partial(latent_kernel, size),
        out_shape=(held_like(normed), pltpu.VMEM((tokens, latent_width), f32)),
        in_specs=[SMEM] + [VMEM] * (1 + 2 * size),
        out_specs=(VMEM,) * 2,
        input_output_aliases={1: 0},
        cost_estimate=NOTHING,
        compiler_params=PARAMS,
    )(flags, pin(normed), *[pin(half) for half in halves])

    gain, x, inverse, latent, latent_grads, arrivals, grads, *sends = pl.pallas_call(
        functools.partial(top_kernel, size, bounds),
        out_shape=(
            held_like(gain),
            held_like(x),
            held_like(inverse),
            held_like(latent),
            pltpu.VMEM((tokens, latent_width), bf16),
            pltpu.VMEM((tokens, width), bf16),
            pltpu.VMEM((tokens, width), bf16),
        )
        + tuple(jax.ShapeDtypeStruct((end - row, width), bf16) for row, end in bounds),
        in_specs=[SMEM] + [VMEM] * (6 + 2 * size),
        out_specs=(VMEM,) * (7 + len(bounds)),
        input_output_aliases={3: 0, 4: 1, 5: 2, 6: 3},
        cost_estimate=NOTHING,
        compiler_params=PARAMS,
    )(
        flags, ground_truth_series, mask, pin(gain), pin(x), pin(inverse), pin(latent),
        *[pin(part) for part in halves],
    )

    def hop(block, sender, distance=1):
        return move(
            block, [(sender * size + i, (sender - distance) * size + i) for i in range(size)]
        )

    received = [hop(send, top) for send in sends]

    message = jax.ShapeDtypeStruct((tokens, shard + latent_width), bf16)
    shards = (*halves, *up_rest)
    state = (gain, inverse, latent, x, latent_grads, arrivals, grads)

    def run_stage(stage, bounds, received, state, shards, sends=True):
        rows = bounds[-1][1] - bounds[0][0]
        if not stage:
            outs = (message,) * size
        else:
            outs = (jax.ShapeDtypeStruct((rows, width), bf16),) * sends
        first = 1 + len(received)
        results = pl.pallas_call(
            functools.partial(stage_kernel, stage, bounds, size, len(state), len(shards)),
            out_shape=tuple(held_like(part) for part in state) + outs,
            in_specs=[SMEM] + [VMEM] * (len(received) + len(state) + len(shards)),
            out_specs=(VMEM,) * (len(state) + len(outs)),
            input_output_aliases={first + i: i for i in range(len(state))},
            cost_estimate=NOTHING,
            compiler_params=PARAMS,
        )(flags, *received, *[pin(part) for part in state + shards])
        return tuple(results[: len(state)]), results[len(state) :]

    def run_pair(stage, bound, received, state):
        rows = bound[1] - bound[0]
        results = pl.pallas_call(
            functools.partial(pair_kernel, stage, bound, size, len(state)),
            out_shape=tuple(held_like(part) for part in state)
            + (jax.ShapeDtypeStruct((rows, width), bf16),) * 2,
            in_specs=[SMEM] + [VMEM] * (1 + len(state)),
            out_specs=(VMEM,) * (len(state) + 2),
            input_output_aliases={2 + i: i for i in range(len(state))},
            cost_estimate=NOTHING,
            compiler_params=PARAMS,
        )(flags, received, *[pin(part) for part in state])
        return tuple(results[: len(state)]), results[len(state) :]

    def send_messages(messages):
        return [messages[0]] + [
            move(messages[k], peers(range(sections), size, k)) for k in range(1, size)
        ]

    state_kept = pl.pallas_call(
        functools.partial(keep_kernel, size, len(shards)),
        out_shape=tuple(held_like(part) for part in state)
        + (pltpu.VMEM((latent_width, shard), bf16),) * size
        + (pltpu.VMEM((up_block, up_lanes), bf16),) * size
        + (
            jax.ShapeDtypeStruct(
                (size * (latent_width + up_block + tokens + GAIN_ROWS) + 4 * tokens, shard), bf16
            ),
        ),
        in_specs=[SMEM] + [VMEM] * (len(state) + len(shards)),
        out_specs=(VMEM,) * (len(state) + 2 * size + 1),
        input_output_aliases={1 + i: i for i in range(len(state))},
        cost_estimate=NOTHING,
        compiler_params=PARAMS,
    )(flags, *[pin(part) for part in state + shards])
    state, kept, bundle = tuple(state_kept[:7]), tuple(state_kept[7:-1]), state_kept[-1:]
    pairs = list(range(3, top - 1, 2))
    bundle = tuple(
        move(part, [((s - 1) * size + i, s * size + i) for s in pairs for i in range(size)])
        for part in bundle
    )

    sent = []
    for bound, block in zip(bounds, received):
        state, outs = run_stage(top - 1, [bound], [block], state, shards)
        sent.append(hop(outs[0], top - 1))
    received = sent

    state = state + kept + bundle

    waiting = []
    for stage in reversed(pairs):
        sent, side = [], []
        for bound, block in zip(bounds, received):
            state, outs = run_pair(stage, bound, block, state)
            sent.append(hop(outs[1], stage, 2))
            side.append(hop(outs[0], stage))
        received = sent
        for asides, bound, block in waiting:
            base, _ = run_stage(asides, [bound], [block], state[:-1], (), False)
            state = base + state[-1:]
        waiting = [(stage - 1, bound, block) for bound, block in zip(bounds, side)]
    latent, *messages = pl.pallas_call(
        functools.partial(message_kernel, size),
        out_shape=(held_like(state[2]),) + (message,) * size,
        in_specs=[SMEM] + [VMEM] * 2,
        out_specs=(VMEM,) * (1 + size),
        input_output_aliases={2: 0},
        cost_estimate=NOTHING,
        compiler_params=PARAMS,
    )(flags, pin(normed), pin(state[2]))
    early = send_messages(messages)
    latent, *early = pl.pallas_call(
        touch_kernel,
        out_shape=(held_like(latent),) + tuple(held_like(part) for part in early),
        in_specs=[VMEM] * (1 + size),
        out_specs=(VMEM,) * (1 + size),
        input_output_aliases={i: i for i in range(1 + size)},
        cost_estimate=NOTHING,
        compiler_params=PARAMS,
    )(pin(latent), *[pin(part) for part in early])
    state = state[:2] + (latent,) + state[3:]
    state = state[:-1]

    sent = []
    for bound, block in zip(bounds, received):
        state, outs = run_stage(1, [bound], [block], state, ())
        sent.append(hop(outs[0], 1))
    received = sent
    for asides, bound, block in waiting:
        state, _ = run_stage(asides, [bound], [block], state, (), False)
    shards = ()
    state, outs = run_stage(0, bounds, received, state, shards)
    late = send_messages(outs)
    down_grads, up_grads = pl.pallas_call(
        functools.partial(weight_kernel, size),
        out_shape=(
            jax.ShapeDtypeStruct((shard, latent_width), bf16),
            jax.ShapeDtypeStruct((latent_width, shard), bf16),
        ),
        in_specs=[VMEM] * (2 * size),
        out_specs=(VMEM,) * 2,
        scratch_shapes=[pltpu.VMEM((size * tokens, shard + latent_width), bf16)] * 2,
        cost_estimate=NOTHING,
        compiler_params=PARAMS,
    )(*early, *late)
    return (state[6][None], down_grads[None], up_grads[None])


def solution(mesh):
    placed = (
        P("section", "dp", None),
        P("section", None),
        P("section", "dp", None),
        P("section", None, "dp"),
        P("dp", None),
        P("dp", None),
        P("dp"),
    )
    return jax.shard_map(
        per_device,
        mesh=mesh,
        in_specs=placed,
        out_specs=(P("section", "dp", None), P("section", "dp", None), P("section", None, "dp")),
        check_vma=False,
    )
```

```python
import functools

import jax
import jax.numpy as jnp
from jax import lax
from jax.experimental import pallas as pl
from jax.experimental.pallas import tpu as pltpu
from jax.sharding import PartitionSpec as P

EPSILON = 1e-05
CHUNK_SHARES = (4, 4)
GAIN_ROWS = 16
ANY = pl.BlockSpec(memory_space=pl.ANY)
VMEM = pl.BlockSpec(memory_space=pltpu.VMEM)
SMEM = pl.BlockSpec(memory_space=pltpu.SMEM)
NOTHING = pl.CostEstimate(flops=0, bytes_accessed=0, transcendentals=0)
PARAMS = pltpu.CompilerParams(vmem_limit_bytes=20 * 1024 * 1024)


def dot_nn(left, right):
    return lax.dot_general(
        left, right, (((1,), (0,)), ((), ())), preferred_element_type=jnp.float32
    )


def dot_nt(left, right):
    return lax.dot_general(
        left, right, (((1,), (1,)), ((), ())), preferred_element_type=jnp.float32
    )


def dot_tn(left, right):
    return lax.dot_general(
        left, right, (((0,), (0,)), ((), ())), preferred_element_type=jnp.float32
    )


def silu_slope(latent):
    sigmoid = jax.nn.sigmoid(latent)
    return sigmoid * (1.0 + latent * (1.0 - sigmoid))


def move(block, pairs):
    return lax.ppermute(block, ("section", "dp"), pairs)


def peers(sections, size, k):
    return [(s * size + i, s * size + (i ^ k)) for s in sections for i in range(size)]


def gather(block, sections, size):
    return [block] + [move(block, peers(sections, size, k)) for k in range(1, size)]


def gather_halves(low, high, sections, size):
    if size != 4:
        return list(zip(gather(low, sections, size), gather(high, sections, size)))
    across, along = peers(sections, size, 1), peers(sections, size, 2)
    low_along = move(low, along)
    high_across = move(high, across)
    high_along = move(high, along)
    low_across = move(low, across)
    low_far = move(low_along, across)
    high_far = move(high_across, along)
    return [(low, high), (low_across, high_across), (low_along, high_along), (low_far, high_far)]


def pin(block):
    return pltpu.with_memory_space_constraint(block, pltpu.VMEM)


def stay(block):
    return pltpu.with_memory_space_constraint(block, pltpu.HBM)


def held_like(block):
    return pltpu.VMEM(block.shape, block.dtype)


def columns(dp_index, k, width):
    return pl.ds(pl.multiple_of((dp_index ^ k) * width, width), width)


def half_columns(dp_index, k, half, width):
    start = (dp_index ^ k) * width + half * (width // 2)
    return pl.ds(pl.multiple_of(start, width // 2), width // 2)


def prepare_kernel(flags, down, up, readout, *refs):
    low, high, *rest, down_held, up_held, readout_held, sems = refs
    copies = [
        pltpu.make_async_copy(down, down_held, sems.at[0]),
        pltpu.make_async_copy(up, up_held, sems.at[1]),
        pltpu.make_async_copy(readout, readout_held, sems.at[2]),
    ]
    for copy in copies:
        copy.start()
    latent_width, shard = up_held.shape[1:]
    horizon = readout_held.shape[1]
    half = shard // 2
    head_rows = low.shape[0] - latent_width
    copies[0].wait()
    turned = down_held[0].T
    low[:latent_width] = turned[:, :half]
    high[:latent_width] = turned[:, half:]
    copies[1].wait()
    copies[2].wait()
    values = up_held[0]

    @pl.when(flags[2] == 1)
    def _():
        product = dot_nn(values, readout_held[...]).astype(jnp.bfloat16)
        turned_readout = readout_held[...].T
        rows = latent_width * horizon // shard
        for out, start in ((low, 0), (high, half)):
            out[latent_width : latent_width + horizon] = turned_readout[:, start : start + half]
            for at in range(0, half, horizon):
                row = (start + at) // horizon * rows
                out[latent_width + horizon :, at : at + horizon] = product[row : row + rows]

    @pl.when(flags[2] == 0)
    def _():
        block = min(latent_width, shard)
        blocks = [values[:, at : at + block].T for at in range(0, shard, block)]
        whole = blocks[0] if len(blocks) == 1 else jnp.concatenate(blocks, axis=1)
        low[latent_width:] = whole[:head_rows, :half]
        high[latent_width:] = whole[:head_rows, half:]
        if rest:
            rest[0][...] = whole[head_rows:]


def norm_kernel(x, gain, x_out, normed_out, inverse_out, gain_out):
    values = x[...].astype(jnp.float32)
    inverse = lax.rsqrt(jnp.mean(values * values, axis=-1, keepdims=True) + EPSILON)
    x_out[...] = x[...]
    normed_out[...] = (values * inverse * gain[...].astype(jnp.float32)).astype(jnp.bfloat16)
    inverse_out[...] = jnp.broadcast_to(inverse, inverse_out.shape)
    gain_out[...] = gain[...]


def top_kernel(size, bounds, *refs):
    flags, truth, mask = refs[:3]
    halves = refs[7 : 7 + 2 * size]
    gain, x, inverse, latent_ref, latent_grad_out, arriving_out, grads_out = refs[
        7 + 2 * size : 14 + 2 * size
    ]
    sends = refs[14 + 2 * size :]
    dp_index = flags[0]
    width = x.shape[1] // size
    latent_width = latent_ref.shape[1]
    horizon = truth.shape[1]
    head = slice(latent_width, latent_width + horizon)

    @pl.when(flags[2] == 1)
    def _():
        latent = latent_ref[...]
        activated = jax.nn.silu(latent).astype(jnp.bfloat16)
        estimate = None
        product = None
        for k in range(size):
            extra = []
            for half in range(2):
                ref = halves[2 * k + half]
                part = dot_nt(x[:, half_columns(dp_index, k, half, width)], ref[head])
                estimate = part if estimate is None else estimate + part
                extra += [
                    ref[latent_width + horizon :, at : at + horizon]
                    for at in range(0, width // 2, horizon)
                ]
            extra = jnp.concatenate(extra, axis=0).astype(jnp.float32)
            product = extra if product is None else product + extra
        product = product.astype(jnp.bfloat16)
        estimate = estimate + dot_nn(activated, product)
        error = (mask[:, :1] * (estimate - truth[...])).astype(jnp.bfloat16)
        hidden_grad = dot_nt(error, product)
        latent_grad = (hidden_grad * silu_slope(latent)).astype(jnp.bfloat16)
        latent_grad_out[...] = latent_grad
        scale = inverse[:, :1]
        mean = jnp.sum(latent_grad.astype(jnp.float32) * latent, axis=-1, keepdims=True) / (
            width * size
        )
        slope = scale * scale * mean
        for k in range(size):
            for half in range(2):
                at_k = half_columns(dp_index, k, half, width)
                ref = halves[2 * k + half]
                arriving = dot_nn(error, ref[head]).astype(jnp.bfloat16)
                arriving_out[:, at_k] = arriving
                scaled = dot_nn(latent_grad, ref[:latent_width])
                grads = (
                    arriving.astype(jnp.float32)
                    + scale * (scaled * gain[:, at_k].astype(jnp.float32))
                    - x[:, at_k].astype(jnp.float32) * slope
                ).astype(jnp.bfloat16)
                grads_out[:, at_k] = grads
                for (row, end), send in zip(bounds, sends):
                    send[:, at_k] = grads[row:end]


def latent_kernel(size, *refs):
    flags, normed = refs[:2]
    down = refs[2 : 2 + 2 * size]
    latent = refs[3 + 2 * size]
    width = normed.shape[1] // size
    total = None
    for k in range(size):
        for half in range(2):
            block = normed[:, half_columns(flags[0], k, half, width)]
            part = dot_nt(block, down[2 * k + half][: latent.shape[1]])
            total = part if total is None else total + part
    latent[...] = total


def keep_kernel(size, count, more, *refs):
    flags = refs[0]
    gain, inverse, latent, x = refs[1:5]
    raw = refs[8 : 8 + count]
    kept = refs[15 + count : 15 + count + 2 * size]
    bundle, sems = refs[15 + count + 2 * size :]
    tokens, width = x.shape
    latent_width = latent.shape[1]
    shard = width // size
    rows = raw[0].shape[0] - latent_width

    @pl.when(flags[3] == 1)
    def _():
        copies = [
            pltpu.make_async_copy(raw[2 * size + k], kept[size + k].at[pl.ds(rows, more)], sems.at[k])
            for k in range(size)
            if more
        ]
        for copy in copies:
            copy.start()
        for k in range(size):
            for half in range(2):
                here = slice(half * (shard // 2), (half + 1) * (shard // 2))
                kept[k][:, here] = raw[2 * k + half][:latent_width]
                kept[size + k][:rows, here] = raw[2 * k + half][latent_width:]
        for copy in copies:
            copy.wait()

    @pl.when(flags[4] == 1)
    def _():
        block = kept[-1].shape[0]
        for k in range(size):
            bundle[k * latent_width : (k + 1) * latent_width] = kept[k][...]
            row = size * latent_width + k * block
            bundle[row : row + block] = kept[size + k][...]
        at = size * (latent_width + block)
        for k in range(size):
            here = slice(k * shard, (k + 1) * shard)
            bundle[at + k * tokens : at + (k + 1) * tokens] = x[:, here]
            row = at + size * tokens + k * GAIN_ROWS
            bundle[row : row + GAIN_ROWS] = jnp.broadcast_to(gain[:, here], (GAIN_ROWS, shard))
        at += size * (tokens + GAIN_ROWS)
        for values in (latent[...], inverse[...]):
            high = values.astype(jnp.bfloat16)
            low = (values - high.astype(jnp.float32)).astype(jnp.bfloat16)
            for part in (high, low):
                bundle[at : at + tokens, : part.shape[1]] = part
                at += tokens


def message_kernel(size, *refs):
    flags, normed = refs[:2]
    latent = refs[3]
    messages = refs[4:]
    shard = normed.shape[1] // size
    activated = jax.nn.silu(latent[...]).astype(jnp.bfloat16)
    for k in range(size):
        messages[k][:, :shard] = normed[:, columns(flags[0], k, shard)]
        messages[k][:, shard:] = activated


def step_back(dp_index, size, width, take, down, up, lat, scale, gain, x, write):
    latent_width = lat.shape[1]
    shard = width // size
    block = min(latent_width, shard)
    hidden_grad = None
    for k in range(size):
        arriving = take(columns(dp_index, k, shard))
        for at in range(0, shard, block):
            lanes = at // block * latent_width
            part = dot_nn(arriving[:, at : at + block], up(k, slice(lanes, lanes + latent_width)))
            hidden_grad = part if hidden_grad is None else hidden_grad + part
    latent_grad = (hidden_grad * silu_slope(lat)).astype(jnp.bfloat16)
    mean = jnp.sum(latent_grad.astype(jnp.float32) * lat, axis=-1, keepdims=True) / width
    slope = scale * scale * mean
    for k in range(size):
        for half in range(2):
            place = half_columns(dp_index, k, half, shard)
            arriving = take(place)
            scaled = dot_nn(latent_grad, down(k, half))
            value = (
                arriving.astype(jnp.float32)
                + scale * (scaled * gain(k, half).astype(jnp.float32))
                - x(k, half).astype(jnp.float32) * slope
            ).astype(jnp.bfloat16)
            write(place, arriving, value)
    return latent_grad


def kept_of(kept, size, shard):
    def down(k, half):
        return kept[k][:, half * (shard // 2) : (half + 1) * (shard // 2)]

    return down, lambda k, lanes: kept[size + k][:, lanes]


def stage_kernel(stage, bounds, size, held, *refs):
    flags = refs[0]
    pieces = refs[1 : 1 + len(bounds)]
    at = 1 + len(bounds)
    state = refs[at + held : at + 2 * held]
    outs = refs[at + 2 * held :]
    shard = state[3].shape[1] // size
    down, up = kept_of(state[7:], size, shard)
    state = state[:7]
    gain, inverse, latent, x, latent_grads, arrivals, grads = state
    at_rows = slice(bounds[0][0], bounds[-1][1])

    def take(place):
        parts = [piece[:, place] for piece in pieces]
        return parts[0] if len(parts) == 1 else jnp.concatenate(parts, axis=0)

    def write(place, arriving, value):
        arrivals[at_rows, place] = arriving
        grads[at_rows, place] = value
        if stage and outs:
            outs[0][:, place] = value

    @pl.when(flags[1] == stage)
    def _():
        latent_grads[at_rows] = step_back(
            flags[0],
            size,
            x.shape[1],
            take,
            down,
            up,
            latent[at_rows],
            inverse[at_rows][:, :1],
            lambda k, half: gain[:, half_columns(flags[0], k, half, shard)],
            lambda k, half: x[at_rows, half_columns(flags[0], k, half, shard)],
            write,
        )

    if stage == 0:
        for k in range(size):
            outs[k][:, :shard] = arrivals[:, columns(flags[0], k, shard)]
            outs[k][:, shard:] = latent_grads[...]


def pair_kernel(stage, bound, size, held, *refs):
    flags, received = refs[:2]
    state = refs[2 + held : 9 + held]
    kept = refs[9 + held : 9 + held + 2 * size]
    bundle = refs[1 + 2 * held]
    middle, last = refs[2 + 2 * held :]
    gain, inverse, latent, x, latent_grads, arrivals, grads = state
    tokens = x.shape[0]
    latent_width = latent.shape[1]
    shard = x.shape[1] // size
    down, up = kept_of(kept, size, shard)
    block = kept[-1].shape[0]
    at_rows = slice(*bound)

    def write(place, arriving, value):
        arrivals[at_rows, place] = arriving
        grads[at_rows, place] = value
        middle[:, place] = value

    def write_last(place, arriving, value):
        last[:, place] = value

    def next_down(k, half):
        here = slice(half * (shard // 2), (half + 1) * (shard // 2))
        return bundle[k * latent_width : (k + 1) * latent_width, here]

    def both(index, lanes):
        row = size * (latent_width + block + tokens + GAIN_ROWS) + index * tokens + bound[0]
        end = row + bound[1] - bound[0]
        high = bundle[row:end, :lanes].astype(jnp.float32)
        return high + bundle[row + tokens : end + tokens, :lanes].astype(jnp.float32)

    def next_x(k, half):
        here = slice(half * (shard // 2), (half + 1) * (shard // 2))
        start = size * (latent_width + block) + (flags[0] ^ k) * tokens + bound[0]
        return bundle[pl.ds(pl.multiple_of(start, 16), bound[1] - bound[0]), here]

    def next_gain(k, half):
        here = slice(half * (shard // 2), (half + 1) * (shard // 2))
        start = size * (latent_width + block + tokens) + (flags[0] ^ k) * GAIN_ROWS
        return bundle[pl.ds(pl.multiple_of(start, 16), GAIN_ROWS), here][:1]

    def next_up(k, lanes):
        row = size * latent_width + k * block
        return bundle[row : row + block, lanes]

    @pl.when(flags[1] == stage)
    def _():
        latent_grads[at_rows] = step_back(
            flags[0],
            size,
            x.shape[1],
            lambda place: received[:, place],
            down,
            up,
            latent[at_rows],
            inverse[at_rows][:, :1],
            lambda k, half: gain[:, half_columns(flags[0], k, half, shard)],
            lambda k, half: x[at_rows, half_columns(flags[0], k, half, shard)],
            write,
        )
        step_back(
            flags[0],
            size,
            x.shape[1],
            lambda place: middle[:, place],
            next_down,
            next_up,
            both(0, latent_width),
            both(2, 128)[:, :1],
            next_gain,
            next_x,
            write_last,
        )


def touch_kernel(*refs):
    pass


def merge_kernel(size, split, *refs):
    flags, latent, early = refs[0], refs[1], refs[2 : 2 + size]
    above = (early[0],) + refs[2 + size : 1 + 2 * size]
    left = refs[2 + 2 * size]
    tokens = early[0].shape[0]

    def fill(sources):
        for k in range(size):
            left[:, k * tokens : (k + 1) * tokens] = sources[k][...].T

    pl.when(flags[1] < split)(lambda: fill(early))
    pl.when(flags[1] >= split)(lambda: fill(above))


def weight_kernel(size, left, *refs):
    late = refs[:size]
    down_grads, up_grads, right = refs[size:]
    tokens = late[0].shape[0]
    shard = down_grads.shape[0]
    for k in range(size):
        right[k * tokens : (k + 1) * tokens] = late[k][...]
    down_grads[...] = dot_nn(left[:shard], right[:, shard:]).astype(jnp.bfloat16)
    up_grads[...] = dot_nn(left[shard:], right[:, :shard]).astype(jnp.bfloat16)


def per_device(
    section_inputs, norm_gain, down_proj, up_proj, readout_matrix, ground_truth_series, valid_len
):
    size = lax.axis_size("dp")
    sections = lax.axis_size("section")
    top = sections - 1
    dp_index = lax.axis_index("dp")
    section = lax.axis_index("section")
    f32, bf16 = jnp.float32, jnp.bfloat16

    x = section_inputs[0]
    tokens, width = x.shape
    shard, latent_width = down_proj.shape[1:]
    horizon = readout_matrix.shape[1]
    share = tokens // sum(CHUNK_SHARES)
    ends = [share * sum(CHUNK_SHARES[: i + 1]) for i in range(len(CHUNK_SHARES))]
    bounds = list(zip([0] + ends, ends))

    flags = jnp.stack(
        [
            dp_index.astype(jnp.int32),
            section.astype(jnp.int32),
            (section == top).astype(jnp.int32),
            (section < top).astype(jnp.int32),
            ((section < top - 1) & (section % 2 == 0)).astype(jnp.int32),
        ]
    )
    everyone, rest = list(range(sections)), list(range(top))
    up_block = min(latent_width, shard)
    up_lanes = latent_width * shard // up_block
    head_rows = horizon + latent_width * horizon // shard
    more = max(up_block - head_rows, 0)
    low, high, *up_rest = pl.pallas_call(
        prepare_kernel,
        out_shape=(jax.ShapeDtypeStruct((latent_width + head_rows, shard // 2), bf16),) * 2
        + (jax.ShapeDtypeStruct((more, up_lanes), bf16),) * (more > 0),
        in_specs=[SMEM] + [ANY] * 3,
        out_specs=(VMEM,) * (2 + (more > 0)),
        scratch_shapes=[
            pltpu.VMEM((1, shard, latent_width), bf16),
            pltpu.VMEM((1, latent_width, shard), bf16),
            pltpu.VMEM((shard, horizon), bf16),
            pltpu.SemaphoreType.DMA((3,)),
        ],
        cost_estimate=NOTHING,
        compiler_params=PARAMS,
    )(flags, stay(down_proj), stay(up_proj), stay(readout_matrix))
    halves = gather_halves(low, high, everyone, size)
    if more:
        up_rest, first = lax.optimization_barrier((up_rest[0], halves[2 % size][0]))
        halves[2 % size] = (first, halves[2 % size][1])
        up_rest = gather(up_rest, rest, size)
    halves = [half for pair in halves for half in pair]

    x, normed, inverse, gain = pl.pallas_call(
        norm_kernel,
        out_shape=(
            pltpu.VMEM((tokens, width), bf16),
            pltpu.VMEM((tokens, width), bf16),
            pltpu.VMEM((tokens, 128), f32),
            pltpu.VMEM((1, width), bf16),
        ),
        in_specs=[VMEM] * 2,
        out_specs=(VMEM,) * 4,
        cost_estimate=NOTHING,
        compiler_params=PARAMS,
    )(x, norm_gain)
    per_micro = tokens // valid_len.shape[0]
    mask = (
        (jnp.arange(per_micro)[None, :] < valid_len[:, None]).astype(f32).reshape(tokens, 1)
    )
    mask = jnp.broadcast_to(mask, (tokens, 128))

    normed, latent = pl.pallas_call(
        functools.partial(latent_kernel, size),
        out_shape=(held_like(normed), pltpu.VMEM((tokens, latent_width), f32)),
        in_specs=[SMEM] + [VMEM] * (1 + 2 * size),
        out_specs=(VMEM,) * 2,
        input_output_aliases={1: 0},
        cost_estimate=NOTHING,
        compiler_params=PARAMS,
    )(flags, pin(normed), *[pin(half) for half in halves])

    gain, x, inverse, latent, latent_grads, arrivals, grads, *sends = pl.pallas_call(
        functools.partial(top_kernel, size, bounds),
        out_shape=(
            held_like(gain),
            held_like(x),
            held_like(inverse),
            held_like(latent),
            pltpu.VMEM((tokens, latent_width), bf16),
            pltpu.VMEM((tokens, width), bf16),
            pltpu.VMEM((tokens, width), bf16),
        )
        + tuple(jax.ShapeDtypeStruct((end - row, width), bf16) for row, end in bounds),
        in_specs=[SMEM] + [VMEM] * (6 + 2 * size),
        out_specs=(VMEM,) * (7 + len(bounds)),
        input_output_aliases={3: 0, 4: 1, 5: 2, 6: 3},
        cost_estimate=NOTHING,
        compiler_params=PARAMS,
    )(
        flags, ground_truth_series, mask, pin(gain), pin(x), pin(inverse), pin(latent),
        *[pin(part) for part in halves],
    )

    def hop(block, sender, distance=1):
        return move(
            block, [(sender * size + i, (sender - distance) * size + i) for i in range(size)]
        )

    received = [hop(send, top) for send in sends]

    message = jax.ShapeDtypeStruct((tokens, shard + latent_width), bf16)
    shards = (*halves, *up_rest)
    state = (gain, inverse, latent, x, latent_grads, arrivals, grads)

    def run_stage(stage, bounds, received, state, sends=True):
        rows = bounds[-1][1] - bounds[0][0]
        if not stage:
            outs = (message,) * size
        else:
            outs = (jax.ShapeDtypeStruct((rows, width), bf16),) * sends
        first = 1 + len(received)
        results = pl.pallas_call(
            functools.partial(stage_kernel, stage, bounds, size, len(state)),
            out_shape=tuple(held_like(part) for part in state) + outs,
            in_specs=[SMEM] + [VMEM] * (len(received) + len(state)),
            out_specs=(VMEM,) * (len(state) + len(outs)),
            input_output_aliases={first + i: i for i in range(len(state))},
            cost_estimate=NOTHING,
            compiler_params=PARAMS,
        )(flags, *received, *[pin(part) for part in state])
        return tuple(results[: len(state)]), results[len(state) :]

    def run_pair(stage, bound, received, state):
        rows = bound[1] - bound[0]
        results = pl.pallas_call(
            functools.partial(pair_kernel, stage, bound, size, len(state)),
            out_shape=tuple(held_like(part) for part in state)
            + (jax.ShapeDtypeStruct((rows, width), bf16),) * 2,
            in_specs=[SMEM] + [VMEM] * (1 + len(state)),
            out_specs=(VMEM,) * (len(state) + 2),
            input_output_aliases={2 + i: i for i in range(len(state))},
            cost_estimate=NOTHING,
            compiler_params=PARAMS,
        )(flags, received, *[pin(part) for part in state])
        return tuple(results[: len(state)]), results[len(state) :]

    def send_messages(messages, among):
        return [messages[0]] + [move(messages[k], peers(among, size, k)) for k in range(1, size)]

    def hold(state, blocks):
        latent, *blocks = pl.pallas_call(
            touch_kernel,
            out_shape=(held_like(state[2]),) + tuple(held_like(part) for part in blocks),
            in_specs=[VMEM] * (1 + len(blocks)),
            out_specs=(VMEM,) * (1 + len(blocks)),
            input_output_aliases={i: i for i in range(1 + len(blocks))},
            cost_estimate=NOTHING,
            compiler_params=PARAMS,
        )(pin(state[2]), *[pin(part) for part in blocks])
        return state[:2] + (latent,) + state[3:], blocks

    state_kept = pl.pallas_call(
        functools.partial(keep_kernel, size, len(shards), more),
        out_shape=tuple(held_like(part) for part in state)
        + (pltpu.VMEM((latent_width, shard), bf16),) * size
        + (pltpu.VMEM((up_block, up_lanes), bf16),) * size
        + (
            jax.ShapeDtypeStruct(
                (size * (latent_width + up_block + tokens + GAIN_ROWS) + 4 * tokens, shard), bf16
            ),
        ),
        in_specs=[SMEM]
        + [VMEM] * (len(state) + 2 * size)
        + [ANY] * (len(shards) - 2 * size),
        out_specs=(VMEM,) * (len(state) + 2 * size + 1),
        scratch_shapes=[pltpu.SemaphoreType.DMA((size,))],
        input_output_aliases={1 + i: i for i in range(len(state))},
        cost_estimate=NOTHING,
        compiler_params=PARAMS,
    )(flags, *[pin(part) for part in (*state, *halves)], *up_rest)
    state, kept, bundle = tuple(state_kept[:7]), tuple(state_kept[7:-1]), state_kept[-1:]
    pairs = list(range(3, top - 1, 2))
    bundle = tuple(
        move(part, [((s - 1) * size + i, s * size + i) for s in pairs for i in range(size)])
        for part in bundle
    )

    state = state + kept
    sent = []
    for bound, block in zip(bounds, received):
        state, outs = run_stage(top - 1, [bound], [block], state)
        sent.append(hop(outs[0], top - 1))
    received = sent

    state = state + bundle

    latent, *messages = pl.pallas_call(
        functools.partial(message_kernel, size),
        out_shape=(held_like(state[2]),) + (message,) * size,
        in_specs=[SMEM] + [VMEM] * 2,
        out_specs=(VMEM,) * (1 + size),
        input_output_aliases={2: 0},
        cost_estimate=NOTHING,
        compiler_params=PARAMS,
    )(flags, pin(normed), pin(state[2]))
    state = state[:2] + (latent,) + state[3:]
    split = pairs[-1] - 1
    early = send_messages(messages, range(split))
    above = send_messages(messages, range(split, sections))

    waiting = []
    for stage in reversed(pairs):
        sent, side = [], []
        for bound, block in zip(bounds, received):
            state, outs = run_pair(stage, bound, block, state)
            sent.append(hop(outs[1], stage, 2))
            side.append(hop(outs[0], stage))
            if stage == pairs[-1] and len(sent) == 1:
                state, early = hold(state, early)
        received = sent
        for asides, bound, block in waiting:
            base, _ = run_stage(asides, [bound], [block], state[:-1], False)
            state = base + state[-1:]
        waiting = [(stage - 1, bound, block) for bound, block in zip(bounds, side)]
        if stage == pairs[0]:
            latent, left = pl.pallas_call(
                functools.partial(merge_kernel, size, split),
                out_shape=(
                    held_like(state[2]),
                    pltpu.VMEM((shard + latent_width, size * tokens), bf16),
                ),
                in_specs=[SMEM] + [VMEM] * (2 * size),
                out_specs=(VMEM,) * 2,
                input_output_aliases={1: 0},
                cost_estimate=NOTHING,
                compiler_params=PARAMS,
            )(flags, pin(state[2]), *early, *above[1:])
            state = state[:2] + (latent,) + state[3:]
    state = state[:-1]

    sent = []
    for bound, block in zip(bounds, received):
        state, outs = run_stage(1, [bound], [block], state)
        sent.append(hop(outs[0], 1))
    received = sent
    for asides, bound, block in waiting:
        state, _ = run_stage(asides, [bound], [block], state, False)
    state, outs = run_stage(0, bounds, received, state)
    late = send_messages(outs, everyone)
    down_grads, up_grads = pl.pallas_call(
        functools.partial(weight_kernel, size),
        out_shape=(
            jax.ShapeDtypeStruct((shard, latent_width), bf16),
            jax.ShapeDtypeStruct((latent_width, shard), bf16),
        ),
        in_specs=[VMEM] * (1 + size),
        out_specs=(VMEM,) * 2,
        scratch_shapes=[pltpu.VMEM((size * tokens, shard + latent_width), bf16)],
        compiler_params=PARAMS,
    )(pin(left), *late)
    return (state[6][None], down_grads[None], up_grads[None])


def solution(mesh):
    placed = (
        P("section", "dp", None),
        P("section", None),
        P("section", "dp", None),
        P("section", None, "dp"),
        P("dp", None),
        P("dp", None),
        P("dp"),
    )
    return jax.shard_map(
        per_device,
        mesh=mesh,
        in_specs=placed,
        out_specs=(P("section", "dp", None), P("section", "dp", None), P("section", None, "dp")),
        check_vma=False,
    )
```

```python
import functools

import jax
import jax.numpy as jnp
from jax import lax
from jax.experimental import pallas as pl
from jax.experimental.pallas import tpu as pltpu
from jax.sharding import PartitionSpec as P

EPSILON = 1e-05
CHUNK_SHARES = (4, 4)
GAIN_ROWS = 16
ANY = pl.BlockSpec(memory_space=pl.ANY)
VMEM = pl.BlockSpec(memory_space=pltpu.VMEM)
SMEM = pl.BlockSpec(memory_space=pltpu.SMEM)
NOTHING = pl.CostEstimate(flops=0, bytes_accessed=0, transcendentals=0)
PARAMS = pltpu.CompilerParams(vmem_limit_bytes=20 * 1024 * 1024)


def dot_nn(left, right):
    return lax.dot_general(
        left, right, (((1,), (0,)), ((), ())), preferred_element_type=jnp.float32
    )


def dot_nt(left, right):
    return lax.dot_general(
        left, right, (((1,), (1,)), ((), ())), preferred_element_type=jnp.float32
    )


def dot_tn(left, right):
    return lax.dot_general(
        left, right, (((0,), (0,)), ((), ())), preferred_element_type=jnp.float32
    )


def silu_slope(latent):
    sigmoid = jax.nn.sigmoid(latent)
    return sigmoid * (1.0 + latent * (1.0 - sigmoid))


def move(block, pairs):
    return lax.ppermute(block, ("section", "dp"), pairs)


def peers(sections, size, k):
    return [(s * size + i, s * size + (i ^ k)) for s in sections for i in range(size)]


def gather(block, sections, size):
    return [block] + [move(block, peers(sections, size, k)) for k in range(1, size)]


def gather_halves(low, high, sections, size):
    if size != 4:
        return list(zip(gather(low, sections, size), gather(high, sections, size)))
    across, along = peers(sections, size, 1), peers(sections, size, 2)
    low_along = move(low, along)
    high_across = move(high, across)
    high_along = move(high, along)
    low_across = move(low, across)
    low_far = move(low_along, across)
    high_far = move(high_across, along)
    return [(low, high), (low_across, high_across), (low_along, high_along), (low_far, high_far)]


def pin(block):
    return pltpu.with_memory_space_constraint(block, pltpu.VMEM)


def stay(block):
    return pltpu.with_memory_space_constraint(block, pltpu.HBM)


def held_like(block):
    return pltpu.VMEM(block.shape, block.dtype)


def columns(dp_index, k, width):
    return pl.ds(pl.multiple_of((dp_index ^ k) * width, width), width)


def half_columns(dp_index, k, half, width):
    start = (dp_index ^ k) * width + half * (width // 2)
    return pl.ds(pl.multiple_of(start, width // 2), width // 2)


def prepare_kernel(flags, down, up, readout, *refs):
    low, high, *rest, down_held, up_held, readout_held, sems = refs
    copies = [
        pltpu.make_async_copy(down, down_held, sems.at[0]),
        pltpu.make_async_copy(up, up_held, sems.at[1]),
        pltpu.make_async_copy(readout, readout_held, sems.at[2]),
    ]
    for copy in copies:
        copy.start()
    latent_width, shard = up_held.shape[1:]
    horizon = readout_held.shape[1]
    half = shard // 2
    head_rows = low.shape[0] - latent_width
    copies[0].wait()
    turned = down_held[0].T
    low[:latent_width] = turned[:, :half]
    high[:latent_width] = turned[:, half:]
    copies[1].wait()
    copies[2].wait()
    values = up_held[0]

    @pl.when(flags[2] == 1)
    def _():
        product = dot_nn(values, readout_held[...]).astype(jnp.bfloat16)
        turned_readout = readout_held[...].T
        rows = latent_width * horizon // shard
        for out, start in ((low, 0), (high, half)):
            out[latent_width : latent_width + horizon] = turned_readout[:, start : start + half]
            for at in range(0, half, horizon):
                row = (start + at) // horizon * rows
                out[latent_width + horizon :, at : at + horizon] = product[row : row + rows]

    @pl.when(flags[2] == 0)
    def _():
        block = min(latent_width, shard)
        blocks = [values[:, at : at + block].T for at in range(0, shard, block)]
        whole = blocks[0] if len(blocks) == 1 else jnp.concatenate(blocks, axis=1)
        low[latent_width:] = whole[:head_rows, :half]
        high[latent_width:] = whole[:head_rows, half:]
        if rest:
            rest[0][...] = whole[head_rows:]


def norm_kernel(x, gain, truth, x_out, normed_out, inverse_out, gain_out, truth_out):
    truth_out[...] = truth[...]
    values = x[...].astype(jnp.float32)
    inverse = lax.rsqrt(jnp.mean(values * values, axis=-1, keepdims=True) + EPSILON)
    x_out[...] = x[...]
    normed_out[...] = (values * inverse * gain[...].astype(jnp.float32)).astype(jnp.bfloat16)
    inverse_out[...] = jnp.broadcast_to(inverse, inverse_out.shape)
    gain_out[...] = gain[...]


def top_kernel(size, bounds, *refs):
    flags, truth, mask = refs[:3]
    halves = refs[7 : 7 + 2 * size]
    gain, x, inverse, normed, latent_ref, latent_grad_out, arriving_out, grads_out = refs[
        7 + 2 * size : 15 + 2 * size
    ]
    sends = refs[15 + 2 * size :]
    dp_index = flags[0]
    width = x.shape[1] // size
    latent_width = latent_ref.shape[1]
    horizon = truth.shape[1]
    head = slice(latent_width, latent_width + horizon)

    @pl.when(flags[2] == 1)
    def _():
        latent = latent_of(dp_index, size, normed, halves, latent_width)
        latent_ref[...] = latent
        activated = jax.nn.silu(latent).astype(jnp.bfloat16)
        estimate = None
        product = None
        for k in range(size):
            extra = []
            for half in range(2):
                ref = halves[2 * k + half]
                part = dot_nt(x[:, half_columns(dp_index, k, half, width)], ref[head])
                estimate = part if estimate is None else estimate + part
                extra += [
                    ref[latent_width + horizon :, at : at + horizon]
                    for at in range(0, width // 2, horizon)
                ]
            extra = jnp.concatenate(extra, axis=0).astype(jnp.float32)
            product = extra if product is None else product + extra
        product = product.astype(jnp.bfloat16)
        estimate = estimate + dot_nn(activated, product)
        error = (mask[:, :1] * (estimate - truth[...])).astype(jnp.bfloat16)
        hidden_grad = dot_nt(error, product)
        latent_grad = (hidden_grad * silu_slope(latent)).astype(jnp.bfloat16)
        latent_grad_out[...] = latent_grad
        scale = inverse[:, :1]
        mean = jnp.sum(latent_grad.astype(jnp.float32) * latent, axis=-1, keepdims=True) / (
            width * size
        )
        slope = scale * scale * mean
        for k in range(size):
            for half in range(2):
                at_k = half_columns(dp_index, k, half, width)
                ref = halves[2 * k + half]
                arriving = dot_nn(error, ref[head]).astype(jnp.bfloat16)
                arriving_out[:, at_k] = arriving
                scaled = dot_nn(latent_grad, ref[:latent_width])
                grads = (
                    arriving.astype(jnp.float32)
                    + scale * (scaled * gain[:, at_k].astype(jnp.float32))
                    - x[:, at_k].astype(jnp.float32) * slope
                ).astype(jnp.bfloat16)
                grads_out[:, at_k] = grads
                for (row, end), send in zip(bounds, sends):
                    send[:, at_k] = grads[row:end]


def latent_of(dp_index, size, normed, halves, latent_width):
    width = normed.shape[1] // size
    total = None
    for k in range(size):
        for half in range(2):
            block = normed[:, half_columns(dp_index, k, half, width)]
            part = dot_nt(block, halves[2 * k + half][:latent_width])
            total = part if total is None else total + part
    return total


def keep_kernel(size, count, more, *refs):
    flags = refs[0]
    gain, inverse, _, x = refs[1:5]
    raw = refs[9 : 9 + count]
    latent, normed = refs[11 + count], refs[16 + count]
    kept = refs[17 + count : 17 + count + 2 * size]
    bundle, sems = refs[17 + count + 2 * size :]
    tokens, width = x.shape
    latent_width = latent.shape[1]
    shard = width // size
    rows = raw[0].shape[0] - latent_width

    @pl.when(flags[3] == 1)
    def _():
        sources = list(raw[2 * size :])
        if len(sources) < size and more:
            sources[2:] = [raw[-1].at[pl.ds(0, more)], raw[-1].at[pl.ds(more, more)]]
        copies = [
            pltpu.make_async_copy(source, kept[size + k].at[pl.ds(rows, more)], sems.at[k])
            for k, source in enumerate(sources)
        ]
        for copy in copies:
            copy.start()
        latent[...] = latent_of(flags[0], size, normed, raw, latent_width)
        for k in range(size):
            for half in range(2):
                here = slice(half * (shard // 2), (half + 1) * (shard // 2))
                kept[k][:, here] = raw[2 * k + half][:latent_width]
                kept[size + k][:rows, here] = raw[2 * k + half][latent_width:]
        for copy in copies:
            copy.wait()

    @pl.when(flags[4] == 1)
    def _():
        block = kept[-1].shape[0]
        for k in range(size):
            bundle[k * latent_width : (k + 1) * latent_width] = kept[k][...]
            row = size * latent_width + k * block
            bundle[row : row + block] = kept[size + k][...]
        at = size * (latent_width + block)
        for k in range(size):
            here = slice(k * shard, (k + 1) * shard)
            bundle[at + k * tokens : at + (k + 1) * tokens] = x[:, here]
            row = at + size * tokens + k * GAIN_ROWS
            bundle[row : row + GAIN_ROWS] = jnp.broadcast_to(gain[:, here], (GAIN_ROWS, shard))
        at += size * (tokens + GAIN_ROWS)
        for values in (latent[...], inverse[...]):
            high = values.astype(jnp.bfloat16)
            low = (values - high.astype(jnp.float32)).astype(jnp.bfloat16)
            for part in (high, low):
                bundle[at : at + tokens, : part.shape[1]] = part
                at += tokens


def message_kernel(size, *refs):
    flags, normed = refs[:2]
    latent = refs[3]
    messages = refs[4:]
    shard = normed.shape[1] // size
    activated = jax.nn.silu(latent[...]).astype(jnp.bfloat16)
    for k in range(size):
        messages[k][:, :shard] = normed[:, columns(flags[0], k, shard)]
        messages[k][:, shard:] = activated


def step_back(dp_index, size, width, take, down, up, lat, scale, gain, x, write):
    latent_width = lat.shape[1]
    shard = width // size
    block = min(latent_width, shard)
    hidden_grad = None
    for k in range(size):
        arriving = take(columns(dp_index, k, shard))
        for at in range(0, shard, block):
            lanes = at // block * latent_width
            part = dot_nn(arriving[:, at : at + block], up(k, slice(lanes, lanes + latent_width)))
            hidden_grad = part if hidden_grad is None else hidden_grad + part
    latent_grad = (hidden_grad * silu_slope(lat)).astype(jnp.bfloat16)
    mean = jnp.sum(latent_grad.astype(jnp.float32) * lat, axis=-1, keepdims=True) / width
    slope = scale * scale * mean
    for k in range(size):
        for half in range(2):
            place = half_columns(dp_index, k, half, shard)
            arriving = take(place)
            scaled = dot_nn(latent_grad, down(k, half))
            value = (
                arriving.astype(jnp.float32)
                + scale * (scaled * gain(k, half).astype(jnp.float32))
                - x(k, half).astype(jnp.float32) * slope
            ).astype(jnp.bfloat16)
            write(place, arriving, value)
    return latent_grad


def kept_of(kept, size, shard):
    def down(k, half):
        return kept[k][:, half * (shard // 2) : (half + 1) * (shard // 2)]

    return down, lambda k, lanes: kept[size + k][:, lanes]


def stage_kernel(stage, bounds, size, held, *refs):
    flags = refs[0]
    pieces = refs[1 : 1 + len(bounds)]
    at = 1 + len(bounds)
    state = refs[at + held : at + 2 * held]
    outs = refs[at + 2 * held :]
    shard = state[3].shape[1] // size
    down, up = kept_of(state[7:], size, shard)
    state = state[:7]
    gain, inverse, latent, x, latent_grads, arrivals, grads = state
    tokens = x.shape[0]
    at_rows = slice(bounds[0][0], bounds[-1][1])

    def take(place):
        parts = [
            piece[slice(*bound) if piece.shape[0] == tokens else slice(None), place]
            for bound, piece in zip(bounds, pieces)
        ]
        return parts[0] if len(parts) == 1 else jnp.concatenate(parts, axis=0)

    def write(place, arriving, value):
        arrivals[at_rows, place] = arriving
        grads[at_rows, place] = value
        if stage and outs:
            outs[0][:, place] = value

    @pl.when(flags[1] == stage)
    def _():
        latent_grads[at_rows] = step_back(
            flags[0],
            size,
            x.shape[1],
            take,
            down,
            up,
            latent[at_rows],
            inverse[at_rows][:, :1],
            lambda k, half: gain[:, half_columns(flags[0], k, half, shard)],
            lambda k, half: x[at_rows, half_columns(flags[0], k, half, shard)],
            write,
        )

    if stage == 0:
        for k in range(size):
            outs[k][:, :shard] = arrivals[:, columns(flags[0], k, shard)]
            outs[k][:, shard:] = latent_grads[...]


def pair_kernel(stage, bound, size, held, *refs):
    flags, received = refs[:2]
    state = refs[2 + held : 9 + held]
    kept = refs[9 + held : 9 + held + 2 * size]
    bundle = refs[1 + 2 * held]
    middle, last = refs[2 + 2 * held :]
    gain, inverse, latent, x, latent_grads, arrivals, grads = state
    tokens = x.shape[0]
    latent_width = latent.shape[1]
    shard = x.shape[1] // size
    down, up = kept_of(kept, size, shard)
    block = kept[-1].shape[0]
    at_rows = slice(*bound)

    def write(place, arriving, value):
        arrivals[at_rows, place] = arriving
        grads[at_rows, place] = value
        middle[:, place] = value

    def write_last(place, arriving, value):
        last[:, place] = value

    def next_down(k, half):
        here = slice(half * (shard // 2), (half + 1) * (shard // 2))
        return bundle[k * latent_width : (k + 1) * latent_width, here]

    def both(index, lanes):
        row = size * (latent_width + block + tokens + GAIN_ROWS) + index * tokens + bound[0]
        end = row + bound[1] - bound[0]
        high = bundle[row:end, :lanes].astype(jnp.float32)
        return high + bundle[row + tokens : end + tokens, :lanes].astype(jnp.float32)

    def next_x(k, half):
        here = slice(half * (shard // 2), (half + 1) * (shard // 2))
        start = size * (latent_width + block) + (flags[0] ^ k) * tokens + bound[0]
        return bundle[pl.ds(pl.multiple_of(start, 16), bound[1] - bound[0]), here]

    def next_gain(k, half):
        here = slice(half * (shard // 2), (half + 1) * (shard // 2))
        start = size * (latent_width + block + tokens) + (flags[0] ^ k) * GAIN_ROWS
        return bundle[pl.ds(pl.multiple_of(start, 16), GAIN_ROWS), here][:1]

    def next_up(k, lanes):
        row = size * latent_width + k * block
        return bundle[row : row + block, lanes]

    @pl.when(flags[1] == stage)
    def _():
        latent_grads[at_rows] = step_back(
            flags[0],
            size,
            x.shape[1],
            lambda place: received[:, place],
            down,
            up,
            latent[at_rows],
            inverse[at_rows][:, :1],
            lambda k, half: gain[:, half_columns(flags[0], k, half, shard)],
            lambda k, half: x[at_rows, half_columns(flags[0], k, half, shard)],
            write,
        )
        step_back(
            flags[0],
            size,
            x.shape[1],
            lambda place: middle[:, place],
            next_down,
            next_up,
            both(0, latent_width),
            both(2, 128)[:, :1],
            next_gain,
            next_x,
            write_last,
        )


def touch_kernel(*refs):
    pass


def merge_kernel(size, split, *refs):
    flags, latent, early = refs[0], refs[1], refs[2 : 2 + size]
    above = (early[0],) + refs[2 + size : 1 + 2 * size]
    left = refs[2 + 2 * size]
    tokens = early[0].shape[0]

    def fill(sources):
        for k in range(size):
            left[:, k * tokens : (k + 1) * tokens] = sources[k][...].T

    pl.when(flags[1] < split)(lambda: fill(early))
    pl.when(flags[1] >= split)(lambda: fill(above))


def weight_kernel(size, left, *refs):
    late = refs[:size]
    down_grads, up_grads, right = refs[size:]
    tokens = late[0].shape[0]
    shard = down_grads.shape[0]
    for k in range(size):
        right[k * tokens : (k + 1) * tokens] = late[k][...]
    down_grads[...] = dot_nn(left[:shard], right[:, shard:]).astype(jnp.bfloat16)
    up_grads[...] = dot_nn(left[shard:], right[:, :shard]).astype(jnp.bfloat16)


def per_device(
    section_inputs, norm_gain, down_proj, up_proj, readout_matrix, ground_truth_series, valid_len
):
    size = lax.axis_size("dp")
    sections = lax.axis_size("section")
    top = sections - 1
    dp_index = lax.axis_index("dp")
    section = lax.axis_index("section")
    f32, bf16 = jnp.float32, jnp.bfloat16

    x = section_inputs[0]
    tokens, width = x.shape
    shard, latent_width = down_proj.shape[1:]
    horizon = readout_matrix.shape[1]
    share = tokens // sum(CHUNK_SHARES)
    ends = [share * sum(CHUNK_SHARES[: i + 1]) for i in range(len(CHUNK_SHARES))]
    bounds = list(zip([0] + ends, ends))

    flags = jnp.stack(
        [
            dp_index.astype(jnp.int32),
            section.astype(jnp.int32),
            (section == top).astype(jnp.int32),
            (section < top).astype(jnp.int32),
            ((section < top - 1) & (section % 2 == 0)).astype(jnp.int32),
        ]
    )
    everyone, rest = list(range(sections)), list(range(top))
    up_block = min(latent_width, shard)
    up_lanes = latent_width * shard // up_block
    head_rows = horizon + latent_width * horizon // shard
    more = max(up_block - head_rows, 0)
    low, high, *up_rest = pl.pallas_call(
        prepare_kernel,
        out_shape=(jax.ShapeDtypeStruct((latent_width + head_rows, shard // 2), bf16),) * 2
        + (jax.ShapeDtypeStruct((more, up_lanes), bf16),) * (more > 0),
        in_specs=[SMEM] + [ANY] * 3,
        out_specs=(VMEM,) * (2 + (more > 0)),
        scratch_shapes=[
            pltpu.VMEM((1, shard, latent_width), bf16),
            pltpu.VMEM((1, latent_width, shard), bf16),
            pltpu.VMEM((shard, horizon), bf16),
            pltpu.SemaphoreType.DMA((3,)),
        ],
        cost_estimate=NOTHING,
        compiler_params=PARAMS,
    )(flags, stay(down_proj), stay(up_proj), stay(readout_matrix))
    halves = gather_halves(low, high, everyone, size)
    if more:
        up_rest = up_rest[0]
        if size == 4:
            across = move(up_rest, peers(rest, size, 1))
            along = move(jnp.concatenate([up_rest, across]), peers(rest, size, 2))
            up_rest = [up_rest, across, along]
        else:
            up_rest = gather(up_rest, rest, size)
    halves = [half for pair in halves for half in pair]

    x, normed, inverse, gain, truth = pl.pallas_call(
        norm_kernel,
        out_shape=(
            pltpu.VMEM((tokens, width), bf16),
            pltpu.VMEM((tokens, width), bf16),
            pltpu.VMEM((tokens, 128), f32),
            pltpu.VMEM((1, width), bf16),
            held_like(ground_truth_series),
        ),
        in_specs=[VMEM] * 3,
        out_specs=(VMEM,) * 5,
        cost_estimate=NOTHING,
        compiler_params=PARAMS,
    )(x, norm_gain, ground_truth_series)
    per_micro = tokens // valid_len.shape[0]
    mask = (
        (jnp.arange(per_micro)[None, :] < valid_len[:, None]).astype(f32).reshape(tokens, 1)
    )
    mask = jnp.broadcast_to(mask, (tokens, 128))

    gain, x, inverse, normed, latent, latent_grads, arrivals, grads, *sends = pl.pallas_call(
        functools.partial(top_kernel, size, [(0, tokens)]),
        out_shape=(
            held_like(gain),
            held_like(x),
            held_like(inverse),
            held_like(normed),
            pltpu.VMEM((tokens, latent_width), f32),
            pltpu.VMEM((tokens, latent_width), bf16),
            pltpu.VMEM((tokens, width), bf16),
            pltpu.VMEM((tokens, width), bf16),
        )
        + (jax.ShapeDtypeStruct((tokens, width), bf16),),
        in_specs=[SMEM] + [VMEM] * (6 + 2 * size),
        out_specs=(VMEM,) * 9,
        input_output_aliases={3: 0, 4: 1, 5: 2, 6: 3},
        cost_estimate=NOTHING,
        compiler_params=PARAMS,
    )(
        flags, pin(truth), mask, pin(gain), pin(x), pin(inverse), pin(normed),
        *[pin(part) for part in halves],
    )

    def hop(block, sender, distance=1):
        return move(
            block, [(sender * size + i, (sender - distance) * size + i) for i in range(size)]
        )

    received = [hop(sends[0], top)] * len(bounds)

    message = jax.ShapeDtypeStruct((tokens, shard + latent_width), bf16)
    shards = (*halves, *up_rest)
    state = (gain, inverse, latent, x, latent_grads, arrivals, grads)

    def run_stage(stage, bounds, received, state, sends=True):
        rows = bounds[-1][1] - bounds[0][0]
        if not stage:
            outs = (message,) * size
        else:
            outs = (jax.ShapeDtypeStruct((rows, width), bf16),) * sends
        first = 1 + len(received)
        results = pl.pallas_call(
            functools.partial(stage_kernel, stage, bounds, size, len(state)),
            out_shape=tuple(held_like(part) for part in state) + outs,
            in_specs=[SMEM] + [VMEM] * (len(received) + len(state)),
            out_specs=(VMEM,) * (len(state) + len(outs)),
            input_output_aliases={first + i: i for i in range(len(state))},
            cost_estimate=NOTHING,
            compiler_params=PARAMS,
        )(flags, *received, *[pin(part) for part in state])
        return tuple(results[: len(state)]), results[len(state) :]

    def run_pair(stage, bound, received, state):
        rows = bound[1] - bound[0]
        results = pl.pallas_call(
            functools.partial(pair_kernel, stage, bound, size, len(state)),
            out_shape=tuple(held_like(part) for part in state)
            + (jax.ShapeDtypeStruct((rows, width), bf16),) * 2,
            in_specs=[SMEM] + [VMEM] * (1 + len(state)),
            out_specs=(VMEM,) * (len(state) + 2),
            input_output_aliases={2 + i: i for i in range(len(state))},
            cost_estimate=NOTHING,
            compiler_params=PARAMS,
        )(flags, received, *[pin(part) for part in state])
        return tuple(results[: len(state)]), results[len(state) :]

    def send_messages(messages, among):
        return [messages[0]] + [move(messages[k], peers(among, size, k)) for k in range(1, size)]

    def hold(state, blocks):
        latent, *blocks = pl.pallas_call(
            touch_kernel,
            out_shape=(held_like(state[2]),) + tuple(held_like(part) for part in blocks),
            in_specs=[VMEM] * (1 + len(blocks)),
            out_specs=(VMEM,) * (1 + len(blocks)),
            input_output_aliases={i: i for i in range(1 + len(blocks))},
            cost_estimate=NOTHING,
            compiler_params=PARAMS,
        )(pin(state[2]), *[pin(part) for part in blocks])
        return state[:2] + (latent,) + state[3:], blocks

    state_kept = pl.pallas_call(
        functools.partial(keep_kernel, size, len(shards), more),
        out_shape=tuple(held_like(part) for part in (*state, normed))
        + (pltpu.VMEM((latent_width, shard), bf16),) * size
        + (pltpu.VMEM((up_block, up_lanes), bf16),) * size
        + (
            jax.ShapeDtypeStruct(
                (size * (latent_width + up_block + tokens + GAIN_ROWS) + 4 * tokens, shard), bf16
            ),
        ),
        in_specs=[SMEM]
        + [VMEM] * (len(state) + 1 + 2 * size)
        + [ANY] * (len(shards) - 2 * size),
        out_specs=(VMEM,) * (len(state) + 2 * size + 2),
        scratch_shapes=[pltpu.SemaphoreType.DMA((size,))],
        input_output_aliases={1 + i: i for i in range(len(state) + 1)},
        cost_estimate=NOTHING,
        compiler_params=PARAMS,
    )(flags, *[pin(part) for part in (*state, normed, *halves)], *up_rest)
    state, normed = tuple(state_kept[:7]), state_kept[7]
    kept, bundle = tuple(state_kept[8:-1]), state_kept[-1:]
    pairs = list(range(3, top - 1, 2))
    bundle = tuple(
        move(part, [((s - 1) * size + i, s * size + i) for s in pairs for i in range(size)])
        for part in bundle
    )

    state = state + kept
    sent = []
    for bound, block in zip(bounds, received):
        state, outs = run_stage(top - 1, [bound], [block], state)
        sent.append(hop(outs[0], top - 1))
    received = sent

    state = state + bundle

    latent, *messages = pl.pallas_call(
        functools.partial(message_kernel, size),
        out_shape=(held_like(state[2]),) + (message,) * size,
        in_specs=[SMEM] + [VMEM] * 2,
        out_specs=(VMEM,) * (1 + size),
        input_output_aliases={2: 0},
        cost_estimate=NOTHING,
        compiler_params=PARAMS,
    )(flags, pin(normed), pin(state[2]))
    state = state[:2] + (latent,) + state[3:]
    split = pairs[-1] - 1
    early = send_messages(messages, range(split))
    above = send_messages(messages, range(split, sections))

    waiting = []
    for stage in reversed(pairs):
        sent, side = [], []
        for bound, block in zip(bounds, received):
            state, outs = run_pair(stage, bound, block, state)
            sent.append(hop(outs[1], stage, 2))
            side.append(hop(outs[0], stage))
            if stage == pairs[-1] and len(sent) == 1:
                state, early = hold(state, early)
        received = sent
        for asides, bound, block in waiting:
            base, _ = run_stage(asides, [bound], [block], state[:-1], False)
            state = base + state[-1:]
        waiting = [(stage - 1, bound, block) for bound, block in zip(bounds, side)]
        if stage == pairs[0]:
            latent, left = pl.pallas_call(
                functools.partial(merge_kernel, size, split),
                out_shape=(
                    held_like(state[2]),
                    pltpu.VMEM((shard + latent_width, size * tokens), bf16),
                ),
                in_specs=[SMEM] + [VMEM] * (2 * size),
                out_specs=(VMEM,) * 2,
                input_output_aliases={1: 0},
                cost_estimate=NOTHING,
                compiler_params=PARAMS,
            )(flags, pin(state[2]), *early, *above[1:])
            state = state[:2] + (latent,) + state[3:]
    state = state[:-1]

    sent = []
    for bound, block in zip(bounds, received):
        state, outs = run_stage(1, [bound], [block], state)
        sent.append(hop(outs[0], 1))
    received = sent
    for asides, bound, block in waiting:
        state, _ = run_stage(asides, [bound], [block], state, False)
    state, outs = run_stage(0, bounds, received, state)
    late = send_messages(outs, everyone)
    down_grads, up_grads = pl.pallas_call(
        functools.partial(weight_kernel, size),
        out_shape=(
            jax.ShapeDtypeStruct((shard, latent_width), bf16),
            jax.ShapeDtypeStruct((latent_width, shard), bf16),
        ),
        in_specs=[VMEM] * (1 + size),
        out_specs=(VMEM,) * 2,
        scratch_shapes=[pltpu.VMEM((size * tokens, shard + latent_width), bf16)],
        compiler_params=PARAMS,
    )(pin(left), *late)
    return (state[6][None], down_grads[None], up_grads[None])


def solution(mesh):
    placed = (
        P("section", "dp", None),
        P("section", None),
        P("section", "dp", None),
        P("section", None, "dp"),
        P("dp", None),
        P("dp", None),
        P("dp"),
    )
    return jax.shard_map(
        per_device,
        mesh=mesh,
        in_specs=placed,
        out_specs=(P("section", "dp", None), P("section", "dp", None), P("section", None, "dp")),
        check_vma=False,
    )
```

```python
import functools

import jax
import jax.numpy as jnp
from jax import lax
from jax.experimental import pallas as pl
from jax.experimental.pallas import tpu as pltpu
from jax.sharding import PartitionSpec as P

EPSILON = 1e-05
CHUNK_SHARES = (4, 4)
GAIN_ROWS = 16
ANY = pl.BlockSpec(memory_space=pl.ANY)
VMEM = pl.BlockSpec(memory_space=pltpu.VMEM)
SMEM = pl.BlockSpec(memory_space=pltpu.SMEM)
NOTHING = pl.CostEstimate(flops=0, bytes_accessed=0, transcendentals=0)
PARAMS = pltpu.CompilerParams(vmem_limit_bytes=20 * 1024 * 1024)


def dot_nn(left, right):
    return lax.dot_general(
        left, right, (((1,), (0,)), ((), ())), preferred_element_type=jnp.float32
    )


def dot_nt(left, right):
    return lax.dot_general(
        left, right, (((1,), (1,)), ((), ())), preferred_element_type=jnp.float32
    )


def dot_tn(left, right):
    return lax.dot_general(
        left, right, (((0,), (0,)), ((), ())), preferred_element_type=jnp.float32
    )


def silu_slope(latent):
    sigmoid = jax.nn.sigmoid(latent)
    return sigmoid * (1.0 + latent * (1.0 - sigmoid))


def move(block, pairs):
    return lax.ppermute(block, ("section", "dp"), pairs)


def peers(sections, size, k):
    return [(s * size + i, s * size + (i ^ k)) for s in sections for i in range(size)]


def gather(block, sections, size):
    return [block] + [move(block, peers(sections, size, k)) for k in range(1, size)]


def gather_halves(low, high, sections, size):
    if size != 4:
        return list(zip(gather(low, sections, size), gather(high, sections, size)))
    across, along = peers(sections, size, 1), peers(sections, size, 2)
    low_along = move(low, along)
    high_across = move(high, across)
    high_along = move(high, along)
    low_across = move(low, across)
    low_far = move(low_along, across)
    high_far = move(high_across, along)
    return [(low, high), (low_across, high_across), (low_along, high_along), (low_far, high_far)]


def pin(block):
    return pltpu.with_memory_space_constraint(block, pltpu.VMEM)


def stay(block):
    return pltpu.with_memory_space_constraint(block, pltpu.HBM)


def held_like(block):
    return pltpu.VMEM(block.shape, block.dtype)


def columns(dp_index, k, width):
    return pl.ds(pl.multiple_of((dp_index ^ k) * width, width), width)


def half_columns(dp_index, k, half, width):
    start = (dp_index ^ k) * width + half * (width // 2)
    return pl.ds(pl.multiple_of(start, width // 2), width // 2)


def prepare_kernel(flags, down, up, readout, *refs):
    low, high, *rest, down_held, up_held, readout_held, sems = refs
    copies = [
        pltpu.make_async_copy(down, down_held, sems.at[0]),
        pltpu.make_async_copy(up, up_held, sems.at[1]),
        pltpu.make_async_copy(readout, readout_held, sems.at[2]),
    ]
    for copy in copies:
        copy.start()
    latent_width, shard = up_held.shape[1:]
    horizon = readout_held.shape[1]
    half = shard // 2
    head_rows = low.shape[0] - latent_width
    copies[0].wait()
    turned = down_held[0].T
    low[:latent_width] = turned[:, :half]
    high[:latent_width] = turned[:, half:]
    copies[1].wait()
    copies[2].wait()
    values = up_held[0]

    @pl.when(flags[2] == 1)
    def _():
        product = dot_nn(values, readout_held[...]).astype(jnp.bfloat16)
        turned_readout = readout_held[...].T
        rows = latent_width * horizon // shard
        for out, start in ((low, 0), (high, half)):
            out[latent_width : latent_width + horizon] = turned_readout[:, start : start + half]
            for at in range(0, half, horizon):
                row = (start + at) // horizon * rows
                out[latent_width + horizon :, at : at + horizon] = product[row : row + rows]

    @pl.when(flags[2] == 0)
    def _():
        block = min(latent_width, shard)
        blocks = [values[:, at : at + block].T for at in range(0, shard, block)]
        whole = blocks[0] if len(blocks) == 1 else jnp.concatenate(blocks, axis=1)
        low[latent_width:] = whole[:head_rows, :half]
        high[latent_width:] = whole[:head_rows, half:]
        if rest:
            rest[0][...] = whole[head_rows:]


def norm_kernel(x, gain, truth, x_out, normed_out, inverse_out, gain_out, truth_out):
    truth_out[...] = truth[...]
    values = x[...].astype(jnp.float32)
    inverse = lax.rsqrt(jnp.mean(values * values, axis=-1, keepdims=True) + EPSILON)
    x_out[...] = x[...]
    normed_out[...] = (values * inverse * gain[...].astype(jnp.float32)).astype(jnp.bfloat16)
    inverse_out[...] = jnp.broadcast_to(inverse, inverse_out.shape)
    gain_out[...] = gain[...]


def top_kernel(size, bounds, *refs):
    flags, truth, mask = refs[:3]
    halves = refs[7 : 7 + 2 * size]
    gain, x, inverse, normed, latent_ref, latent_grad_out, arriving_out, grads_out = refs[
        7 + 2 * size : 15 + 2 * size
    ]
    sends = refs[15 + 2 * size :]
    dp_index = flags[0]
    width = x.shape[1] // size
    latent_width = latent_ref.shape[1]
    horizon = truth.shape[1]
    head = slice(latent_width, latent_width + horizon)

    @pl.when(flags[2] == 1)
    def _():
        latent = latent_of(dp_index, size, normed, halves, latent_width)
        latent_ref[...] = latent
        activated = jax.nn.silu(latent).astype(jnp.bfloat16)
        estimate = None
        product = None
        for k in range(size):
            extra = []
            for half in range(2):
                ref = halves[2 * k + half]
                part = dot_nt(x[:, half_columns(dp_index, k, half, width)], ref[head])
                estimate = part if estimate is None else estimate + part
                extra += [
                    ref[latent_width + horizon :, at : at + horizon]
                    for at in range(0, width // 2, horizon)
                ]
            extra = jnp.concatenate(extra, axis=0).astype(jnp.float32)
            product = extra if product is None else product + extra
        product = product.astype(jnp.bfloat16)
        estimate = estimate + dot_nn(activated, product)
        error = (mask[:, :1] * (estimate - truth[...])).astype(jnp.bfloat16)
        hidden_grad = dot_nt(error, product)
        latent_grad = (hidden_grad * silu_slope(latent)).astype(jnp.bfloat16)
        latent_grad_out[...] = latent_grad
        scale = inverse[:, :1]
        mean = jnp.sum(latent_grad.astype(jnp.float32) * latent, axis=-1, keepdims=True) / (
            width * size
        )
        slope = scale * scale * mean
        for k in range(size):
            for half in range(2):
                at_k = half_columns(dp_index, k, half, width)
                ref = halves[2 * k + half]
                arriving = dot_nn(error, ref[head]).astype(jnp.bfloat16)
                arriving_out[:, at_k] = arriving
                scaled = dot_nn(latent_grad, ref[:latent_width])
                grads = (
                    arriving.astype(jnp.float32)
                    + scale * (scaled * gain[:, at_k].astype(jnp.float32))
                    - x[:, at_k].astype(jnp.float32) * slope
                ).astype(jnp.bfloat16)
                grads_out[:, at_k] = grads
                for (row, end), send in zip(bounds, sends):
                    send[:, at_k] = grads[row:end]


def latent_of(dp_index, size, normed, halves, latent_width):
    width = normed.shape[1] // size
    total = None
    for k in range(size):
        for half in range(2):
            block = normed[:, half_columns(dp_index, k, half, width)]
            part = dot_nt(block, halves[2 * k + half][:latent_width])
            total = part if total is None else total + part
    return total


def keep_kernel(size, count, more, *refs):
    flags = refs[0]
    gain, inverse, _, x = refs[1:5]
    raw = refs[9 : 9 + count]
    latent, normed = refs[11 + count], refs[16 + count]
    kept = refs[17 + count : 17 + count + 2 * size]
    bundle, sems = refs[17 + count + 2 * size :]
    tokens, width = x.shape
    latent_width = latent.shape[1]
    shard = width // size
    rows = raw[0].shape[0] - latent_width

    @pl.when(flags[3] == 1)
    def _():
        sources = list(raw[2 * size :])
        if len(sources) < size and more:
            sources[2:] = [raw[-1].at[pl.ds(0, more)], raw[-1].at[pl.ds(more, more)]]
        copies = [
            pltpu.make_async_copy(source, kept[size + k].at[pl.ds(rows, more)], sems.at[k])
            for k, source in enumerate(sources)
        ]
        for copy in copies:
            copy.start()
        latent[...] = latent_of(flags[0], size, normed, raw, latent_width)
        for k in range(size):
            for half in range(2):
                here = slice(half * (shard // 2), (half + 1) * (shard // 2))
                kept[k][:, here] = raw[2 * k + half][:latent_width]
                kept[size + k][:rows, here] = raw[2 * k + half][latent_width:]
        for copy in copies:
            copy.wait()

    @pl.when(flags[4] == 1)
    def _():
        block = kept[-1].shape[0]
        for k in range(size):
            bundle[k * latent_width : (k + 1) * latent_width] = kept[k][...]
            row = size * latent_width + k * block
            bundle[row : row + block] = kept[size + k][...]
        at = size * (latent_width + block)
        for k in range(size):
            here = slice(k * shard, (k + 1) * shard)
            bundle[at + k * tokens : at + (k + 1) * tokens] = x[:, here]
            row = at + size * tokens + k * GAIN_ROWS
            bundle[row : row + GAIN_ROWS] = jnp.broadcast_to(gain[:, here], (GAIN_ROWS, shard))
        at += size * (tokens + GAIN_ROWS)
        for values in (latent[...], inverse[...]):
            high = values.astype(jnp.bfloat16)
            low = (values - high.astype(jnp.float32)).astype(jnp.bfloat16)
            for part in (high, low):
                bundle[at : at + tokens, : part.shape[1]] = part
                at += tokens


def message_kernel(size, *refs):
    flags, normed = refs[:2]
    latent = refs[3]
    messages = refs[4:]
    shard = normed.shape[1] // size
    activated = jax.nn.silu(latent[...]).astype(jnp.bfloat16)
    for k in range(size):
        messages[k][:, :shard] = normed[:, columns(flags[0], k, shard)]
        messages[k][:, shard:] = activated


def step_back(dp_index, size, width, take, down, up, lat, scale, gain, x, write):
    latent_width = lat.shape[1]
    shard = width // size
    block = min(latent_width, shard)
    hidden_grad = None
    for k in range(size):
        arriving = take(columns(dp_index, k, shard))
        for at in range(0, shard, block):
            lanes = at // block * latent_width
            part = dot_nn(arriving[:, at : at + block], up(k, slice(lanes, lanes + latent_width)))
            hidden_grad = part if hidden_grad is None else hidden_grad + part
    latent_grad = (hidden_grad * silu_slope(lat)).astype(jnp.bfloat16)
    mean = jnp.sum(latent_grad.astype(jnp.float32) * lat, axis=-1, keepdims=True) / width
    slope = scale * scale * mean
    for k in range(size):
        for half in range(2):
            place = half_columns(dp_index, k, half, shard)
            arriving = take(place)
            scaled = dot_nn(latent_grad, down(k, half))
            value = (
                arriving.astype(jnp.float32)
                + scale * (scaled * gain(k, half).astype(jnp.float32))
                - x(k, half).astype(jnp.float32) * slope
            ).astype(jnp.bfloat16)
            write(place, arriving, value)
    return latent_grad


def kept_of(kept, size, shard):
    def down(k, half):
        return kept[k][:, half * (shard // 2) : (half + 1) * (shard // 2)]

    return down, lambda k, lanes: kept[size + k][:, lanes]


def stage_kernel(stage, bounds, size, held, *refs):
    flags = refs[0]
    pieces = refs[1 : 1 + len(bounds)]
    at = 1 + len(bounds)
    state = refs[at + held : at + 2 * held]
    outs = refs[at + 2 * held :]
    shard = state[3].shape[1] // size
    down, up = kept_of(state[7:], size, shard)
    state = state[:7]
    gain, inverse, latent, x, latent_grads, arrivals, grads = state
    tokens = x.shape[0]
    at_rows = slice(bounds[0][0], bounds[-1][1])

    def take(place):
        parts = [
            piece[slice(*bound) if piece.shape[0] == tokens else slice(None), place]
            for bound, piece in zip(bounds, pieces)
        ]
        return parts[0] if len(parts) == 1 else jnp.concatenate(parts, axis=0)

    def write(place, arriving, value):
        arrivals[at_rows, place] = arriving
        grads[at_rows, place] = value
        if stage and outs:
            outs[0][:, place] = value

    @pl.when(flags[1] == stage)
    def _():
        latent_grads[at_rows] = step_back(
            flags[0],
            size,
            x.shape[1],
            take,
            down,
            up,
            latent[at_rows],
            inverse[at_rows][:, :1],
            lambda k, half: gain[:, half_columns(flags[0], k, half, shard)],
            lambda k, half: x[at_rows, half_columns(flags[0], k, half, shard)],
            write,
        )

    if stage == 0:
        for k in range(size):
            outs[k][:, :shard] = arrivals[:, columns(flags[0], k, shard)]
            outs[k][:, shard:] = latent_grads[...]


def pair_kernel(stage, bound, size, held, *refs):
    flags, received = refs[:2]
    state = refs[2 + held : 9 + held]
    kept = refs[9 + held : 9 + held + 2 * size]
    bundle = refs[1 + 2 * held]
    middle, last = refs[2 + 2 * held :]
    gain, inverse, latent, x, latent_grads, arrivals, grads = state
    tokens = x.shape[0]
    latent_width = latent.shape[1]
    shard = x.shape[1] // size
    down, up = kept_of(kept, size, shard)
    block = kept[-1].shape[0]
    at_rows = slice(*bound)

    def write(place, arriving, value):
        arrivals[at_rows, place] = arriving
        grads[at_rows, place] = value
        middle[:, place] = value

    def write_last(place, arriving, value):
        last[:, place] = value

    def next_down(k, half):
        here = slice(half * (shard // 2), (half + 1) * (shard // 2))
        return bundle[k * latent_width : (k + 1) * latent_width, here]

    def both(index, lanes):
        row = size * (latent_width + block + tokens + GAIN_ROWS) + index * tokens + bound[0]
        end = row + bound[1] - bound[0]
        high = bundle[row:end, :lanes].astype(jnp.float32)
        return high + bundle[row + tokens : end + tokens, :lanes].astype(jnp.float32)

    def next_x(k, half):
        here = slice(half * (shard // 2), (half + 1) * (shard // 2))
        start = size * (latent_width + block) + (flags[0] ^ k) * tokens + bound[0]
        return bundle[pl.ds(pl.multiple_of(start, 16), bound[1] - bound[0]), here]

    def next_gain(k, half):
        here = slice(half * (shard // 2), (half + 1) * (shard // 2))
        start = size * (latent_width + block + tokens) + (flags[0] ^ k) * GAIN_ROWS
        return bundle[pl.ds(pl.multiple_of(start, 16), GAIN_ROWS), here][:1]

    def next_up(k, lanes):
        row = size * latent_width + k * block
        return bundle[row : row + block, lanes]

    @pl.when(flags[1] == stage)
    def _():
        latent_grads[at_rows] = step_back(
            flags[0],
            size,
            x.shape[1],
            lambda place: received[:, place],
            down,
            up,
            latent[at_rows],
            inverse[at_rows][:, :1],
            lambda k, half: gain[:, half_columns(flags[0], k, half, shard)],
            lambda k, half: x[at_rows, half_columns(flags[0], k, half, shard)],
            write,
        )
        step_back(
            flags[0],
            size,
            x.shape[1],
            lambda place: middle[:, place],
            next_down,
            next_up,
            both(0, latent_width),
            both(2, 128)[:, :1],
            next_gain,
            next_x,
            write_last,
        )


def touch_kernel(*refs):
    pass


def merge_kernel(size, split, *refs):
    flags, latent, early = refs[0], refs[1], refs[2 : 2 + size]
    above = (early[0],) + refs[2 + size : 1 + 2 * size]
    left = refs[2 + 2 * size]
    tokens = early[0].shape[0]

    def fill(sources):
        for k in range(size):
            left[:, k * tokens : (k + 1) * tokens] = sources[k][...].T

    pl.when(flags[1] < split)(lambda: fill(early))
    pl.when(flags[1] >= split)(lambda: fill(above))


def weight_kernel(size, left, *refs):
    late = refs[:1] + refs[size - 1 : 0 : -1]
    down_grads, up_grads, right = refs[size:]
    tokens = late[0].shape[0]
    shard = down_grads.shape[0]
    for k in range(size):
        right[k * tokens : (k + 1) * tokens] = late[k][...]
    down_grads[...] = dot_nn(left[:shard], right[:, shard:]).astype(jnp.bfloat16)
    up_grads[...] = dot_nn(left[shard:], right[:, :shard]).astype(jnp.bfloat16)


def per_device(
    section_inputs, norm_gain, down_proj, up_proj, readout_matrix, ground_truth_series, valid_len
):
    size = lax.axis_size("dp")
    sections = lax.axis_size("section")
    top = sections - 1
    dp_index = lax.axis_index("dp")
    section = lax.axis_index("section")
    f32, bf16 = jnp.float32, jnp.bfloat16

    x = section_inputs[0]
    tokens, width = x.shape
    shard, latent_width = down_proj.shape[1:]
    horizon = readout_matrix.shape[1]
    share = tokens // sum(CHUNK_SHARES)
    ends = [share * sum(CHUNK_SHARES[: i + 1]) for i in range(len(CHUNK_SHARES))]
    bounds = list(zip([0] + ends, ends))

    flags = jnp.stack(
        [
            dp_index.astype(jnp.int32),
            section.astype(jnp.int32),
            (section == top).astype(jnp.int32),
            (section < top).astype(jnp.int32),
            ((section < top - 1) & (section % 2 == 0)).astype(jnp.int32),
        ]
    )
    everyone, rest = list(range(sections)), list(range(top))
    up_block = min(latent_width, shard)
    up_lanes = latent_width * shard // up_block
    head_rows = horizon + latent_width * horizon // shard
    more = max(up_block - head_rows, 0)
    low, high, *up_rest = pl.pallas_call(
        prepare_kernel,
        out_shape=(jax.ShapeDtypeStruct((latent_width + head_rows, shard // 2), bf16),) * 2
        + (jax.ShapeDtypeStruct((more, up_lanes), bf16),) * (more > 0),
        in_specs=[SMEM] + [ANY] * 3,
        out_specs=(VMEM,) * (2 + (more > 0)),
        scratch_shapes=[
            pltpu.VMEM((1, shard, latent_width), bf16),
            pltpu.VMEM((1, latent_width, shard), bf16),
            pltpu.VMEM((shard, horizon), bf16),
            pltpu.SemaphoreType.DMA((3,)),
        ],
        cost_estimate=NOTHING,
        compiler_params=PARAMS,
    )(flags, stay(down_proj), stay(up_proj), stay(readout_matrix))
    halves = gather_halves(low, high, everyone, size)
    if more:
        up_rest = up_rest[0]
        if size == 4:
            across = move(up_rest, peers(rest, size, 1))
            along = move(jnp.concatenate([up_rest, across]), peers(rest, size, 2))
            up_rest = [up_rest, across, along]
        else:
            up_rest = gather(up_rest, rest, size)
    halves = [half for pair in halves for half in pair]

    x, normed, inverse, gain, truth = pl.pallas_call(
        norm_kernel,
        out_shape=(
            pltpu.VMEM((tokens, width), bf16),
            pltpu.VMEM((tokens, width), bf16),
            pltpu.VMEM((tokens, 128), f32),
            pltpu.VMEM((1, width), bf16),
            held_like(ground_truth_series),
        ),
        in_specs=[VMEM] * 3,
        out_specs=(VMEM,) * 5,
        cost_estimate=NOTHING,
        compiler_params=PARAMS,
    )(x, norm_gain, ground_truth_series)
    per_micro = tokens // valid_len.shape[0]
    mask = (
        (jnp.arange(per_micro)[None, :] < valid_len[:, None]).astype(f32).reshape(tokens, 1)
    )
    mask = jnp.broadcast_to(mask, (tokens, 128))

    gain, x, inverse, normed, latent, latent_grads, arrivals, grads, *sends = pl.pallas_call(
        functools.partial(top_kernel, size, [(0, tokens)]),
        out_shape=(
            held_like(gain),
            held_like(x),
            held_like(inverse),
            held_like(normed),
            pltpu.VMEM((tokens, latent_width), f32),
            pltpu.VMEM((tokens, latent_width), bf16),
            pltpu.VMEM((tokens, width), bf16),
            pltpu.VMEM((tokens, width), bf16),
        )
        + (jax.ShapeDtypeStruct((tokens, width), bf16),),
        in_specs=[SMEM] + [VMEM] * (6 + 2 * size),
        out_specs=(VMEM,) * 9,
        input_output_aliases={3: 0, 4: 1, 5: 2, 6: 3},
        cost_estimate=NOTHING,
        compiler_params=PARAMS,
    )(
        flags, pin(truth), mask, pin(gain), pin(x), pin(inverse), pin(normed),
        *[pin(part) for part in halves],
    )

    def hop(block, sender, distance=1):
        return move(
            block, [(sender * size + i, (sender - distance) * size + i) for i in range(size)]
        )

    received = [hop(sends[0], top)] * len(bounds)

    message = jax.ShapeDtypeStruct((tokens, shard + latent_width), bf16)
    shards = (*halves, *up_rest)
    state = (gain, inverse, latent, x, latent_grads, arrivals, grads)

    def run_stage(stage, bounds, received, state, sends=True):
        rows = bounds[-1][1] - bounds[0][0]
        if not stage:
            outs = (message,) * size
        else:
            outs = (jax.ShapeDtypeStruct((rows, width), bf16),) * sends
        first = 1 + len(received)
        results = pl.pallas_call(
            functools.partial(stage_kernel, stage, bounds, size, len(state)),
            out_shape=tuple(held_like(part) for part in state) + outs,
            in_specs=[SMEM] + [VMEM] * (len(received) + len(state)),
            out_specs=(VMEM,) * (len(state) + len(outs)),
            input_output_aliases={first + i: i for i in range(len(state))},
            cost_estimate=NOTHING,
            compiler_params=PARAMS,
        )(flags, *received, *[pin(part) for part in state])
        return tuple(results[: len(state)]), results[len(state) :]

    def run_pair(stage, bound, received, state):
        rows = bound[1] - bound[0]
        results = pl.pallas_call(
            functools.partial(pair_kernel, stage, bound, size, len(state)),
            out_shape=tuple(held_like(part) for part in state)
            + (jax.ShapeDtypeStruct((rows, width), bf16),) * 2,
            in_specs=[SMEM] + [VMEM] * (1 + len(state)),
            out_specs=(VMEM,) * (len(state) + 2),
            input_output_aliases={2 + i: i for i in range(len(state))},
            cost_estimate=NOTHING,
            compiler_params=PARAMS,
        )(flags, received, *[pin(part) for part in state])
        return tuple(results[: len(state)]), results[len(state) :]

    def send_messages(messages, among):
        return [messages[0]] + [move(messages[k], peers(among, size, k)) for k in range(1, size)]

    def hold(state, blocks):
        latent, *blocks = pl.pallas_call(
            touch_kernel,
            out_shape=(held_like(state[2]),) + tuple(held_like(part) for part in blocks),
            in_specs=[VMEM] * (1 + len(blocks)),
            out_specs=(VMEM,) * (1 + len(blocks)),
            input_output_aliases={i: i for i in range(1 + len(blocks))},
            cost_estimate=NOTHING,
            compiler_params=PARAMS,
        )(pin(state[2]), *[pin(part) for part in blocks])
        return state[:2] + (latent,) + state[3:], blocks

    state_kept = pl.pallas_call(
        functools.partial(keep_kernel, size, len(shards), more),
        out_shape=tuple(held_like(part) for part in (*state, normed))
        + (pltpu.VMEM((latent_width, shard), bf16),) * size
        + (pltpu.VMEM((up_block, up_lanes), bf16),) * size
        + (
            jax.ShapeDtypeStruct(
                (size * (latent_width + up_block + tokens + GAIN_ROWS) + 4 * tokens, shard), bf16
            ),
        ),
        in_specs=[SMEM]
        + [VMEM] * (len(state) + 1 + 2 * size)
        + [ANY] * (len(shards) - 2 * size),
        out_specs=(VMEM,) * (len(state) + 2 * size + 2),
        scratch_shapes=[pltpu.SemaphoreType.DMA((size,))],
        input_output_aliases={1 + i: i for i in range(len(state) + 1)},
        cost_estimate=NOTHING,
        compiler_params=PARAMS,
    )(flags, *[pin(part) for part in (*state, normed, *halves)], *up_rest)
    state, normed = tuple(state_kept[:7]), state_kept[7]
    kept, bundle = tuple(state_kept[8:-1]), state_kept[-1:]
    pairs = list(range(3, top - 1, 2))
    bundle = tuple(
        move(part, [((s - 1) * size + i, s * size + i) for s in pairs for i in range(size)])
        for part in bundle
    )

    state = state + kept
    sent = []
    for bound, block in zip(bounds, received):
        state, outs = run_stage(top - 1, [bound], [block], state)
        sent.append(hop(outs[0], top - 1))
    received = sent

    state = state + bundle

    latent, *messages = pl.pallas_call(
        functools.partial(message_kernel, size),
        out_shape=(held_like(state[2]),) + (message,) * size,
        in_specs=[SMEM] + [VMEM] * 2,
        out_specs=(VMEM,) * (1 + size),
        input_output_aliases={2: 0},
        cost_estimate=NOTHING,
        compiler_params=PARAMS,
    )(flags, pin(normed), pin(state[2]))
    state = state[:2] + (latent,) + state[3:]
    split = pairs[-1] - 1
    early = send_messages(messages, range(split))
    above = send_messages(messages, range(split, sections))

    waiting = []
    for stage in reversed(pairs):
        sent, side = [], []
        for bound, block in zip(bounds, received):
            state, outs = run_pair(stage, bound, block, state)
            sent.append(hop(outs[1], stage, 2))
            side.append(hop(outs[0], stage))
            if stage == pairs[-1] and len(sent) == 1:
                state, early = hold(state, early)
        received = sent
        for asides, bound, block in waiting:
            base, _ = run_stage(asides, [bound], [block], state[:-1], False)
            state = base + state[-1:]
        waiting = [(stage - 1, bound, block) for bound, block in zip(bounds, side)]
        if stage == pairs[0]:
            latent, left = pl.pallas_call(
                functools.partial(merge_kernel, size, split),
                out_shape=(
                    held_like(state[2]),
                    pltpu.VMEM((shard + latent_width, size * tokens), bf16),
                ),
                in_specs=[SMEM] + [VMEM] * (2 * size),
                out_specs=(VMEM,) * 2,
                input_output_aliases={1: 0},
                cost_estimate=NOTHING,
                compiler_params=PARAMS,
            )(flags, pin(state[2]), *early, *above[1:])
            state = state[:2] + (latent,) + state[3:]
    state = state[:-1]

    sent = []
    for bound, block in zip(bounds, received):
        state, outs = run_stage(1, [bound], [block], state)
        sent.append(hop(outs[0], 1))
    received = sent
    for asides, bound, block in waiting:
        state, _ = run_stage(asides, [bound], [block], state, False)
    state, outs = run_stage(0, bounds, received, state)
    late = send_messages(outs, everyone)
    down_grads, up_grads = pl.pallas_call(
        functools.partial(weight_kernel, size),
        out_shape=(
            jax.ShapeDtypeStruct((shard, latent_width), bf16),
            jax.ShapeDtypeStruct((latent_width, shard), bf16),
        ),
        in_specs=[VMEM] * (1 + size),
        out_specs=(VMEM,) * 2,
        scratch_shapes=[pltpu.VMEM((size * tokens, shard + latent_width), bf16)],
        compiler_params=PARAMS,
    )(pin(left), late[0], *late[:0:-1])
    return (state[6][None], down_grads[None], up_grads[None])


def solution(mesh):
    placed = (
        P("section", "dp", None),
        P("section", None),
        P("section", "dp", None),
        P("section", None, "dp"),
        P("dp", None),
        P("dp", None),
        P("dp"),
    )
    return jax.shard_map(
        per_device,
        mesh=mesh,
        in_specs=placed,
        out_specs=(P("section", "dp", None), P("section", "dp", None), P("section", None, "dp")),
        check_vma=False,
    )
```

```python
import functools

import jax
import jax.numpy as jnp
from jax import lax
from jax.experimental import pallas as pl
from jax.experimental.pallas import tpu as pltpu
from jax.sharding import PartitionSpec as P

EPSILON = 1e-05
CHUNK_SHARES = (4, 4)
GAIN_ROWS = 16
ANY = pl.BlockSpec(memory_space=pl.ANY)
VMEM = pl.BlockSpec(memory_space=pltpu.VMEM)
SMEM = pl.BlockSpec(memory_space=pltpu.SMEM)
NOTHING = pl.CostEstimate(flops=0, bytes_accessed=0, transcendentals=0)
PARAMS = pltpu.CompilerParams(vmem_limit_bytes=20 * 1024 * 1024)


def dot_nn(left, right):
    return lax.dot_general(
        left, right, (((1,), (0,)), ((), ())), preferred_element_type=jnp.float32
    )


def dot_nt(left, right):
    return lax.dot_general(
        left, right, (((1,), (1,)), ((), ())), preferred_element_type=jnp.float32
    )


def dot_tn(left, right):
    return lax.dot_general(
        left, right, (((0,), (0,)), ((), ())), preferred_element_type=jnp.float32
    )


def silu_slope(latent):
    sigmoid = jax.nn.sigmoid(latent)
    return sigmoid * (1.0 + latent * (1.0 - sigmoid))


def move(block, pairs):
    return lax.ppermute(block, ("section", "dp"), pairs)


def peers(sections, size, k):
    return [(s * size + i, s * size + (i ^ k)) for s in sections for i in range(size)]


def gather(block, sections, size):
    return [block] + [move(block, peers(sections, size, k)) for k in range(1, size)]


def gather_halves(low, high, sections, size):
    if size != 4:
        return list(zip(gather(low, sections, size), gather(high, sections, size)))
    across, along = peers(sections, size, 1), peers(sections, size, 2)
    low_along = move(low, along)
    high_across = move(high, across)
    high_along = move(high, along)
    low_across = move(low, across)
    low_far = move(low_along, across)
    high_far = move(high_across, along)
    return [(low, high), (low_across, high_across), (low_along, high_along), (low_far, high_far)]


def pin(block):
    return pltpu.with_memory_space_constraint(block, pltpu.VMEM)


def stay(block):
    return pltpu.with_memory_space_constraint(block, pltpu.HBM)


def held_like(block):
    return pltpu.VMEM(block.shape, block.dtype)


def columns(dp_index, k, width):
    return pl.ds(pl.multiple_of((dp_index ^ k) * width, width), width)


def half_columns(dp_index, k, half, width):
    start = (dp_index ^ k) * width + half * (width // 2)
    return pl.ds(pl.multiple_of(start, width // 2), width // 2)


def prepare_kernel(flags, down, up, readout, *refs):
    low, high, *rest, down_held, up_held, readout_held, sems = refs
    copies = [
        pltpu.make_async_copy(down, down_held, sems.at[0]),
        pltpu.make_async_copy(up, up_held, sems.at[1]),
        pltpu.make_async_copy(readout, readout_held, sems.at[2]),
    ]
    for copy in copies:
        copy.start()
    latent_width, shard = up_held.shape[1:]
    horizon = readout_held.shape[1]
    half = shard // 2
    head_rows = low.shape[0] - latent_width
    copies[0].wait()
    turned = down_held[0].T
    low[:latent_width] = turned[:, :half]
    high[:latent_width] = turned[:, half:]
    copies[1].wait()
    copies[2].wait()
    values = up_held[0]

    @pl.when(flags[2] == 1)
    def _():
        product = dot_nn(values, readout_held[...]).astype(jnp.bfloat16)
        turned_readout = readout_held[...].T
        rows = latent_width * horizon // shard
        for out, start in ((low, 0), (high, half)):
            out[latent_width : latent_width + horizon] = turned_readout[:, start : start + half]
            for at in range(0, half, horizon):
                row = (start + at) // horizon * rows
                out[latent_width + horizon :, at : at + horizon] = product[row : row + rows]

    @pl.when(flags[2] == 0)
    def _():
        block = min(latent_width, shard)
        blocks = [values[:, at : at + block].T for at in range(0, shard, block)]
        whole = blocks[0] if len(blocks) == 1 else jnp.concatenate(blocks, axis=1)
        low[latent_width:] = whole[:head_rows, :half]
        high[latent_width:] = whole[:head_rows, half:]
        if rest:
            rest[0][...] = whole[head_rows:]


def norm_kernel(x, gain, truth, x_out, normed_out, inverse_out, gain_out, truth_out):
    truth_out[...] = truth[...]
    values = x[...].astype(jnp.float32)
    inverse = lax.rsqrt(jnp.mean(values * values, axis=-1, keepdims=True) + EPSILON)
    x_out[...] = x[...]
    normed_out[...] = (values * inverse * gain[...].astype(jnp.float32)).astype(jnp.bfloat16)
    inverse_out[...] = jnp.broadcast_to(inverse, inverse_out.shape)
    gain_out[...] = gain[...]


def top_kernel(size, bounds, *refs):
    flags, truth, mask = refs[:3]
    halves = refs[7 : 7 + 2 * size]
    gain, x, inverse, normed, latent_ref, latent_grad_out, arriving_out, grads_out = refs[
        7 + 2 * size : 15 + 2 * size
    ]
    sends = refs[15 + 2 * size :]
    dp_index = flags[0]
    width = x.shape[1] // size
    latent_width = latent_ref.shape[1]
    horizon = truth.shape[1]
    head = slice(latent_width, latent_width + horizon)

    @pl.when(flags[2] == 1)
    def _():
        latent = latent_of(dp_index, size, normed, halves, latent_width)
        latent_ref[...] = latent
        activated = jax.nn.silu(latent).astype(jnp.bfloat16)
        estimate = None
        product = None
        for k in range(size):
            extra = []
            for half in range(2):
                ref = halves[2 * k + half]
                part = dot_nt(x[:, half_columns(dp_index, k, half, width)], ref[head])
                estimate = part if estimate is None else estimate + part
                extra += [
                    ref[latent_width + horizon :, at : at + horizon]
                    for at in range(0, width // 2, horizon)
                ]
            extra = jnp.concatenate(extra, axis=0).astype(jnp.float32)
            product = extra if product is None else product + extra
        product = product.astype(jnp.bfloat16)
        estimate = estimate + dot_nn(activated, product)
        error = (mask[:, :1] * (estimate - truth[...])).astype(jnp.bfloat16)
        hidden_grad = dot_nt(error, product)
        latent_grad = (hidden_grad * silu_slope(latent)).astype(jnp.bfloat16)
        latent_grad_out[...] = latent_grad
        scale = inverse[:, :1]
        mean = jnp.sum(latent_grad.astype(jnp.float32) * latent, axis=-1, keepdims=True) / (
            width * size
        )
        slope = scale * scale * mean
        for k in range(size):
            for half in range(2):
                at_k = half_columns(dp_index, k, half, width)
                ref = halves[2 * k + half]
                arriving = dot_nn(error, ref[head]).astype(jnp.bfloat16)
                arriving_out[:, at_k] = arriving
                scaled = dot_nn(latent_grad, ref[:latent_width])
                grads = (
                    arriving.astype(jnp.float32)
                    + scale * (scaled * gain[:, at_k].astype(jnp.float32))
                    - x[:, at_k].astype(jnp.float32) * slope
                ).astype(jnp.bfloat16)
                grads_out[:, at_k] = grads
                for (row, end), send in zip(bounds, sends):
                    send[:, at_k] = grads[row:end]


def latent_of(dp_index, size, normed, halves, latent_width):
    width = normed.shape[1] // size
    total = None
    for k in range(size):
        for half in range(2):
            block = normed[:, half_columns(dp_index, k, half, width)]
            part = dot_nt(block, halves[2 * k + half][:latent_width])
            total = part if total is None else total + part
    return total


def keep_kernel(size, count, more, *refs):
    flags = refs[0]
    gain, inverse, _, x = refs[1:5]
    raw = refs[9 : 9 + count]
    latent, normed = refs[11 + count], refs[16 + count]
    kept = refs[17 + count : 17 + count + 2 * size]
    bundle, sems = refs[17 + count + 2 * size :]
    tokens, width = x.shape
    latent_width = latent.shape[1]
    shard = width // size
    rows = raw[0].shape[0] - latent_width

    @pl.when(flags[3] == 1)
    def _():
        sources = list(raw[2 * size :])
        if len(sources) < size and more:
            sources[2:] = [raw[-1].at[pl.ds(0, more)], raw[-1].at[pl.ds(more, more)]]
        copies = [
            pltpu.make_async_copy(source, kept[size + k].at[pl.ds(rows, more)], sems.at[k])
            for k, source in enumerate(sources)
        ]
        for copy in copies:
            copy.start()
        latent[...] = latent_of(flags[0], size, normed, raw, latent_width)
        for k in range(size):
            for half in range(2):
                here = slice(half * (shard // 2), (half + 1) * (shard // 2))
                kept[k][:, here] = raw[2 * k + half][:latent_width]
                kept[size + k][:rows, here] = raw[2 * k + half][latent_width:]
        for copy in copies:
            copy.wait()

    @pl.when(flags[4] == 1)
    def _():
        block = kept[-1].shape[0]
        for k in range(size):
            bundle[k * latent_width : (k + 1) * latent_width] = kept[k][...]
            row = size * latent_width + k * block
            bundle[row : row + block] = kept[size + k][...]
        at = size * (latent_width + block)
        for k in range(size):
            here = slice(k * shard, (k + 1) * shard)
            bundle[at + k * tokens : at + (k + 1) * tokens] = x[:, here]
            row = at + size * tokens + k * GAIN_ROWS
            bundle[row : row + GAIN_ROWS] = jnp.broadcast_to(gain[:, here], (GAIN_ROWS, shard))
        at += size * (tokens + GAIN_ROWS)
        for values in (latent[...], inverse[...]):
            high = values.astype(jnp.bfloat16)
            low = (values - high.astype(jnp.float32)).astype(jnp.bfloat16)
            for part in (high, low):
                bundle[at : at + tokens, : part.shape[1]] = part
                at += tokens


def message_kernel(size, *refs):
    flags, normed = refs[:2]
    latent = refs[3]
    messages = refs[4:]
    shard = normed.shape[1] // size
    activated = jax.nn.silu(latent[...]).astype(jnp.bfloat16)
    for k in range(size):
        messages[k][:, :shard] = normed[:, columns(flags[0], k, shard)]
        messages[k][:, shard:] = activated


def step_back(dp_index, size, width, take, down, up, lat, scale, gain, x, write):
    latent_width = lat.shape[1]
    shard = width // size
    block = min(latent_width, shard)
    hidden_grad = None
    for k in range(size):
        arriving = take(columns(dp_index, k, shard))
        for at in range(0, shard, block):
            lanes = at // block * latent_width
            part = dot_nn(arriving[:, at : at + block], up(k, slice(lanes, lanes + latent_width)))
            hidden_grad = part if hidden_grad is None else hidden_grad + part
    latent_grad = (hidden_grad * silu_slope(lat)).astype(jnp.bfloat16)
    mean = jnp.sum(latent_grad.astype(jnp.float32) * lat, axis=-1, keepdims=True) / width
    slope = scale * scale * mean
    for k in range(size):
        for half in range(2):
            place = half_columns(dp_index, k, half, shard)
            arriving = take(place)
            scaled = dot_nn(latent_grad, down(k, half))
            value = (
                arriving.astype(jnp.float32)
                + scale * (scaled * gain(k, half).astype(jnp.float32))
                - x(k, half).astype(jnp.float32) * slope
            ).astype(jnp.bfloat16)
            write(place, arriving, value)
    return latent_grad


def kept_of(kept, size, shard):
    def down(k, half):
        return kept[k][:, half * (shard // 2) : (half + 1) * (shard // 2)]

    return down, lambda k, lanes: kept[size + k][:, lanes]


def stage_kernel(stage, bounds, size, held, *refs):
    flags = refs[0]
    pieces = refs[1 : 1 + len(bounds)]
    at = 1 + len(bounds)
    state = refs[at + held : at + 2 * held]
    outs = refs[at + 2 * held :]
    shard = state[3].shape[1] // size
    down, up = kept_of(state[7:], size, shard)
    state = state[:7]
    gain, inverse, latent, x, latent_grads, arrivals, grads = state
    tokens = x.shape[0]
    at_rows = slice(bounds[0][0], bounds[-1][1])

    def take(place):
        parts = [
            piece[slice(*bound) if piece.shape[0] == tokens else slice(None), place]
            for bound, piece in zip(bounds, pieces)
        ]
        return parts[0] if len(parts) == 1 else jnp.concatenate(parts, axis=0)

    def write(place, arriving, value):
        arrivals[at_rows, place] = arriving
        grads[at_rows, place] = value
        if stage and outs:
            outs[0][:, place] = value

    @pl.when(flags[1] == stage)
    def _():
        latent_grads[at_rows] = step_back(
            flags[0],
            size,
            x.shape[1],
            take,
            down,
            up,
            latent[at_rows],
            inverse[at_rows][:, :1],
            lambda k, half: gain[:, half_columns(flags[0], k, half, shard)],
            lambda k, half: x[at_rows, half_columns(flags[0], k, half, shard)],
            write,
        )

    if stage == 0:
        for k in range(size):
            outs[k][:, :shard] = arrivals[:, columns(flags[0], k, shard)]
            outs[k][:, shard:] = latent_grads[...]


def pair_kernel(stage, bound, size, held, *refs):
    flags, received = refs[:2]
    state = refs[2 + held : 9 + held]
    kept = refs[9 + held : 9 + held + 2 * size]
    bundle = refs[1 + 2 * held]
    middle, last = refs[2 + 2 * held :]
    gain, inverse, latent, x, latent_grads, arrivals, grads = state
    tokens = x.shape[0]
    latent_width = latent.shape[1]
    shard = x.shape[1] // size
    down, up = kept_of(kept, size, shard)
    block = kept[-1].shape[0]
    at_rows = slice(*bound)

    def write(place, arriving, value):
        arrivals[at_rows, place] = arriving
        grads[at_rows, place] = value
        middle[:, place] = value

    def write_last(place, arriving, value):
        last[:, place] = value

    def next_down(k, half):
        here = slice(half * (shard // 2), (half + 1) * (shard // 2))
        return bundle[k * latent_width : (k + 1) * latent_width, here]

    def both(index, lanes):
        row = size * (latent_width + block + tokens + GAIN_ROWS) + index * tokens + bound[0]
        end = row + bound[1] - bound[0]
        high = bundle[row:end, :lanes].astype(jnp.float32)
        return high + bundle[row + tokens : end + tokens, :lanes].astype(jnp.float32)

    def next_x(k, half):
        here = slice(half * (shard // 2), (half + 1) * (shard // 2))
        start = size * (latent_width + block) + (flags[0] ^ k) * tokens + bound[0]
        return bundle[pl.ds(pl.multiple_of(start, 16), bound[1] - bound[0]), here]

    def next_gain(k, half):
        here = slice(half * (shard // 2), (half + 1) * (shard // 2))
        start = size * (latent_width + block + tokens) + (flags[0] ^ k) * GAIN_ROWS
        return bundle[pl.ds(pl.multiple_of(start, 16), GAIN_ROWS), here][:1]

    def next_up(k, lanes):
        row = size * latent_width + k * block
        return bundle[row : row + block, lanes]

    @pl.when(flags[1] == stage)
    def _():
        latent_grads[at_rows] = step_back(
            flags[0],
            size,
            x.shape[1],
            lambda place: received[:, place],
            down,
            up,
            latent[at_rows],
            inverse[at_rows][:, :1],
            lambda k, half: gain[:, half_columns(flags[0], k, half, shard)],
            lambda k, half: x[at_rows, half_columns(flags[0], k, half, shard)],
            write,
        )
        step_back(
            flags[0],
            size,
            x.shape[1],
            lambda place: middle[:, place],
            next_down,
            next_up,
            both(0, latent_width),
            both(2, 128)[:, :1],
            next_gain,
            next_x,
            write_last,
        )


def touch_kernel(*refs):
    pass


def merge_kernel(size, split, *refs):
    flags, latent, early = refs[0], refs[1], refs[2 : 2 + size]
    above = (early[0],) + refs[2 + size : 1 + 2 * size]
    left = refs[2 + 2 * size]
    tokens = early[0].shape[0]

    def fill(sources):
        for k in range(size):
            left[:, k * tokens : (k + 1) * tokens] = sources[k][...].T

    pl.when(flags[1] < split)(lambda: fill(early))
    pl.when(flags[1] >= split)(lambda: fill(above))


def weight_kernel(size, left, *refs):
    late = refs[:1] + refs[size - 1 : 0 : -1]
    down_grads, up_grads, right = refs[size:]
    tokens = late[0].shape[0]
    shard = down_grads.shape[0]
    for k in range(size):
        right[k * tokens : (k + 1) * tokens] = late[k][...]
    down_grads[...] = dot_nn(left[:shard], right[:, shard:]).astype(jnp.bfloat16)
    up_grads[...] = dot_nn(left[shard:], right[:, :shard]).astype(jnp.bfloat16)


def per_device(
    section_inputs, norm_gain, down_proj, up_proj, readout_matrix, ground_truth_series, valid_len
):
    size = lax.axis_size("dp")
    sections = lax.axis_size("section")
    top = sections - 1
    dp_index = lax.axis_index("dp")
    section = lax.axis_index("section")
    f32, bf16 = jnp.float32, jnp.bfloat16

    x = section_inputs[0]
    tokens, width = x.shape
    shard, latent_width = down_proj.shape[1:]
    horizon = readout_matrix.shape[1]
    share = tokens // sum(CHUNK_SHARES)
    ends = [share * sum(CHUNK_SHARES[: i + 1]) for i in range(len(CHUNK_SHARES))]
    bounds = list(zip([0] + ends, ends))

    flags = jnp.stack(
        [
            dp_index.astype(jnp.int32),
            section.astype(jnp.int32),
            (section == top).astype(jnp.int32),
            (section < top).astype(jnp.int32),
            ((section < top - 1) & (section % 2 == 0)).astype(jnp.int32),
        ]
    )
    everyone, rest = list(range(sections)), list(range(top))
    up_block = min(latent_width, shard)
    up_lanes = latent_width * shard // up_block
    head_rows = horizon + latent_width * horizon // shard
    more = max(up_block - head_rows, 0)
    low, high, *up_rest = pl.pallas_call(
        prepare_kernel,
        out_shape=(jax.ShapeDtypeStruct((latent_width + head_rows, shard // 2), bf16),) * 2
        + (jax.ShapeDtypeStruct((more, up_lanes), bf16),) * (more > 0),
        in_specs=[SMEM] + [ANY] * 3,
        out_specs=(VMEM,) * (2 + (more > 0)),
        scratch_shapes=[
            pltpu.VMEM((1, shard, latent_width), bf16),
            pltpu.VMEM((1, latent_width, shard), bf16),
            pltpu.VMEM((shard, horizon), bf16),
            pltpu.SemaphoreType.DMA((3,)),
        ],
        cost_estimate=NOTHING,
        compiler_params=PARAMS,
    )(flags, stay(down_proj), stay(up_proj), stay(readout_matrix))
    halves = gather_halves(low, high, everyone, size)
    if more:
        up_rest = up_rest[0]
        if size == 4:
            across = move(up_rest, peers(rest, size, 1))
            along = move(jnp.concatenate([up_rest, across]), peers(rest, size, 2))
            up_rest = [up_rest, across, along]
        else:
            up_rest = gather(up_rest, rest, size)
    halves = [half for pair in halves for half in pair]

    x, normed, inverse, gain, truth = pl.pallas_call(
        norm_kernel,
        out_shape=(
            pltpu.VMEM((tokens, width), bf16),
            pltpu.VMEM((tokens, width), bf16),
            pltpu.VMEM((tokens, 128), f32),
            pltpu.VMEM((1, width), bf16),
            held_like(ground_truth_series),
        ),
        in_specs=[VMEM] * 3,
        out_specs=(VMEM,) * 5,
        cost_estimate=NOTHING,
        compiler_params=PARAMS,
    )(x, norm_gain, ground_truth_series)
    per_micro = tokens // valid_len.shape[0]
    mask = (
        (jnp.arange(per_micro)[None, :] < valid_len[:, None]).astype(f32).reshape(tokens, 1)
    )
    mask = jnp.broadcast_to(mask, (tokens, 128))

    gain, x, inverse, normed, latent, latent_grads, arrivals, grads, *sends = pl.pallas_call(
        functools.partial(top_kernel, size, [(0, tokens)]),
        out_shape=(
            held_like(gain),
            held_like(x),
            held_like(inverse),
            held_like(normed),
            pltpu.VMEM((tokens, latent_width), f32),
            pltpu.VMEM((tokens, latent_width), bf16),
            pltpu.VMEM((tokens, width), bf16),
            pltpu.VMEM((tokens, width), bf16),
        )
        + (jax.ShapeDtypeStruct((tokens, width), bf16),),
        in_specs=[SMEM] + [VMEM] * (6 + 2 * size),
        out_specs=(VMEM,) * 9,
        input_output_aliases={3: 0, 4: 1, 5: 2, 6: 3},
        cost_estimate=NOTHING,
        compiler_params=PARAMS,
    )(
        flags, pin(truth), mask, pin(gain), pin(x), pin(inverse), pin(normed),
        *[pin(part) for part in halves],
    )

    def hop(block, sender, distance=1):
        return move(
            block, [(sender * size + i, (sender - distance) * size + i) for i in range(size)]
        )

    received = [hop(sends[0], top)] * len(bounds)

    message = jax.ShapeDtypeStruct((tokens, shard + latent_width), bf16)
    shards = (*halves, *up_rest)
    state = (gain, inverse, latent, x, latent_grads, arrivals, grads)

    def run_stage(stage, bounds, received, state, sends=True):
        rows = bounds[-1][1] - bounds[0][0]
        if not stage:
            outs = (message,) * size
        else:
            outs = (jax.ShapeDtypeStruct((rows, width), bf16),) * sends
        first = 1 + len(received)
        results = pl.pallas_call(
            functools.partial(stage_kernel, stage, bounds, size, len(state)),
            out_shape=tuple(held_like(part) for part in state) + outs,
            in_specs=[SMEM] + [VMEM] * (len(received) + len(state)),
            out_specs=(VMEM,) * (len(state) + len(outs)),
            input_output_aliases={first + i: i for i in range(len(state))},
            cost_estimate=NOTHING,
            compiler_params=PARAMS,
        )(flags, *received, *[pin(part) for part in state])
        return tuple(results[: len(state)]), results[len(state) :]

    def run_pair(stage, bound, received, state):
        rows = bound[1] - bound[0]
        results = pl.pallas_call(
            functools.partial(pair_kernel, stage, bound, size, len(state)),
            out_shape=tuple(held_like(part) for part in state)
            + (jax.ShapeDtypeStruct((rows, width), bf16),) * 2,
            in_specs=[SMEM] + [VMEM] * (1 + len(state)),
            out_specs=(VMEM,) * (len(state) + 2),
            input_output_aliases={2 + i: i for i in range(len(state))},
            cost_estimate=NOTHING,
            compiler_params=PARAMS,
        )(flags, received, *[pin(part) for part in state])
        return tuple(results[: len(state)]), results[len(state) :]

    def send_messages(messages, among):
        return [messages[0]] + [move(messages[k], peers(among, size, k)) for k in range(1, size)]

    def hold(state, blocks):
        latent, *blocks = pl.pallas_call(
            touch_kernel,
            out_shape=(held_like(state[2]),) + tuple(held_like(part) for part in blocks),
            in_specs=[VMEM] * (1 + len(blocks)),
            out_specs=(VMEM,) * (1 + len(blocks)),
            input_output_aliases={i: i for i in range(1 + len(blocks))},
            cost_estimate=NOTHING,
            compiler_params=PARAMS,
        )(pin(state[2]), *[pin(part) for part in blocks])
        return state[:2] + (latent,) + state[3:], blocks

    state_kept = pl.pallas_call(
        functools.partial(keep_kernel, size, len(shards), more),
        out_shape=tuple(held_like(part) for part in (*state, normed))
        + (pltpu.VMEM((latent_width, shard), bf16),) * size
        + (pltpu.VMEM((up_block, up_lanes), bf16),) * size
        + (
            jax.ShapeDtypeStruct(
                (size * (latent_width + up_block + tokens + GAIN_ROWS) + 4 * tokens, shard), bf16
            ),
        ),
        in_specs=[SMEM]
        + [VMEM] * (len(state) + 1 + 2 * size)
        + [ANY] * (len(shards) - 2 * size),
        out_specs=(VMEM,) * (len(state) + 2 * size + 2),
        scratch_shapes=[pltpu.SemaphoreType.DMA((size,))],
        input_output_aliases={1 + i: i for i in range(len(state) + 1)},
        cost_estimate=NOTHING,
        compiler_params=PARAMS,
    )(flags, *[pin(part) for part in (*state, normed, *halves)], *up_rest)
    state, normed = tuple(state_kept[:7]), state_kept[7]
    kept, bundle = tuple(state_kept[8:-1]), state_kept[-1:]
    pairs = list(range(3, top - 1, 2))
    bundle = tuple(
        move(part, [((s - 1) * size + i, s * size + i) for s in pairs for i in range(size)])
        for part in bundle
    )

    state = state + kept
    sent = []
    for bound, block in zip(bounds, received):
        state, outs = run_stage(top - 1, [bound], [block], state)
        sent.append(hop(outs[0], top - 1))
    received = sent

    state = state + bundle

    latent, *messages = pl.pallas_call(
        functools.partial(message_kernel, size),
        out_shape=(held_like(state[2]),) + (message,) * size,
        in_specs=[SMEM] + [VMEM] * 2,
        out_specs=(VMEM,) * (1 + size),
        input_output_aliases={2: 0},
        cost_estimate=NOTHING,
        compiler_params=PARAMS,
    )(flags, pin(normed), pin(state[2]))
    state = state[:2] + (latent,) + state[3:]
    split = pairs[-1] - 1
    early = send_messages(messages, range(split))
    above = send_messages(messages, range(split, sections))

    waiting = []
    for stage in reversed(pairs):
        sent, side = [], []
        for bound, block in zip(bounds, received):
            state, outs = run_pair(stage, bound, block, state)
            sent.append(hop(outs[1], stage, 2))
            side.append(hop(outs[0], stage))
            if stage == pairs[-1] and len(sent) == 1:
                state, held = hold(state, early[:-1])
                early = [*held, early[-1]]
        received = sent
        for asides, bound, block in waiting:
            base, _ = run_stage(asides, [bound], [block], state[:-1], False)
            state = base + state[-1:]
        waiting = [(stage - 1, bound, block) for bound, block in zip(bounds, side)]
        if stage == pairs[0]:
            latent, left = pl.pallas_call(
                functools.partial(merge_kernel, size, split),
                out_shape=(
                    held_like(state[2]),
                    pltpu.VMEM((shard + latent_width, size * tokens), bf16),
                ),
                in_specs=[SMEM] + [VMEM] * (2 * size),
                out_specs=(VMEM,) * 2,
                input_output_aliases={1: 0},
                cost_estimate=NOTHING,
                compiler_params=PARAMS,
            )(flags, pin(state[2]), *early, *above[1:])
            state = state[:2] + (latent,) + state[3:]
    state = state[:-1]

    sent = []
    for bound, block in zip(bounds, received):
        state, outs = run_stage(1, [bound], [block], state)
        sent.append(hop(outs[0], 1))
    received = sent
    for asides, bound, block in waiting:
        state, _ = run_stage(asides, [bound], [block], state, False)
    state, outs = run_stage(0, bounds, received, state)
    late = send_messages(outs, everyone)
    down_grads, up_grads = pl.pallas_call(
        functools.partial(weight_kernel, size),
        out_shape=(
            jax.ShapeDtypeStruct((shard, latent_width), bf16),
            jax.ShapeDtypeStruct((latent_width, shard), bf16),
        ),
        in_specs=[VMEM] * (1 + size),
        out_specs=(VMEM,) * 2,
        scratch_shapes=[pltpu.VMEM((size * tokens, shard + latent_width), bf16)],
        compiler_params=PARAMS,
    )(pin(left), late[0], *late[:0:-1])
    return (state[6][None], down_grads[None], up_grads[None])


def solution(mesh):
    placed = (
        P("section", "dp", None),
        P("section", None),
        P("section", "dp", None),
        P("section", None, "dp"),
        P("dp", None),
        P("dp", None),
        P("dp"),
    )
    return jax.shard_map(
        per_device,
        mesh=mesh,
        in_specs=placed,
        out_specs=(P("section", "dp", None), P("section", "dp", None), P("section", None, "dp")),
        check_vma=False,
    )
```
